32 devices in a mesh: dp: 4 (over y, core), expert: 8 (over z, x).
Axes of the slice: x: 2, y: 2, z: 4, core: 2. Of those that a mesh axis runs over, the one named last changes fastest.
Arguments:
- hidden_in: bfloat16 [16384, 768], P(('dp', 'expert')), may hold values from -110 to 110
- doc_ids: int32 [32, 512], P(('dp', 'expert')), may hold values from 0 to 7, never falling along the last dimension, each value on 1 to 256 neighbouring positions
- valid_mask: int32 [32, 512], P(('dp', 'expert')), may hold values 0 or 1
- expert_ids: int32 [16384, 2], P(('dp', 'expert')), may hold values from 0 to 63, all different within a row; in each aligned block of 512 rows (0 to 511, 512 to 1023, ...) at most 24 rows name the same one
- bucket_table: int32 [512], replicated, may hold values from 0 to 31, as said below
- norm1_gain: float32 [768], replicated, may hold values from 0.1 to 1.9
- qkv_weight: bfloat16 [768, 2304], replicated, may hold values from -0.21875 to 0.21875
- position_bias: float32 [32, 12], replicated, may hold values from -4 to 4
- out_weight: bfloat16 [768, 768], replicated, may hold values from -0.625 to 0.625
- norm2_gain: float32 [768], replicated, may hold values from 0.1 to 1.9
- router_weight: bfloat16 [768, 64], replicated, may hold values from -0.21875 to 0.21875
- up_weight: bfloat16 [64, 768, 3072], P('expert'), may hold values from -0.21875 to 0.21875
- down_weight: bfloat16 [64, 3072, 768], P('expert'), may hold values from -2.5 to 2.5
- out_grad: bfloat16 [16384, 768], P(('dp', 'expert')), may hold values from -6 to 6
Outputs:
- block_out: bfloat16 [16384, 768], P(('dp', 'expert'))
- input_grad: bfloat16 [16384, 768], P(('dp', 'expert'))
- norm1_grad: float32 [768], replicated
- qkv_grad: float32 [768, 2304], replicated
- bias_grad: float32 [32, 12], replicated
- outw_grad: float32 [768, 768], replicated
- norm2_grad: float32 [768], replicated
- router_grad: float32 [768, 64], replicated
- up_grad: float32 [64, 768, 3072], P('expert', None, 'dp')
- down_grad: float32 [64, 3072, 768], P('expert', 'dp')
- rms_stats: float32 [3], replicated
The draws below stay inside these ranges and needn't reach their ends.
Inputs may be any that keep to these rules, and one draw needn't show every extreme that they name: `doc_ids`: within each sequence document numbers never fall; each document has 1 to 256 tokens. `valid_mask`: 1 marks a real token. `expert_ids`: the two experts of a token differ; within the 512 tokens of one sequence no expert is named by more than 24 tokens, a bound that some block reaches. `bucket_table`: never falls with the distance and rises by at most one from one distance to the next; distances 0 to 3 have buckets 0 to 3; the last distance has bucket 32 - 1.
All inputs are finite; a program needn't handle non-finite values. No bound on the sum of `valid_mask` on one device may be relied on, other than what follows from the above.
Results may differ from the reference program's by a relative error of at most 0.013.
Values may be sent and summed in bfloat16 or wider, within the bound.
No kernel may reach another device: no remote copies, remote signals or barrier semaphores. Data moves between devices by JAX's collectives and lax.ppermute only.
A program may use at most 512 MiB of HBM per device.

```python
import math
import jax
import jax.numpy as jnp
import numpy as np
from jax import lax

D = 768
HEADS = 12
HEAD_DIM = 64
FF = 3072
EXPERTS = 64
TOP = 2
NBUCKET = 32
QBLOCK = 512
DOCS = 8
SEQ = 512
DOC_MOST = 256
CAP = 24
SEQS = 32
TOKENS = 16384


def draw_hidden_in(key, part):
    base_key, row_key, column_key = jax.random.split(key, 3)
    position = jnp.arange(TOKENS, dtype=jnp.float32)[:, None] / TOKENS
    row_scale = 10.0 ** (jax.random.uniform(row_key, (TOKENS, 1)) - 0.5)
    column_scale = 10.0 ** (jax.random.uniform(column_key, (1, D)) - 0.5)
    base_values = jnp.clip(jax.random.normal(base_key, (TOKENS, D)), -6.0, 6.0)
    rising = 3.0 ** (position - 0.5)
    return (base_values * row_scale * column_scale * rising).astype(jnp.bfloat16)


def draw_bucket_table(key, part):
    shuffled = jax.random.permutation(key, SEQ - 4) + 4
    chosen = shuffled[:NBUCKET - 4].astype(jnp.int32)
    nearby = jnp.arange(1, 4, dtype=jnp.int32)
    bounds = jnp.concatenate([nearby, chosen])
    distance = jnp.arange(SEQ, dtype=jnp.int32)
    return jnp.sum((distance[:, None] >= bounds[None, :]).astype(jnp.int32), axis=1)


def with_ends(entries, own_key, smallest, high):
    longest = entries.shape.index(max(entries.shape))
    spots = []
    for shift in (0, 1):
        where = [jax.random.randint(jax.random.fold_in(own_key, axis), (), 0, length) for axis, length in enumerate(entries.shape)]
        where[longest] = (where[longest] + shift) % entries.shape[longest]
        spots.append(tuple(where))
    return entries.at[spots[0]].set(smallest).at[spots[1]].set(high)


def block_levels(own_key, shape, cuts, smallest, largest):
    level = 1.0
    for dim, blocks in cuts:
        steps = jax.random.uniform(jax.random.fold_in(jax.random.fold_in(own_key, 6), dim), (blocks,), jnp.float32, smallest / len(cuts), largest / len(cuts))
        level = level * jnp.repeat(jnp.exp(steps), shape[dim] // blocks).reshape((-1,) + (1,) * (len(shape) - 1 - dim))
    return level


def split_up(count, total, most, lean):
    weights = [(1 << 20) // math.isqrt(rank ** lean) + 1 for rank in range(2, count + 1)]
    rest, given = total - most - (count - 1), [1] * (count - 1)
    while rest > 0:
        candidates = [i for i in range(count - 1) if given[i] < most]
        whole, left = sum([weights[i] for i in candidates]), rest
        for i in candidates:
            extra = min(most - given[i], max(1, left * weights[i] // whole), rest)
            given[i] = given[i] + extra
            rest = rest - extra
    return np.array([most] + given)


def ragged_sizes(key, amount, total, limit, skew):
    if amount == 2:
        one = jax.random.randint(key, (), max(1, total - limit), min(limit, total - 1) + 1)
        return jnp.stack([one, total - one])
    tallies = jnp.asarray(split_up(amount, total, limit, skew), jnp.int32)
    couples = (amount - 1) // 2
    donor, taker = tallies[1:1 + 2 * couples:2], tallies[2:2 + 2 * couples:2]
    slack = jnp.minimum(donor - 1, limit - taker)
    shifted = jax.random.randint(jax.random.fold_in(key, 1), (couples,), 0, 1 << 20) % (slack + 1)
    tallies = tallies.at[1:1 + 2 * couples:2].set(donor - shifted).at[2:2 + 2 * couples:2].set(taker + shifted)
    return tallies[jax.random.permutation(jax.random.fold_in(key, 2), amount)]


def assign_block(rng, own, number, rows, number_of, top, bound, skew):
    sequence = jax.random.permutation(rng, number_of)
    packed, ordinary = portions_of(number_of, rows * top, bound, skew, True), portions_of(number_of, rows * top, bound, skew, False)
    places = jnp.arange(number_of)

    def named(lengths, rotation):
        used = int((lengths > 0).sum())
        fixed = max(1, used // 4)
        passed = fixed + (places - fixed + rotation * (used - fixed)) % max(1, number_of - fixed)
        return jnp.zeros((number_of,), jnp.int32).at[sequence[jnp.where(places < fixed, places, passed)]].set(jnp.asarray(lengths, jnp.int32))

    lengths = jnp.where(number % 4 == 0, named(packed, number // 4), named(ordinary, number - number // 4 - 1))
    mixed = jax.random.permutation(jax.random.fold_in(own, 3), number_of)
    source_of, taker = mixed[0:number_of // 2 * 2:2], mixed[1:number_of // 2 * 2:2]
    room = jnp.minimum(lengths[source_of] - 1, bound - lengths[taker]) // 2
    room = jnp.where((source_of == sequence[0]) | (taker == sequence[0]) | (lengths[taker] == 0), 0, jnp.maximum(room, 0))
    passed = jax.random.randint(jax.random.fold_in(own, 4), (number_of // 2,), 0, 1 << 20) % (room + 1)
    lengths = lengths.at[source_of].add(-passed).at[taker].add(passed)
    members = jnp.searchsorted(jnp.cumsum(lengths), jnp.arange(rows * top), side="right").astype(jnp.int32)
    table = members.reshape(top, rows).T
    table = table[jax.random.permutation(jax.random.fold_in(own, 1), rows)]
    rotation = jax.random.randint(jax.random.fold_in(own, 2), (rows, 1), 0, top)
    return jnp.take_along_axis(table, (jnp.arange(top)[None, :] + rotation) % top, axis=1)


def portions_of(number_of, total, reach, lean, full):
    weights = [(1 << 20) // math.isqrt(grade ** lean) + 1 for grade in range(1, number_of + 1)]
    largest = reach if full else min(reach, max(-(-total // number_of), total * weights[0] // sum(weights)))
    least = 1 if total - largest >= number_of - 1 else 0
    holding, rest = [largest] + [least] * (number_of - 1), total - largest - least * (number_of - 1)
    while rest > 0:
        free = [i for i in range(1, number_of) if holding[i] < largest] or [i for i in range(1, number_of) if holding[i] < reach]
        pool, remaining = sum([weights[i] for i in free]), rest
        for i in free:
            more = min(reach - holding[i], max(1, remaining * weights[i] // pool), rest)
            holding[i] = holding[i] + more
            rest = rest - more
    return np.array(holding)


def bell_draw(stream_key, extent, width, limit, shards=(), kind=jnp.bfloat16):
    level = block_levels(stream_key, extent, shards, -0.22, 0.18) if shards else 1.0
    values = jax.random.normal(stream_key, extent, jnp.float32) * width * level
    return jnp.minimum(jnp.maximum(values, -limit), limit).astype(kind)


def setup_inputs(seed: int = 0) -> dict:
    key_of = jax.random.split(jax.random.key(seed), 15)
    hidden_in = draw_hidden_in(jax.random.fold_in(key_of[14], 71), 0)
    doc_ids = jax.vmap(lambda own: jnp.searchsorted(jnp.cumsum(ragged_sizes(own, DOCS, SEQ, DOC_MOST, 2)), jnp.arange(SEQ), side="right"))(jax.random.split(key_of[1], SEQS)).reshape((SEQS, SEQ)).astype(jnp.int32)
    valid_mask = with_ends((jax.random.randint(key_of[2], (SEQS, SEQ), 0, 8) < 7).astype(jnp.int32), jax.random.fold_in(key_of[2], 1), 0, 1)
    expert_ids_keys = jax.random.split(jax.random.fold_in(key_of[3], 1), TOKENS // SEQ)
    expert_ids_turns = jax.random.permutation(jax.random.fold_in(key_of[3], 3), TOKENS // SEQ)
    expert_ids = jax.vmap(lambda own, number: assign_block(jax.random.fold_in(key_of[3], 2), own, number, SEQ, EXPERTS, TOP, CAP, 2))(expert_ids_keys, expert_ids_turns).reshape((TOKENS, TOP))
    bucket_table = draw_bucket_table(jax.random.fold_in(key_of[14], 71), 0)
    norm1_gain = jnp.clip(1.0 + 0.18 * jax.random.normal(key_of[5], (D,), jnp.float32), 0.1, 1.9)
    qkv_weight = bell_draw(key_of[6], (D, 3 * D), D ** -0.5, 0.21875)
    position_bias = bell_draw(key_of[7], (NBUCKET, HEADS), 1.0, 4.0, (), jnp.float32)
    out_weight = bell_draw(key_of[8], (D, D), (D // 8) ** -0.5, 0.625)
    norm2_gain = jnp.clip(1.0 + 0.18 * jax.random.normal(key_of[9], (D,), jnp.float32), 0.1, 1.9)
    router_weight = bell_draw(key_of[10], (D, EXPERTS), D ** -0.5, 0.21875)
    up_weight = bell_draw(key_of[11], (EXPERTS, D, FF), D ** -0.5, 0.21875, ((0, 8),))
    down_weight = bell_draw(key_of[12], (EXPERTS, FF, D), (max(FF // 512, 1)) ** -0.5, 2.5, ((0, 8),))
    out_grad = bell_draw(key_of[13], (TOKENS, D), 1.0, 6.0, ((0, 32),))
    return dict(hidden_in=hidden_in, doc_ids=doc_ids, valid_mask=valid_mask, expert_ids=expert_ids, bucket_table=bucket_table, norm1_gain=norm1_gain, qkv_weight=qkv_weight, position_bias=position_bias, out_weight=out_weight, norm2_gain=norm2_gain, router_weight=router_weight, up_weight=up_weight, down_weight=down_weight, out_grad=out_grad)


@jax.custom_vjp
def low(v):
    return lax.optimization_barrier(v.astype(jnp.bfloat16)).astype(jnp.float32)

@jax.custom_vjp
def low_back(v):
    return v

def low_keep(v):
    return (low(v), None)

def low_pass(kept, grad):
    return (grad,)

def back_keep(v):
    return (v, None)

def back_low(kept, grad):
    return (low(grad),)
low.defvjp(low_keep, low_pass)
low_back.defvjp(back_keep, back_low)
EPSILON = 1e-06
HIGHEST = lax.Precision.HIGHEST

def rms_normal(values, gain):
    factor = lax.rsqrt(lax.optimization_barrier(jnp.mean(values * values, axis=-1, keepdims=True)) + EPSILON)
    return values * factor * gain

def attention_block(offset, query_rows, key_rows, value_rows, doc_row, valid_row, bias_dist):
    key_index = jnp.arange(SEQ, dtype=jnp.int32)
    query_index = offset + jnp.arange(QBLOCK, dtype=jnp.int32)
    distance = query_index[:, None] - key_index[None, :]
    query_doc = lax.dynamic_slice_in_dim(doc_row, offset, QBLOCK, 0)
    allowed = (distance >= 0) & (query_doc[:, None] == doc_row[None, :]) & ((valid_row[None, :] == 1) | (distance == 0))
    biases = jnp.take(bias_dist, jnp.maximum(distance, 0), axis=1)
    query_part = lax.dynamic_slice_in_dim(query_rows, offset, QBLOCK, 0)
    raw_scores = jnp.einsum('qhd,khd->hqk', query_part, key_rows, precision=HIGHEST) * HEAD_DIM ** (-0.5) + biases
    scores = jnp.where(allowed[None], low_back(raw_scores), -1e+30)
    weights = low(jax.nn.softmax(scores, axis=-1))
    return jnp.einsum('hqk,khd->qhd', weights, value_rows, precision=HIGHEST)

def reference(hidden_in, doc_ids, valid_mask, expert_ids, bucket_table, norm1_gain, qkv_weight, position_bias, out_weight, norm2_gain, router_weight, up_weight, down_weight, out_grad):
    seq_count = hidden_in.shape[0] // SEQ
    inputs_all = hidden_in.astype(jnp.float32).reshape(seq_count, SEQ, D)
    experts_all = expert_ids.reshape(seq_count, SEQ, TOP)
    params = (norm1_gain.astype(jnp.float32), qkv_weight.astype(jnp.float32), position_bias.astype(jnp.float32), out_weight.astype(jnp.float32), norm2_gain.astype(jnp.float32), router_weight.astype(jnp.float32), up_weight.astype(jnp.float32), down_weight.astype(jnp.float32))
    bucket_hot = (bucket_table[:, None] == jnp.arange(NBUCKET, dtype=jnp.int32)[None, :]).astype(jnp.float32)
    block_starts = jnp.arange(SEQ // QBLOCK, dtype=jnp.int32) * QBLOCK

    def sequence_forward(inputs, weights_all):
        input_row, doc_row, valid_row, expert_row = inputs
        gain_one, qkv_mat, bias_table, out_mat, gain_two, router_mat, up_mats, down_mats = weights_all
        normed_one = low(rms_normal(input_row, gain_one))
        qkv_all = low(low_back(jnp.dot(normed_one, qkv_mat, precision=HIGHEST)))
        query_rows = qkv_all[:, :D].reshape(SEQ, HEADS, HEAD_DIM)
        key_rows = qkv_all[:, D:2 * D].reshape(SEQ, HEADS, HEAD_DIM)
        value_rows = qkv_all[:, 2 * D:].reshape(SEQ, HEADS, HEAD_DIM)
        bias_dist = jnp.dot(bucket_hot, bias_table, precision=HIGHEST).T

        def one_block(offset):
            return attention_block(offset, query_rows, key_rows, value_rows, doc_row, valid_row, bias_dist)
        attended = lax.map(jax.checkpoint(one_block), block_starts)
        context = low(low_back(attended.reshape(SEQ, D)))
        branch = low_back(jnp.dot(context, out_mat, precision=HIGHEST))
        residual = input_row + branch
        normed_two = low(rms_normal(residual, gain_two))
        logits = low_back(jnp.dot(normed_two, router_mat, precision=HIGHEST))
        router_probs = jax.nn.softmax(logits, axis=-1)
        gate_values = jnp.take_along_axis(router_probs, expert_row, axis=1)
        flat_ids = expert_row.reshape(-1)
        matches = (flat_ids[:, None] == jnp.arange(EXPERTS, dtype=jnp.int32)[None, :]).astype(jnp.int32)
        ranking = lax.optimization_barrier(jnp.sum(jnp.cumsum(matches, axis=0) * matches, axis=1)) - 1
        places = (flat_ids * CAP + ranking).astype(jnp.int32)
        filled = jnp.zeros((EXPERTS * CAP, D), jnp.float32).at[places].set(jnp.repeat(normed_two, TOP, axis=0))
        filled = low_back(filled).reshape(EXPERTS, CAP, D)
        inner = low_back(jnp.einsum('ecd,edf->ecf', filled, up_mats, precision=HIGHEST))
        active = low(jax.nn.gelu(inner, approximate=True))
        result = low(low_back(jnp.einsum('ecf,efd->ecd', active, down_mats, precision=HIGHEST)))
        picked = result.reshape(EXPERTS * CAP, D)[places].reshape(SEQ, TOP, D)
        mixture = lax.optimization_barrier(jnp.sum(gate_values[:, :, None] * picked, axis=1))
        output = residual + mixture
        validity = valid_row.astype(jnp.float32)[:, None]
        sums = jnp.stack([jnp.sum(validity * output * output), jnp.sum(validity * branch * branch), jnp.sum(validity * mixture * mixture)])
        return (output, sums)

    def forward(inputs_all, weights_all):

        def one_sequence(inputs):
            return sequence_forward(inputs, weights_all)
        outputs, sums = lax.map(jax.checkpoint(one_sequence), (inputs_all, doc_ids, valid_mask, experts_all))
        return (outputs, sums)
    outputs, pullback, sums = jax.vjp(forward, inputs_all, params, has_aux=True)
    input_grad, param_grads = pullback(out_grad.astype(jnp.float32).reshape(seq_count, SEQ, D))
    totals = lax.optimization_barrier(jnp.sum(sums, axis=0))
    count = jnp.maximum(jnp.sum(valid_mask.astype(jnp.float32)), 1.0)
    rms_stats = jnp.sqrt(totals / (count * D))
    return (outputs.reshape(-1, D).astype(jnp.bfloat16), input_grad.reshape(-1, D).astype(jnp.bfloat16), param_grads[0], param_grads[1], param_grads[2], param_grads[3], param_grads[4], param_grads[5], param_grads[6], param_grads[7], rms_stats)
```

```python
import functools

import jax
import jax.numpy as jnp
from jax import lax
from jax.experimental import pallas as pl
from jax.experimental.pallas import tpu as pltpu
from jax.sharding import PartitionSpec as P

HEADS = 12
HEAD_DIM = 64
NBUCKET = 32
CAP = 24
BLOCK = 128
WINDOW = 3
PAIR = 2 * HEAD_DIM
EPSILON = 1e-06
NEGATIVE = -1e30
HIGHEST = lax.Precision.HIGHEST
BF16 = jnp.bfloat16
F32 = jnp.float32
SUBSTEPS = 6
VMEM_LIMIT = 58 * 1024 * 1024


NN = (((1,), (0,)), ((), ()))
NT = (((1,), (1,)), ((), ()))
TN = (((0,), (0,)), ((), ()))


def dot(left, right, dims=NN, precision=None):
    return lax.dot_general(left, right, dims, precision=precision, preferred_element_type=F32)


def iota(shape, dim):
    return lax.broadcasted_iota(jnp.int32, shape, dim)


def whole(shape):
    return pl.BlockSpec(shape, lambda *_: (0,) * len(shape))


def params(**more):
    return pltpu.CompilerParams(vmem_limit_bytes=VMEM_LIMIT, **more)


def cost(microseconds):
    return pl.CostEstimate(
        flops=int(microseconds * 1.1e9), bytes_accessed=1000, transcendentals=0
    )


def windows(length):
    found = []
    row = 0
    for number in range(length // BLOCK):
        first = max(number - WINDOW + 1, 0)
        keys = (number - first + 1) * BLOCK
        found.append((number * BLOCK, first * BLOCK, keys, row))
        row += keys
    return found, row


def rms(values):
    return lax.rsqrt(jnp.mean(values * values, axis=-1, keepdims=True) + EPSILON)


def hot_columns(row0, row1, count, offset):
    slots = iota((count, row0.shape[1]), 0) + offset
    return jnp.where((slots == row0) | (slots == row1), 1.0, 0.0).astype(BF16)


def hot_rows(col0, col1, count, offset):
    slots = iota((col0.shape[0], count), 1) + offset
    return jnp.where((slots == col0) | (slots == col1), 1.0, 0.0).astype(BF16)


def route_kernel(ids_ref, send_ref, keep_ref, grad_ref, row_ref, col_ref, rows_ref):
    length = grad_ref.shape[0]
    experts = rows_ref.shape[0] // CAP
    before = iota((length, length), 0) < iota((length, length), 1)
    upper = jnp.where(before, 1.0, 0.0).astype(BF16)
    after = iota((length, length), 0) > iota((length, length), 1)
    lower = jnp.where(after, 1.0, 0.0).astype(BF16)
    number = iota((experts, length), 0)
    hot = [number == ids_ref[c : c + 1, :] for c in range(2)]
    both = jnp.where(hot[0] | hot[1], 1.0, 0.0).astype(BF16)
    rank = dot(both, upper)
    rows = []
    for c in range(2):
        mine = jnp.sum(jnp.where(hot[c], rank, 0.0), axis=0, keepdims=True).astype(jnp.int32)
        rows.append(ids_ref[c : c + 1, :] * CAP + mine)
        row_ref[c : c + 1, :] = send_ref[c : c + 1, :] * CAP + mine
    number = iota((length, experts), 1)
    hot = [number == keep_ref[:, c : c + 1] for c in range(2)]
    both = jnp.where(hot[0] | hot[1], 1.0, 0.0).astype(BF16)
    rank = dot(lower, both)
    for c in range(2):
        mine = jnp.sum(jnp.where(hot[c], rank, 0.0), axis=1, keepdims=True).astype(jnp.int32)
        for kind in range(2):
            at = slice(2 * kind + c, 2 * kind + c + 1)
            col_ref[:, at] = keep_ref[:, at] * CAP + mine
    chosen = hot_columns(rows[0], rows[1], rows_ref.shape[0], 0)
    rows_ref[...] = dot(chosen, grad_ref[...]).astype(BF16)


def route(ids, send_ids, keep_ids, out_grad, slots):
    length, width = out_grad.shape
    return pl.pallas_call(
        route_kernel,
        out_shape=(
            jax.ShapeDtypeStruct((2, length), jnp.int32),
            jax.ShapeDtypeStruct((length, 4), jnp.int32),
            jax.ShapeDtypeStruct((slots, width), BF16),
        ),
        compiler_params=params(),
        cost_estimate=cost(5),
        name="route",
    )(ids.T, send_ids.T, jnp.concatenate([keep_ids, ids], axis=1), out_grad)


def forward_kernel(
    x_ref, gain1_ref, qkvw_ref, outw_ref, gain2_ref, docr_ref, docc_ref, validc_ref, bucket_ref,
    pbias_ref, row_ref,
    probs_ref, qkv_ref, n1t_ref, ctx_ref, residual_ref, stat_ref, *rest,
):
    rows_refs, (mask_s, bias_s, toeplitz_s) = rest[:-3], rest[-3:]
    pair = pl.program_id(0)
    length, width = x_ref.shape
    spans, _ = windows(length)

    @pl.when(pair == 0)
    def _():
        x = x_ref[...].astype(F32)
        n1 = (x * rms(x) * gain1_ref[...]).astype(BF16)
        n1t_ref[...] = n1.T
        for j in range(3):
            part = slice(j * width, (j + 1) * width)
            qkv_ref[:, part] = dot(n1, qkvw_ref[:, part]).astype(BF16)
        for q0, k0, keys, row in spans:
            shape = (keys, BLOCK)
            distance = (iota(shape, 1) + q0) - (iota(shape, 0) + k0)
            allowed = (
                (distance >= 0)
                & (docc_ref[k0 : k0 + keys, :] == docr_ref[:, q0 : q0 + BLOCK])
                & ((validc_ref[k0 : k0 + keys, :] == 1) | (distance == 0))
            )
            mask_s[row : row + keys, :] = jnp.where(allowed, 0.0, NEGATIVE)
        span = bias_s.shape[1]
        hot = jnp.where(iota((NBUCKET, span), 0) == bucket_ref[...], 1.0, 0.0)
        bias_s[...] = dot(pbias_ref[...], hot, precision=HIGHEST)

    for side in range(2):
        head_bias = bias_s[pl.ds(2 * pair + side, 1), :]
        for m in range(WINDOW):
            ahead = head_bias[:, m * BLOCK : (m + 1) * BLOCK]
            back = max(m - 1, 0)
            behind = head_bias[:, back * BLOCK : (back + 1) * BLOCK]
            lanes = jnp.broadcast_to(
                jnp.concatenate([ahead, behind], axis=1), (BLOCK, 2 * BLOCK)
            )
            rolled = pltpu.roll(lanes, 0, 1, stride=1, stride_axis=0)
            place = (WINDOW - 1 - m) * BLOCK
            toeplitz_s[place : place + BLOCK, side * BLOCK : (side + 1) * BLOCK] = rolled[
                :, :BLOCK
            ]

    at = pl.multiple_of(pair * PAIR, PAIR)
    first_head = iota((BLOCK, PAIR), 1) < HEAD_DIM
    top = iota((PAIR, BLOCK), 0) < HEAD_DIM
    for q0, k0, keys, row in spans:
        q = qkv_ref[q0 : q0 + BLOCK, pl.ds(at, PAIR)].astype(F32) * HEAD_DIM ** (-0.5)
        stacked = jnp.concatenate(
            [jnp.where(first_head, q, 0.0), jnp.where(first_head, 0.0, q)], axis=0
        ).astype(BF16)
        k = qkv_ref[k0 : k0 + keys, pl.ds(pl.multiple_of(width + at, PAIR), PAIR)]
        v = qkv_ref[k0 : k0 + keys, pl.ds(pl.multiple_of(2 * width + at, PAIR), PAIR)]
        scores = dot(k, stacked, NT)
        masked = mask_s[row : row + keys, :]
        for side in range(2):
            lanes = slice(side * BLOCK, (side + 1) * BLOCK)
            s = scores[:, lanes] + toeplitz_s[WINDOW * BLOCK - keys :, lanes] + masked
            peak = jnp.max(s, axis=0, keepdims=True)
            e = jnp.exp(s - peak)
            total = jnp.sum(e, axis=0, keepdims=True)
            probs_ref[0, row : row + keys, lanes] = (e * (1.0 / total)).astype(BF16)
        both = dot(v, probs_ref[0, row : row + keys, :], TN)
        ctx = jnp.where(top, both[:, :BLOCK], both[:, BLOCK:])
        ctx_ref[pl.ds(at, PAIR), q0 : q0 + BLOCK] = ctx.astype(BF16)

    @pl.when(pair == pl.num_programs(0) - 1)
    def _():
        branch = dot(ctx_ref[...], outw_ref[...], TN)
        valid = validc_ref[...].astype(F32)
        stat_ref[...] = jnp.sum(valid * branch * branch, axis=0, keepdims=True)
        residual = x_ref[...].astype(F32) + branch
        residual_ref[...] = residual
        n2 = (residual * rms(residual) * gain2_ref[...]).astype(BF16)
        offset = 0
        for out in rows_refs:
            chosen = hot_columns(row_ref[0:1, :], row_ref[1:2, :], out.shape[0], offset)
            out[...] = dot(chosen, n2).astype(BF16)
            offset += out.shape[0]


def attention_forward(
    x, gain1, qkvw, outw, gain2, docs, valid, bucket_table, position_bias, place_row, sizes
):
    length, width = x.shape
    _, stored = windows(length)
    pairs = width // PAIR
    span = WINDOW * BLOCK
    padded_heads = -(-HEADS // 8) * 8
    bias_t = jnp.zeros((padded_heads, NBUCKET), F32).at[:HEADS].set(position_bias.T)
    arguments = (
        x, gain1[None], qkvw, outw, gain2[None], docs, docs.T, valid.T,
        bucket_table[None, :span], bias_t, place_row,
    )
    out_shape = (
        jax.ShapeDtypeStruct((pairs, stored, 2 * BLOCK), BF16),
        jax.ShapeDtypeStruct((length, 3 * width), BF16),
        jax.ShapeDtypeStruct((width, length), BF16),
        jax.ShapeDtypeStruct((width, length), BF16),
        jax.ShapeDtypeStruct((length, width), F32),
        jax.ShapeDtypeStruct((1, width), F32),
    ) + tuple(jax.ShapeDtypeStruct((n, width), BF16) for n in sizes)
    return pl.pallas_call(
        forward_kernel,
        grid=(pairs,),
        in_specs=[whole(a.shape) for a in arguments],
        out_specs=[pl.BlockSpec((1, stored, 2 * BLOCK), lambda p: (p, 0, 0))]
        + [whole(s.shape) for s in out_shape[1:]],
        out_shape=out_shape,
        scratch_shapes=[
            pltpu.VMEM((stored, BLOCK), F32),
            pltpu.VMEM((padded_heads, span), F32),
            pltpu.VMEM((span, 2 * BLOCK), F32),
        ],
        compiler_params=params(),
        cost_estimate=cost(22),
        name="attention_forward",
    )(*arguments)


def expert_gate(rows, router, expert):
    logits = dot(rows, router)
    shifted = jnp.exp(logits - jnp.max(logits, axis=-1, keepdims=True))
    probs = shifted / jnp.sum(shifted, axis=-1, keepdims=True)
    mine = iota(probs.shape, 1) == expert
    return probs, mine, jnp.sum(jnp.where(mine, probs, 0.0), axis=-1, keepdims=True)


GELU_SCALE = 0.7978845608028654
GELU_CUBE = 0.044715


def gelu_parts(v):
    square = v * v
    t = jnp.tanh(v * (GELU_SCALE + (GELU_SCALE * GELU_CUBE) * square))
    half = 0.5 * v
    value = half + half * t
    slope = 0.5 + 0.5 * t + half * (1.0 - t * t) * (
        GELU_SCALE + (3.0 * GELU_SCALE * GELU_CUBE) * square
    )
    return value, slope


def active_grad_kernel(grads_ref, down_ref, out_ref, g_s, grads_s):
    e, f = pl.program_id(0), pl.program_id(1)

    @pl.when((e == 0) & (f == 0))
    def _():
        grads_s[...] = grads_ref[...].astype(F32)

    @pl.when(f == 0)
    def _():
        here = pl.ds(pl.multiple_of(e * CAP, CAP), CAP)
        g_s[...] = grads_s[:, here, :].reshape(g_s.shape).astype(BF16)

    out_ref[0] = dot(g_s[...], down_ref[0], NT).astype(BF16)


def active_grads(grads, down_weight, blocks=1):
    owners, slots, width = grads.shape
    experts, inner, _ = down_weight.shape
    step, count = inner // blocks, owners * CAP
    return pl.pallas_call(
        active_grad_kernel,
        grid=(experts, blocks),
        in_specs=[
            whole(grads.shape),
            pl.BlockSpec((1, step, width), lambda e, f: (e, f, 0)),
        ],
        out_specs=pl.BlockSpec((1, count, step), lambda e, f: (e, 0, f)),
        out_shape=jax.ShapeDtypeStruct((experts, count, inner), BF16),
        scratch_shapes=[pltpu.VMEM((count, width), BF16), pltpu.VMEM(grads.shape, F32)],
        compiler_params=params(),
        cost_estimate=cost(22),
        name="active_grads",
    )(grads, down_weight)


def expert_kernel(scalar_ref, *refs, parts, aliased, last):
    rows_refs, refs = refs[:parts], refs[parts:]
    side_ref, up_ref, router_ref = refs[:3]
    refs = refs[3 + aliased :]
    back_refs, refs = refs[: 1 + last], refs[1 + last :]
    active_ref, router_grad_ref = refs[:2]
    rows_s, back_s, x_s, probs_s, gate_s, sum_s, dx_s, grad_s = refs[2:]
    e, f = pl.program_id(0), pl.program_id(1)
    experts, blocks = pl.num_programs(0), pl.num_programs(1)
    me = scalar_ref[1]
    expert = scalar_ref[0] + e
    count, width = x_s.shape
    owners = rows_s.shape[0]
    here = pl.ds(pl.multiple_of(e * CAP, CAP), CAP)

    @pl.when((e == 0) & (f == 0))
    def _():
        if parts == 1:
            rows_s[...] = rows_refs[0][...].astype(F32)
        else:
            for k in range(parts):
                rows_s[me ^ k] = rows_refs[k][...].astype(F32)
        router_grad_ref[...] = jnp.zeros_like(router_grad_ref)

    @pl.when(f == 0)
    def _():
        x = rows_s[:, here, :].reshape(count, width).astype(BF16)
        x_s[...] = x
        probs, _, gate = expert_gate(x, router_ref[...], expert)
        probs_s[...] = probs
        gate_s[...] = jnp.broadcast_to(gate, gate_s.shape)
        sum_s[...] = jnp.zeros_like(sum_s)
        dx_s[...] = jnp.zeros_like(dx_s)

    gate = gate_s[:, :1]
    x = x_s[...]
    step = up_ref.shape[2] // SUBSTEPS
    total = None
    inner = dot(x, up_ref[0, :, :step])
    for s in range(SUBSTEPS):
        here_f = slice(s * step, (s + 1) * step)
        later = dot(x, up_ref[0, :, (s + 1) * step : (s + 2) * step]) if s + 1 < SUBSTEPS else None
        value, slope = gelu_parts(inner)
        side = side_ref[0, :, here_f].astype(F32) * gate
        part = jnp.sum(value * side, axis=-1, keepdims=True)
        total = part if total is None else total + part
        active_ref[0, :, here_f] = (gate * value).astype(BF16)
        grad_s[:, here_f] = (side * slope).astype(BF16)
        inner = later
    sum_s[...] += total
    dx_s[...] += dot(grad_s[...], up_ref[0], NT)

    @pl.when(f == blocks - 1)
    def _():
        probs = probs_s[...]
        mine = iota(probs.shape, 1) == expert
        logit_grad = (sum_s[:, :1] * (jnp.where(mine, 1.0, 0.0) - probs)).astype(BF16)
        router_grad_ref[...] += dot(logit_grad, x_s[...], TN)
        dx = dx_s[...] + dot(logit_grad, router_ref[...], NT)
        back_s[:, here, :] = dx.reshape(owners, CAP, width)

    @pl.when((e == experts - 1) & (f == blocks - 1))
    def _():
        if last:
            for source in range(owners):
                back_refs[source % 2][source // 2] = back_s[me ^ source].astype(BF16)
        else:
            back_refs[0][...] = back_s[...].astype(BF16)


def run_experts(rows, side, up_weight, router, scalars, first, old, last, blocks=1):
    parts = len(rows)
    slots, width = rows[0].shape[-2:]
    owners = parts if parts > 1 else rows[0].shape[0]
    experts = slots // CAP
    local, _, inner = up_weight.shape
    step, count, kinds = inner // blocks, owners * CAP, router.shape[1]
    backs = [jax.ShapeDtypeStruct((owners, slots, width), BF16)]
    if last:
        backs = [jax.ShapeDtypeStruct((owners // 2, slots, width), BF16)] * 2
    in_specs = [whole(r.shape) for r in rows] + [
        pl.BlockSpec((1, count, step), lambda e, f, _: (first + e, 0, f)),
        pl.BlockSpec((1, width, step), lambda e, f, _: (first + e, 0, f)),
        whole(router.shape),
    ]
    arguments = (*rows, side, up_weight, router)
    aliases = {}
    if old is not None:
        aliases = {1 + len(arguments): len(backs)}
        in_specs.append(pl.BlockSpec(memory_space=pl.ANY))
        arguments += (old,)
    return pl.pallas_call(
        functools.partial(expert_kernel, parts=parts, aliased=len(aliases), last=last),
        grid_spec=pltpu.PrefetchScalarGridSpec(
            num_scalar_prefetch=1,
            grid=(experts, blocks),
            in_specs=in_specs,
            out_specs=[whole(back.shape) for back in backs]
            + [
                pl.BlockSpec((1, count, step), lambda e, f, _: (first + e, 0, f)),
                whole((kinds, width)),
            ],
            scratch_shapes=[
                pltpu.VMEM((owners, slots, width), F32),
                pltpu.VMEM((owners, slots, width), F32),
                pltpu.VMEM((count, width), BF16),
                pltpu.VMEM((count, kinds), F32),
                pltpu.VMEM((count, BLOCK), F32),
                pltpu.VMEM((count, BLOCK), F32),
                pltpu.VMEM((count, width), F32),
                pltpu.VMEM((count, step), BF16),
            ],
        ),
        out_shape=(
            *backs,
            jax.ShapeDtypeStruct((local, count, inner), BF16),
            jax.ShapeDtypeStruct((kinds, width), F32),
        ),
        input_output_aliases=aliases,
        compiler_params=params(),
        cost_estimate=cost(22),
        name="experts",
    )(scalars + jnp.array([first, 0], jnp.int32), *arguments)


def expert_out_kernel(active_ref, down_ref, out_ref, sum_s, all_s):
    e, f = pl.program_id(0), pl.program_id(1)
    experts, blocks = pl.num_programs(0), pl.num_programs(1)
    part = dot(active_ref[0], down_ref[0])

    @pl.when(f == 0)
    def _():
        sum_s[...] = part

    @pl.when(f > 0)
    def _():
        sum_s[...] += part

    @pl.when(f == blocks - 1)
    def _():
        here = pl.ds(pl.multiple_of(e * CAP, CAP), CAP)
        all_s[:, here, :] = sum_s[...].reshape(all_s.shape[0], CAP, all_s.shape[2])

    @pl.when((e == experts - 1) & (f == blocks - 1))
    def _():
        out_ref[...] = all_s[...].astype(BF16)


def expert_outputs(active, down_weight, blocks=1):
    experts, count, inner = active.shape
    width = down_weight.shape[2]
    step, owners = inner // blocks, count // CAP
    shape = (owners, experts * CAP, width)
    return pl.pallas_call(
        expert_out_kernel,
        grid=(experts, blocks),
        in_specs=[
            pl.BlockSpec((1, count, step), lambda e, f: (e, 0, f)),
            pl.BlockSpec((1, step, width), lambda e, f: (e, f, 0)),
        ],
        out_specs=whole(shape),
        out_shape=jax.ShapeDtypeStruct(shape, BF16),
        scratch_shapes=[pltpu.VMEM((count, width), F32), pltpu.VMEM(shape, F32)],
        compiler_params=params(),
        cost_estimate=cost(0.01),
        name="expert_outputs",
    )(active, down_weight)


def expert_wgrad_kernel(
    scalar_ref, rows_ref, grads_ref, up_ref, down_ref, router_ref, *rest, turned
):
    up_out, down_out, x_s, g_s, wide_s = rest[-5:]
    j, tile = pl.program_id(0), pl.program_id(1)
    count, width = x_s.shape
    taken, _, owners, _, _ = rows_ref.shape
    me = scalar_ref[2]
    for side in range(2):

        @pl.when(j == side)
        def _():
            part = slice(side * CAP, (side + 1) * CAP)
            for k in range(taken):
                for source in range(owners):
                    place = source ^ me if turned else source
                    wide_s[k, source] = rows_ref[k, 0, place].astype(F32)[part, :]
            x = wide_s[...].reshape(count, width).astype(BF16)
            x_s[...] = x
            _, _, gate = expert_gate(x, router_ref[...], scalar_ref[0] + side)
            g = grads_ref[...].astype(F32)[:, :, part, :].reshape(count, width)
            g_s[...] = (gate * g).astype(BF16)

    x, g = x_s[...], g_s[...]
    value, slope = gelu_parts(dot(x, up_ref[0]))
    inner_grad = (dot(g, down_ref[0], NT) * slope).astype(BF16)

    @pl.when(tile == 0)
    def _():
        down_out[0] = dot(value.astype(BF16), g, TN)
        up_out[0] = dot(x, inner_grad, TN)

    @pl.when(tile > 0)
    def _():
        down_out[0] += dot(value.astype(BF16), g, TN)
        up_out[0] += dot(x, inner_grad, TN)


def expert_wgrads(
    rows, grads, up_weight, down_weight, router, scalars, first, turned, old
):
    groups, chunks, owners, _, width = rows.shape
    local, _, inner = up_weight.shape
    each = local // chunks
    share = inner // groups
    taken = max(min(groups, 32 // owners), 1)
    count = taken * owners * CAP
    chunk, at = first // each, first % each // 2
    in_specs = [
        pl.BlockSpec((taken, 1, owners, 2 * CAP, width), lambda j, t, _: (t, chunk, 0, at, 0)),
        pl.BlockSpec((taken, owners, 2 * CAP, width), lambda j, t, _: (t, 0, first // 2, 0)),
        pl.BlockSpec((1, width, share), lambda j, t, s: (first + j, 0, s[1])),
        pl.BlockSpec((1, share, width), lambda j, t, s: (first + j, s[1], 0)),
        whole(router.shape),
    ]
    arguments = (rows, grads, up_weight, down_weight, router)
    aliases = {}
    if old is not None:
        aliases = {6: 0, 7: 1}
        in_specs += [pl.BlockSpec(memory_space=pl.ANY)] * 2
        arguments += tuple(old)
    return pl.pallas_call(
        functools.partial(expert_wgrad_kernel, turned=turned),
        grid_spec=pltpu.PrefetchScalarGridSpec(
            num_scalar_prefetch=1,
            grid=(2, groups // taken),
            in_specs=in_specs,
            out_specs=[
                pl.BlockSpec((1, width, share), lambda j, t, _: (first + j, 0, 0)),
                pl.BlockSpec((1, share, width), lambda j, t, _: (first + j, 0, 0)),
            ],
            scratch_shapes=[
                pltpu.VMEM((count, width), BF16),
                pltpu.VMEM((count, width), BF16),
                pltpu.VMEM((taken, owners, CAP, width), F32),
            ],
        ),
        out_shape=(
            jax.ShapeDtypeStruct((local, width, share), F32),
            jax.ShapeDtypeStruct((local, share, width), F32),
        ),
        input_output_aliases=aliases,
        compiler_params=params(),
        cost_estimate=cost(0.01),
        name="expert_wgrads",
    )(scalars + jnp.array([first, 0, 0], jnp.int32), *arguments)


def residual_kernel(
    col_ref, residual_ref, gain_ref, grad_ref, outw_ref, ctx_ref, router_ref, *rest
):
    back_refs = rest[:-4]
    gain_grad_ref, residual_grad_ref, early_ref, ctx_grad_ref = rest[-4:]
    offset = 0
    n2_grad = None
    for back in back_refs:
        chosen = hot_rows(col_ref[:, 0:1], col_ref[:, 1:2], back.shape[0], offset)
        part = dot(chosen, back[...])
        n2_grad = part if n2_grad is None else n2_grad + part
        offset += back.shape[0]
    residual = residual_ref[...]
    factor = rms(residual)
    unit = residual * factor
    gain_grad_ref[...] = jnp.sum(n2_grad * unit, axis=0, keepdims=True)
    scaled = n2_grad * gain_ref[...]
    centre = jnp.mean(scaled * unit, axis=-1, keepdims=True)
    residual_grad = grad_ref[...].astype(F32) + factor * (scaled - unit * centre)
    residual_grad_ref[...] = residual_grad
    branch_grad = residual_grad.astype(BF16)
    width = ctx_ref.shape[0]
    early_ref[:width, :] = dot(ctx_ref[...], branch_grad).astype(BF16)
    used = width + router_ref.shape[0]
    early_ref[width:used, :] = router_ref[...].astype(BF16)
    if used < early_ref.shape[0]:
        early_ref[used:, :] = jnp.zeros((early_ref.shape[0] - used, width), BF16)
    ctx_grad_ref[...] = dot(branch_grad, outw_ref[...], NT).astype(BF16)


def residual_backward(
    place_col, residual, gain2, out_grad, outw, ctx_t, router_grad, backs, early
):
    length, width = residual.shape
    return pl.pallas_call(
        residual_kernel,
        out_shape=(
            jax.ShapeDtypeStruct((1, width), F32),
            jax.ShapeDtypeStruct((length, width), F32),
            jax.ShapeDtypeStruct((early, width), BF16),
            jax.ShapeDtypeStruct((length, width), BF16),
        ),
        compiler_params=params(),
        cost_estimate=cost(0.01),
        name="residual_backward",
    )(place_col, residual, gain2[None], out_grad, outw, ctx_t, router_grad, *backs)


def attention_backward_kernel(
    q_ref, k_ref, v_ref, dctx_ref, probs_ref, n1t_ref,
    dq_ref, dk_ref, dv_ref, wgrad_ref, bias_ref,
    dqt_s, dk_s, dv_s, diagonal_s,
):
    length = q_ref.shape[0]
    spans, _ = windows(length)
    first_head = iota((BLOCK, PAIR), 1) < HEAD_DIM
    top = iota((PAIR, BLOCK), 0) < HEAD_DIM
    scale = HEAD_DIM ** (-0.5)
    dk_s[...] = jnp.zeros_like(dk_s)
    dv_s[...] = jnp.zeros_like(dv_s)
    diagonal_s[...] = jnp.zeros_like(diagonal_s)

    def stack(values):
        values = values.astype(F32)
        return jnp.concatenate(
            [jnp.where(first_head, values, 0.0), jnp.where(first_head, 0.0, values)], axis=0
        ).astype(BF16)

    for q0, k0, keys, row in spans:
        q = stack(q_ref[q0 : q0 + BLOCK, :])
        dctx = stack(dctx_ref[q0 : q0 + BLOCK, :])
        span = slice(k0, k0 + keys)
        probs = probs_ref[0, row : row + keys, :]
        prob_side = dot(v_ref[span, :], dctx, NT)
        halves = []
        for side in range(2):
            lanes = slice(side * BLOCK, (side + 1) * BLOCK)
            p = probs[:, lanes].astype(F32)
            d = prob_side[:, lanes]
            centre = jnp.sum(p * d, axis=0, keepdims=True)
            s = p * (d - centre)
            diagonal_s[WINDOW * BLOCK - keys :, lanes] += s
            halves.append(s.astype(BF16))
        score_grad = jnp.concatenate(halves, axis=1)
        dk_s[span, :] += dot(score_grad, q)
        dv_s[span, :] += dot(probs, dctx)
        both = dot(k_ref[span, :], score_grad, TN)
        dqt_s[:, q0 : q0 + BLOCK] = jnp.where(top, both[:, :BLOCK], both[:, BLOCK:])
    dq = (dqt_s[...].T * scale).astype(BF16)
    dk = (dk_s[...] * scale).astype(BF16)
    dv = dv_s[...].astype(BF16)
    dq_ref[...] = dq
    dk_ref[...] = dk
    dv_ref[...] = dv
    for j, rows in enumerate((dq, dk, dv)):
        wgrad_ref[j] = dot(n1t_ref[...], rows).astype(wgrad_ref.dtype)
    bias_ref[...] = jnp.zeros_like(bias_ref)
    for side in range(2):
        lanes = slice(side * BLOCK, (side + 1) * BLOCK)
        pieces = []
        for m in range(WINDOW):
            place = (WINDOW - 1 - m) * BLOCK
            block = diagonal_s[place : place + BLOCK, lanes]
            skewed = jnp.zeros((8, 2 * BLOCK), F32)
            for k in range(0, BLOCK, 8):
                eight = block[k : k + 8, :]
                wide = jnp.concatenate([eight, jnp.zeros_like(eight)], axis=1)
                skewed += wide if k == 0 else pltpu.roll(wide, 2 * BLOCK - k, 1)
            for bit in (1, 2, 4):
                moved = pltpu.roll(skewed, 2 * BLOCK - bit, 1)
                skewed = jnp.where(iota(skewed.shape, 0) & bit != 0, moved, skewed)
            pieces.append(jnp.sum(skewed, axis=0, keepdims=True))
        for m in range(WINDOW):
            total = pieces[m][:, :BLOCK]
            if m + 1 < WINDOW:
                total = total + pieces[m + 1][:, BLOCK:]
            bias_ref[0, side : side + 1, m * BLOCK : (m + 1) * BLOCK] = total


def attention_backward(qkv, ctx_grad, probs, n1_t, first, count):
    length, width = ctx_grad.shape
    stored = probs.shape[1]
    pairs = width // PAIR
    span = WINDOW * BLOCK
    column = pl.BlockSpec((length, PAIR), lambda p: (0, p))
    return pl.pallas_call(
        attention_backward_kernel,
        grid=(count,),
        in_specs=[
            pl.BlockSpec((length, PAIR), lambda p: (0, first + p)),
            pl.BlockSpec((length, PAIR), lambda p: (0, pairs + first + p)),
            pl.BlockSpec((length, PAIR), lambda p: (0, 2 * pairs + first + p)),
            pl.BlockSpec((length, PAIR), lambda p: (0, first + p)),
            pl.BlockSpec((1, stored, 2 * BLOCK), lambda p: (first + p, 0, 0)),
            whole(n1_t.shape),
        ],
        out_specs=[
            column,
            column,
            column,
            pl.BlockSpec((3, width, PAIR), lambda p: (0, 0, p)),
            pl.BlockSpec((1, 8, span), lambda p: (p, 0, 0)),
        ],
        out_shape=(
            jax.ShapeDtypeStruct((length, count * PAIR), BF16),
            jax.ShapeDtypeStruct((length, count * PAIR), BF16),
            jax.ShapeDtypeStruct((length, count * PAIR), BF16),
            jax.ShapeDtypeStruct((3, width, count * PAIR), BF16),
            jax.ShapeDtypeStruct((count, 8, span), F32),
        ),
        scratch_shapes=[
            pltpu.VMEM((PAIR, length), F32),
            pltpu.VMEM((length, PAIR), F32),
            pltpu.VMEM((length, PAIR), F32),
            pltpu.VMEM((span, 2 * BLOCK), F32),
        ],
        compiler_params=params(),
        cost_estimate=cost(0.01),
        name="attention_backward",
    )(qkv, qkv, qkv, ctx_grad, probs, n1_t)


def input_kernel(x_ref, gain_ref, residual_grad_ref, qkvw_ref, *rest):
    parts, (grad_ref, gain_grad_ref) = rest[:-2], rest[-2:]
    x = x_ref[...].astype(F32)
    factor = rms(x)
    unit = x * factor
    n1_grad = None
    at = 0
    for part in parts:
        columns = part.shape[1]
        term = dot(part[...], qkvw_ref[:, at : at + columns], NT)
        n1_grad = term if n1_grad is None else n1_grad + term
        at += columns
    gain_grad_ref[...] = jnp.sum(n1_grad * unit, axis=0, keepdims=True)
    scaled = n1_grad * gain_ref[...]
    centre = jnp.mean(scaled * unit, axis=-1, keepdims=True)
    grad_ref[...] = (residual_grad_ref[...] + factor * (scaled - unit * centre)).astype(BF16)


def input_backward(x, gain1, residual_grad, qkvw, parts):
    length, width = x.shape
    return pl.pallas_call(
        input_kernel,
        out_shape=(
            jax.ShapeDtypeStruct((length, width), BF16),
            jax.ShapeDtypeStruct((1, width), F32),
        ),
        compiler_params=params(),
        cost_estimate=cost(0.01),
        name="input_backward",
    )(x, gain1[None], residual_grad, qkvw, *parts)


def output_kernel(col_ref, residual_ref, validc_ref, rows_ref, block_ref, stat_ref):
    chosen = hot_rows(col_ref[:, 2:3], col_ref[:, 3:4], rows_ref.shape[0], 0)
    mixture = dot(chosen, rows_ref[...])
    output = residual_ref[...] + mixture
    block_ref[...] = output.astype(BF16)
    valid = validc_ref[...].astype(F32)
    stat_ref[0:1, :] = jnp.sum(valid * output * output, axis=0, keepdims=True)
    stat_ref[1:2, :] = jnp.sum(valid * mixture * mixture, axis=0, keepdims=True)


def block_output(place_col, residual, valid, rows):
    length, width = residual.shape
    return pl.pallas_call(
        output_kernel,
        out_shape=(
            jax.ShapeDtypeStruct((length, width), BF16),
            jax.ShapeDtypeStruct((2, width), F32),
        ),
        compiler_params=params(),
        cost_estimate=cost(0.01),
        name="block_output",
    )(place_col, residual, valid.T, rows)


def swap(values, axis, bit):
    size = lax.axis_size(axis)
    return lax.ppermute(values, axis, [(i, i ^ bit) for i in range(size)])


def axis_bits(axis):
    size = lax.axis_size(axis)
    bits = []
    bit = 1
    while bit < size:
        bits.append((axis, bit))
        bit *= 2
    return bits


def spread(keep, away):
    arrived = swap(away, "expert", 1)
    found = []
    for j in range(keep.shape[0]):
        for part in (keep[j], arrived[j]):
            found.append(swap(part, "expert", 2 * j) if j else part)
    return found


def after(values, *others):
    return lax.optimization_barrier((values, others))[0]


def levels():
    groups, owners = lax.axis_size("dp"), lax.axis_size("expert")
    dp, expert = lax.axis_index("dp"), lax.axis_index("expert")
    axes = ("dp", "expert")

    def sender(width, fold):
        def send(values, k):
            def target(i):
                d, e = fold(i // owners, i % owners, k)
                return d * owners + e

            return lax.ppermute(values, axes, [(i, target(i)) for i in range(groups * owners)])

        return send

    return [
        (2, dp % 2, sender(2, lambda d, e, k: (d ^ k, e))),
        (
            groups,
            dp // 2 * 2 + expert % 2,
            sender(groups, lambda d, e, k: (d ^ (k // 2 * 2), e ^ (k % 2))),
        ),
        (owners // 2, expert // 2, sender(owners // 2, lambda d, e, k: (d, e ^ (2 * k)))),
    ]


def sum_everywhere(arrays, fillers):
    steps = levels()
    fillers = iter(fillers)

    def fill(terms, ready):
        found = [run(ready) for run in next(fillers, ())]
        return after(terms, *found) if found else terms

    count, place, send = steps[0]
    terms = []
    for v in arrays:
        share = v.shape[0] // 2
        mine, away = (
            lax.dynamic_slice_in_dim(v, (place ^ k) * share, share, 0) for k in range(2)
        )
        terms.append((mine, send(away, 1)))
    terms = fill(terms, arrays)
    values = jnp.concatenate([a.astype(F32) + b.astype(F32) for a, b in terms]).astype(BF16)
    for count, place, send in steps[1:]:
        share = values.shape[0] // count
        blocks = [
            lax.dynamic_slice_in_dim(values, (place ^ k) * share, share, 0) for k in range(count)
        ]
        sent = fill([send(blocks[k], k) for k in range(1, count)], blocks)
        values = sum(t.astype(F32) for t in blocks[:1] + sent).astype(BF16)
    for count, place, send in reversed(steps[1:]):
        share = values.shape[0]
        sent = fill([send(values, k) for k in range(1, count)], values)
        found = jnp.zeros((count * share, values.shape[1]), BF16)
        for k, piece in enumerate([values] + sent):
            found = lax.dynamic_update_slice_in_dim(found, piece, (place ^ k) * share, 0)
        values = found
    _, place, send = steps[0]
    other = fill(send(values, 1), values)
    for rest in fillers:
        for run in rest:
            run(values)
    return values, other, place


def widen_kernel(place_ref, mine_ref, other_ref, out_ref):
    half = (2 * pl.program_id(1) + pl.program_id(0)) // 3

    @pl.when(place_ref[0] == half)
    def _():
        out_ref[...] = mine_ref[...].astype(F32)

    @pl.when(place_ref[0] != half)
    def _():
        out_ref[...] = other_ref[...].astype(F32)


def widen(mine, other, place, width):
    rows = width // 2
    block = pl.BlockSpec((rows, width), lambda r, j, _: ((2 * j + r) % 3, 0))
    return pl.pallas_call(
        widen_kernel,
        grid_spec=pltpu.PrefetchScalarGridSpec(
            num_scalar_prefetch=1,
            grid=(2, 3),
            in_specs=[block, block],
            out_specs=pl.BlockSpec((rows, width), lambda r, j, _: (r, j)),
        ),
        out_shape=jax.ShapeDtypeStruct((width, 3 * width), F32),
        compiler_params=params(),
        cost_estimate=cost(5),
        name="widen",
    )(place.astype(jnp.int32)[None], mine, other)


def sum_small(values):
    axes = ("dp", "expert")
    devices = lax.axis_size("dp") * lax.axis_size("expert")
    sent = jnp.broadcast_to(values[None], (devices,) + values.shape)
    return jnp.sum(lax.all_to_all(sent, axes, 0, 0, tiled=True), axis=0)


def on_device(
    hidden_in, doc_ids, valid_mask, expert_ids, bucket_table, norm1_gain, qkv_weight, position_bias,
    out_weight, norm2_gain, router_weight, up_weight, down_weight, out_grad,
):
    length, width = hidden_in.shape
    local = up_weight.shape[0]
    owners = lax.axis_size("expert")
    groups = lax.axis_size("dp")
    devices = owners * groups
    kinds = router_weight.shape[1]
    chunks = 2 if local % 4 == 0 else 1
    each = local // chunks
    half = owners // 2
    me = lax.axis_index("expert").astype(jnp.int32)
    group = lax.axis_index("dp").astype(jnp.int32)
    scalars = jnp.stack([me * local, me])
    group_scalars = jnp.stack([me * local, group, me])

    owner, inside = expert_ids // local, expert_ids % local
    far = owner ^ me
    chunk, within = inside // each, inside % each
    last = chunk == chunks - 1
    turned = far % 2 * half + far // 2
    send_ids = (chunk * owners + jnp.where(chunk == 0, turned, owner)) * each + within
    keep_ids = (chunk * owners + jnp.where(last, far, owner)) * each + within
    place_row, place_col, grad_rows = route(
        expert_ids, send_ids, keep_ids, out_grad, owners * local * CAP
    )
    to_owners = functools.partial(
        lax.all_to_all, axis_name="expert", split_axis=0, concat_axis=0, tiled=True
    )
    grads = to_owners(grad_rows.reshape(owners, local * CAP, width))
    size = owners * each * CAP
    probs, qkv, n1_t, ctx_t, residual, branch_stat, keep, away, *other = attention_forward(
        hidden_in, norm1_gain, qkv_weight, out_weight, norm2_gain, doc_ids, valid_mask,
        bucket_table, position_bias, place_row, (size // 2, size // 2) + (size,) * (chunks - 1),
    )
    shape = (half, each * CAP, width)
    rows = spread(keep.reshape(shape), away.reshape(shape))
    rows_first = rows[1]
    side = active_grads(after(grads, rows_first), down_weight)
    backs, seen, router_parts = [], [], []
    active = None
    for c in range(chunks):
        later = None
        if c + 1 < chunks:
            later = [to_owners(after(other[c], side, *rows).reshape(owners, each * CAP, width))]
        *back, active, router_part = run_experts(
            rows, side, up_weight, router_weight, scalars, c * each, active, c + 1 == chunks
        )
        if c + 1 < chunks:
            backs.append(to_owners(back[0]))
        seen += rows
        rows = later
        router_parts.append(router_part)
    keep, away = back
    last_backs = spread(keep, away)
    outs = expert_outputs(after(active, last_backs[1]), down_weight)
    backs = after(backs + last_backs, outs)
    router_grad = functools.reduce(jnp.add, router_parts)
    backs = [b.reshape(-1, width) for b in backs]

    gain2_grad, residual_grad, early, ctx_grad = residual_backward(
        place_col, residual, norm2_gain, out_grad, out_weight, ctx_t, router_grad, backs,
        -(-(4 * width + kinds) // devices) * devices - 3 * width,
    )
    heads = width // PAIR
    dq, dk, dv, wgrad, by_distance = attention_backward(qkv, ctx_grad, probs, n1_t, 0, heads)
    outs = to_owners(after(outs, *backs)).reshape(owners * local * CAP, width)
    rows_gathered = lax.all_gather(
        jnp.concatenate([r.reshape(-1, width) for r in after(seen, *back)]).reshape(
            chunks, owners, each * CAP, width
        ),
        "dp",
    )
    grads_gathered = lax.all_gather(after(grads, rows_first), "dp")
    expert_grads = [None]

    def expert_pair(first, ready):
        expert_grads[0] = expert_wgrads(
            rows_gathered, after(grads_gathered, ready), up_weight, down_weight, router_weight, group_scalars,
            first, first // each == 0, expert_grads[0],
        )
        return expert_grads[0]

    span = by_distance.shape[2]
    by_head = by_distance[:, :2, :].reshape(HEADS, span)
    hot = (bucket_table[:span, None] == jnp.arange(NBUCKET)[None, :]).astype(F32)
    bias_part = jnp.dot(by_head, hot, precision=HIGHEST).T
    results = {}

    def first_norm(ready):
        results["input"] = input_backward(
            hidden_in, norm1_gain, after(residual_grad, ready), qkv_weight, (dq, dk, dv)
        )
        return results["input"]

    def last_sum(ready):
        results["output"] = block_output(place_col, residual, valid_mask, after(outs, ready))
        return results["output"]

    def short_sums(ready):
        out_stats = results["output"][1]
        counts = jnp.stack(
            [
                jnp.sum(out_stats[0]),
                jnp.sum(branch_stat),
                jnp.sum(out_stats[1]),
                jnp.sum(valid_mask.astype(F32)),
            ]
        )
        short = jnp.concatenate(
            [results["input"][1][0], gain2_grad[0], bias_part.reshape(-1), counts]
        )
        results["total"] = short.shape[0]
        short = jnp.pad(short, (0, -short.shape[0] % 1024)).reshape(-1, 128)
        results["short"] = sum_small(short).reshape(-1)
        return [results["short"]]

    experts = [functools.partial(expert_pair, first) for first in range(0, local, 2)]
    fillers = [[first_norm], experts[:1], [last_sum] + experts[1:2], [short_sums] + experts[2:3]]
    fillers += [experts[3:]]
    mine, other, place = sum_everywhere([wgrad.reshape(3 * width, width), early], fillers)
    block_out, input_grad = results["output"][0], results["input"][0]
    small, total = results["short"], results["total"]
    gain1_sum, gain2_sum = small[:width], small[width : 2 * width]
    bias_sum = small[2 * width : 2 * width + HEADS * NBUCKET].reshape(NBUCKET, HEADS)
    stat_sums = small[total - 4 : total]
    rms_stats = jnp.sqrt(stat_sums[:3] / (jnp.maximum(stat_sums[3], 1.0) * width))
    early_mine, early_other = mine[3 * width // 2 :], other[3 * width // 2 :]
    early_sum = jnp.concatenate(
        [
            jnp.where(place == 0, early_mine, early_other),
            jnp.where(place == 0, early_other, early_mine),
        ]
    ).astype(F32)
    return (
        block_out,
        input_grad,
        gain1_sum,
        widen(mine, other, place, width),
        bias_sum,
        early_sum[:width],
        gain2_sum,
        early_sum[width : width + kinds].T,
        *expert_grads[0],
        rms_stats,
    )


def solution(mesh):
    spread = P(("dp", "expert"), None)
    placed = (spread,) * 4 + (P(),) * 7 + (P("expert", None, None),) * 2 + (spread,)
    return jax.shard_map(
        on_device,
        mesh=mesh,
        in_specs=placed,
        out_specs=(spread, spread)
        + (P(),) * 6
        + (P("expert", None, "dp"), P("expert", "dp", None), P()),
        check_vma=False,
    )
```

```python
import functools

import jax
import jax.numpy as jnp
from jax import lax
from jax.experimental import pallas as pl
from jax.experimental.pallas import tpu as pltpu
from jax.sharding import PartitionSpec as P

HEADS = 12
HEAD_DIM = 64
NBUCKET = 32
CAP = 24
BLOCK = 128
WINDOW = 3
PAIR = 2 * HEAD_DIM
EPSILON = 1e-06
NEGATIVE = -1e30
HIGHEST = lax.Precision.HIGHEST
BF16 = jnp.bfloat16
F32 = jnp.float32
SUBSTEPS = 6
VMEM_LIMIT = 58 * 1024 * 1024


NN = (((1,), (0,)), ((), ()))
NT = (((1,), (1,)), ((), ()))
TN = (((0,), (0,)), ((), ()))


def dot(left, right, dims=NN, precision=None):
    return lax.dot_general(left, right, dims, precision=precision, preferred_element_type=F32)


def iota(shape, dim):
    return lax.broadcasted_iota(jnp.int32, shape, dim)


def whole(shape):
    return pl.BlockSpec(shape, lambda *_: (0,) * len(shape))


def params(**more):
    return pltpu.CompilerParams(vmem_limit_bytes=VMEM_LIMIT, **more)


def cost(microseconds):
    return pl.CostEstimate(
        flops=int(microseconds * 1.1e9), bytes_accessed=1000, transcendentals=0
    )


def windows(length):
    found = []
    row = 0
    for number in range(length // BLOCK):
        first = max(number - WINDOW + 1, 0)
        keys = (number - first + 1) * BLOCK
        found.append((number * BLOCK, first * BLOCK, keys, row))
        row += keys
    return found, row


def rms(values):
    return lax.rsqrt(jnp.mean(values * values, axis=-1, keepdims=True) + EPSILON)


def hot_columns(row0, row1, count, offset):
    slots = iota((count, row0.shape[1]), 0) + offset
    return jnp.where((slots == row0) | (slots == row1), 1.0, 0.0).astype(BF16)


def hot_rows(col0, col1, count, offset):
    slots = iota((col0.shape[0], count), 1) + offset
    return jnp.where((slots == col0) | (slots == col1), 1.0, 0.0).astype(BF16)


def route_kernel(ids_ref, send_ref, keep_ref, grad_ref, row_ref, col_ref, rows_ref):
    length = grad_ref.shape[0]
    experts = rows_ref.shape[0] // CAP
    before = iota((length, length), 0) < iota((length, length), 1)
    upper = jnp.where(before, 1.0, 0.0).astype(BF16)
    after = iota((length, length), 0) > iota((length, length), 1)
    lower = jnp.where(after, 1.0, 0.0).astype(BF16)
    number = iota((experts, length), 0)
    hot = [number == ids_ref[c : c + 1, :] for c in range(2)]
    both = jnp.where(hot[0] | hot[1], 1.0, 0.0).astype(BF16)
    rank = dot(both, upper)
    rows = []
    for c in range(2):
        mine = jnp.sum(jnp.where(hot[c], rank, 0.0), axis=0, keepdims=True).astype(jnp.int32)
        rows.append(ids_ref[c : c + 1, :] * CAP + mine)
        row_ref[c : c + 1, :] = send_ref[c : c + 1, :] * CAP + mine
    number = iota((length, experts), 1)
    hot = [number == keep_ref[:, c : c + 1] for c in range(2)]
    both = jnp.where(hot[0] | hot[1], 1.0, 0.0).astype(BF16)
    rank = dot(lower, both)
    for c in range(2):
        mine = jnp.sum(jnp.where(hot[c], rank, 0.0), axis=1, keepdims=True).astype(jnp.int32)
        for kind in range(2):
            at = slice(2 * kind + c, 2 * kind + c + 1)
            col_ref[:, at] = keep_ref[:, at] * CAP + mine
    chosen = hot_columns(rows[0], rows[1], rows_ref.shape[0], 0)
    rows_ref[...] = dot(chosen, grad_ref[...]).astype(BF16)


def route(ids, send_ids, keep_ids, out_grad, slots):
    length, width = out_grad.shape
    return pl.pallas_call(
        route_kernel,
        out_shape=(
            jax.ShapeDtypeStruct((2, length), jnp.int32),
            jax.ShapeDtypeStruct((length, 4), jnp.int32),
            jax.ShapeDtypeStruct((slots, width), BF16),
        ),
        compiler_params=params(),
        cost_estimate=cost(5),
        name="route",
    )(ids.T, send_ids.T, jnp.concatenate([keep_ids, ids], axis=1), out_grad)


def forward_kernel(
    x_ref, gain1_ref, qkvw_ref, outw_ref, gain2_ref, docr_ref, docc_ref, validc_ref, bucket_ref,
    pbias_ref, row_ref,
    probs_ref, qkv_ref, n1t_ref, ctx_ref, residual_ref, stat_ref, *rest,
):
    rows_refs, (mask_s, bias_s, toeplitz_s) = rest[:-3], rest[-3:]
    pair = pl.program_id(0)
    length, width = x_ref.shape
    spans, _ = windows(length)

    @pl.when(pair == 0)
    def _():
        x = x_ref[...].astype(F32)
        n1 = (x * rms(x) * gain1_ref[...]).astype(BF16)
        n1t_ref[...] = n1.T
        for j in range(3):
            part = slice(j * width, (j + 1) * width)
            qkv_ref[:, part] = dot(n1, qkvw_ref[:, part]).astype(BF16)
        for q0, k0, keys, row in spans:
            shape = (keys, BLOCK)
            distance = (iota(shape, 1) + q0) - (iota(shape, 0) + k0)
            allowed = (
                (distance >= 0)
                & (docc_ref[k0 : k0 + keys, :] == docr_ref[:, q0 : q0 + BLOCK])
                & ((validc_ref[k0 : k0 + keys, :] == 1) | (distance == 0))
            )
            mask_s[row : row + keys, :] = jnp.where(allowed, 0.0, NEGATIVE)
        span = bias_s.shape[1]
        hot = jnp.where(iota((NBUCKET, span), 0) == bucket_ref[...], 1.0, 0.0)
        bias_s[...] = dot(pbias_ref[...], hot, precision=HIGHEST)

    for side in range(2):
        head_bias = bias_s[pl.ds(2 * pair + side, 1), :]
        for m in range(WINDOW):
            ahead = head_bias[:, m * BLOCK : (m + 1) * BLOCK]
            back = max(m - 1, 0)
            behind = head_bias[:, back * BLOCK : (back + 1) * BLOCK]
            lanes = jnp.broadcast_to(
                jnp.concatenate([ahead, behind], axis=1), (BLOCK, 2 * BLOCK)
            )
            rolled = pltpu.roll(lanes, 0, 1, stride=1, stride_axis=0)
            place = (WINDOW - 1 - m) * BLOCK
            toeplitz_s[place : place + BLOCK, side * BLOCK : (side + 1) * BLOCK] = rolled[
                :, :BLOCK
            ]

    at = pl.multiple_of(pair * PAIR, PAIR)
    first_head = iota((BLOCK, PAIR), 1) < HEAD_DIM
    top = iota((PAIR, BLOCK), 0) < HEAD_DIM
    for q0, k0, keys, row in spans:
        q = qkv_ref[q0 : q0 + BLOCK, pl.ds(at, PAIR)].astype(F32) * HEAD_DIM ** (-0.5)
        stacked = jnp.concatenate(
            [jnp.where(first_head, q, 0.0), jnp.where(first_head, 0.0, q)], axis=0
        ).astype(BF16)
        k = qkv_ref[k0 : k0 + keys, pl.ds(pl.multiple_of(width + at, PAIR), PAIR)]
        v = qkv_ref[k0 : k0 + keys, pl.ds(pl.multiple_of(2 * width + at, PAIR), PAIR)]
        scores = dot(k, stacked, NT)
        masked = mask_s[row : row + keys, :]
        for side in range(2):
            lanes = slice(side * BLOCK, (side + 1) * BLOCK)
            s = scores[:, lanes] + toeplitz_s[WINDOW * BLOCK - keys :, lanes] + masked
            peak = jnp.max(s, axis=0, keepdims=True)
            e = jnp.exp(s - peak)
            total = jnp.sum(e, axis=0, keepdims=True)
            probs_ref[0, row : row + keys, lanes] = (e * (1.0 / total)).astype(BF16)
        both = dot(v, probs_ref[0, row : row + keys, :], TN)
        ctx = jnp.where(top, both[:, :BLOCK], both[:, BLOCK:])
        ctx_ref[pl.ds(at, PAIR), q0 : q0 + BLOCK] = ctx.astype(BF16)

    @pl.when(pair == pl.num_programs(0) - 1)
    def _():
        branch = dot(ctx_ref[...], outw_ref[...], TN)
        valid = validc_ref[...].astype(F32)
        stat_ref[...] = jnp.sum(valid * branch * branch, axis=0, keepdims=True)
        residual = x_ref[...].astype(F32) + branch
        residual_ref[...] = residual
        n2 = (residual * rms(residual) * gain2_ref[...]).astype(BF16)
        offset = 0
        for out in rows_refs:
            chosen = hot_columns(row_ref[0:1, :], row_ref[1:2, :], out.shape[0], offset)
            out[...] = dot(chosen, n2).astype(BF16)
            offset += out.shape[0]


def attention_forward(
    x, gain1, qkvw, outw, gain2, docs, valid, bucket_table, position_bias, place_row, sizes
):
    length, width = x.shape
    _, stored = windows(length)
    pairs = width // PAIR
    span = WINDOW * BLOCK
    padded_heads = -(-HEADS // 8) * 8
    bias_t = jnp.zeros((padded_heads, NBUCKET), F32).at[:HEADS].set(position_bias.T)
    arguments = (
        x, gain1[None], qkvw, outw, gain2[None], docs, docs.T, valid.T,
        bucket_table[None, :span], bias_t, place_row,
    )
    out_shape = (
        jax.ShapeDtypeStruct((pairs, stored, 2 * BLOCK), BF16),
        jax.ShapeDtypeStruct((length, 3 * width), BF16),
        jax.ShapeDtypeStruct((width, length), BF16),
        jax.ShapeDtypeStruct((width, length), BF16),
        jax.ShapeDtypeStruct((length, width), F32),
        jax.ShapeDtypeStruct((1, width), F32),
    ) + tuple(jax.ShapeDtypeStruct((n, width), BF16) for n in sizes)
    return pl.pallas_call(
        forward_kernel,
        grid=(pairs,),
        in_specs=[whole(a.shape) for a in arguments],
        out_specs=[pl.BlockSpec((1, stored, 2 * BLOCK), lambda p: (p, 0, 0))]
        + [whole(s.shape) for s in out_shape[1:]],
        out_shape=out_shape,
        scratch_shapes=[
            pltpu.VMEM((stored, BLOCK), F32),
            pltpu.VMEM((padded_heads, span), F32),
            pltpu.VMEM((span, 2 * BLOCK), F32),
        ],
        compiler_params=params(),
        cost_estimate=cost(22),
        name="attention_forward",
    )(*arguments)


def expert_gate(rows, router, expert):
    logits = dot(rows, router)
    shifted = jnp.exp(logits - jnp.max(logits, axis=-1, keepdims=True))
    probs = shifted / jnp.sum(shifted, axis=-1, keepdims=True)
    mine = iota(probs.shape, 1) == expert
    return probs, mine, jnp.sum(jnp.where(mine, probs, 0.0), axis=-1, keepdims=True)


GELU_SCALE = 0.7978845608028654
GELU_CUBE = 0.044715


def gelu_parts(v):
    square = v * v
    t = jnp.tanh(v * (GELU_SCALE + (GELU_SCALE * GELU_CUBE) * square))
    half = 0.5 * v
    value = half + half * t
    slope = 0.5 + 0.5 * t + half * (1.0 - t * t) * (
        GELU_SCALE + (3.0 * GELU_SCALE * GELU_CUBE) * square
    )
    return value, slope


def active_grad_kernel(grads_ref, down_ref, out_ref, g_s, grads_s, *, first):
    e, f = pl.program_id(0), pl.program_id(1)

    @pl.when((e == 0) & (f == 0))
    def _():
        grads_s[...] = grads_ref[...].astype(F32)

    @pl.when(f == 0)
    def _():
        here = pl.ds(pl.multiple_of((first + e) * CAP, CAP), CAP)
        g_s[...] = grads_s[:, here, :].reshape(g_s.shape).astype(BF16)

    out_ref[0] = dot(g_s[...], down_ref[0], NT).astype(BF16)


def active_grads(grads, down_weight, first, experts, blocks=1):
    owners, _, width = grads.shape
    inner = down_weight.shape[1]
    step, count = inner // blocks, owners * CAP
    return pl.pallas_call(
        functools.partial(active_grad_kernel, first=first),
        grid=(experts, blocks),
        in_specs=[
            whole(grads.shape),
            pl.BlockSpec((1, step, width), lambda e, f: (first + e, f, 0)),
        ],
        out_specs=pl.BlockSpec((1, count, step), lambda e, f: (e, 0, f)),
        out_shape=jax.ShapeDtypeStruct((experts, count, inner), BF16),
        scratch_shapes=[pltpu.VMEM((count, width), BF16), pltpu.VMEM(grads.shape, F32)],
        compiler_params=params(),
        cost_estimate=cost(22),
        name="active_grads",
    )(grads, down_weight)


def expert_kernel(scalar_ref, *refs, parts, aliased, last):
    rows_refs, refs = refs[:parts], refs[parts:]
    side_ref, up_ref, router_ref = refs[:3]
    refs = refs[3 + aliased :]
    back_refs, refs = refs[: 1 + last], refs[1 + last :]
    all_ref, active_ref, router_grad_ref = refs[:3]
    rows_s, back_s, x_s, probs_s, gate_s, sum_s, dx_s, grad_s = refs[3:]
    e, f = pl.program_id(0), pl.program_id(1)
    experts, blocks = pl.num_programs(0), pl.num_programs(1)
    me = scalar_ref[1]
    expert = scalar_ref[0] + e
    count, width = x_s.shape
    owners = rows_s.shape[0]
    here = pl.ds(pl.multiple_of(e * CAP, CAP), CAP)

    @pl.when((e == 0) & (f == 0))
    def _():
        if parts == 1:
            all_ref[0] = rows_refs[0][...]
            rows_s[...] = rows_refs[0][...].astype(F32)
        else:
            for k in range(parts):
                all_ref[0, me ^ k] = rows_refs[k][...]
                rows_s[me ^ k] = rows_refs[k][...].astype(F32)
        router_grad_ref[...] = jnp.zeros_like(router_grad_ref)

    @pl.when(f == 0)
    def _():
        x = rows_s[:, here, :].reshape(count, width).astype(BF16)
        x_s[...] = x
        probs, _, gate = expert_gate(x, router_ref[...], expert)
        probs_s[...] = probs
        gate_s[...] = jnp.broadcast_to(gate, gate_s.shape)
        sum_s[...] = jnp.zeros_like(sum_s)
        dx_s[...] = jnp.zeros_like(dx_s)

    gate = gate_s[:, :1]
    x = x_s[...]
    step = up_ref.shape[2] // SUBSTEPS
    total = None
    inner = dot(x, up_ref[0, :, :step])
    for s in range(SUBSTEPS):
        here_f = slice(s * step, (s + 1) * step)
        later = dot(x, up_ref[0, :, (s + 1) * step : (s + 2) * step]) if s + 1 < SUBSTEPS else None
        value, slope = gelu_parts(inner)
        side = side_ref[0, :, here_f].astype(F32) * gate
        part = jnp.sum(value * side, axis=-1, keepdims=True)
        total = part if total is None else total + part
        active_ref[0, :, here_f] = (gate * value).astype(BF16)
        grad_s[:, here_f] = (side * slope).astype(BF16)
        inner = later
    sum_s[...] += total
    dx_s[...] += dot(grad_s[...], up_ref[0], NT)

    @pl.when(f == blocks - 1)
    def _():
        probs = probs_s[...]
        mine = iota(probs.shape, 1) == expert
        logit_grad = (sum_s[:, :1] * (jnp.where(mine, 1.0, 0.0) - probs)).astype(BF16)
        router_grad_ref[...] += dot(logit_grad, x_s[...], TN)
        dx = dx_s[...] + dot(logit_grad, router_ref[...], NT)
        back_s[:, here, :] = dx.reshape(owners, CAP, width)

    @pl.when((e == experts - 1) & (f == blocks - 1))
    def _():
        if last:
            for source in range(owners):
                back_refs[source % 2][source // 2] = back_s[me ^ source].astype(BF16)
        else:
            back_refs[0][...] = back_s[...].astype(BF16)


def run_experts(
    rows, side, up_weight, router, scalars, first, old, last
):
    parts = len(rows)
    slots, width = rows[0].shape[-2:]
    owners = parts if parts > 1 else rows[0].shape[0]
    experts = slots // CAP
    local, _, inner = up_weight.shape
    count, kinds = owners * CAP, router.shape[1]
    blocks = 1 if count <= 256 else 3
    step = inner // blocks
    backs = [jax.ShapeDtypeStruct((owners, slots, width), BF16)]
    if last:
        backs = [jax.ShapeDtypeStruct((owners // 2, slots, width), BF16)] * 2
    in_specs = [whole(r.shape) for r in rows] + [
        pl.BlockSpec((1, count, step), lambda e, f, _: (e, 0, f)),
        pl.BlockSpec((1, width, step), lambda e, f, _: (first + e, 0, f)),
        whole(router.shape),
    ]
    arguments = (*rows, side, up_weight, router)
    aliases = {}
    if old is not None:
        aliases = {1 + len(arguments) + k: len(backs) + k for k in range(2)}
        in_specs += [pl.BlockSpec(memory_space=pl.ANY)] * 2
        arguments += tuple(old)
    return pl.pallas_call(
        functools.partial(expert_kernel, parts=parts, aliased=len(aliases), last=last),
        grid_spec=pltpu.PrefetchScalarGridSpec(
            num_scalar_prefetch=1,
            grid=(experts, blocks),
            in_specs=in_specs,
            out_specs=[whole(back.shape) for back in backs]
            + [
                pl.BlockSpec((1, owners, slots, width), lambda e, f, _: (first // experts, 0, 0, 0)),
                pl.BlockSpec((1, count, step), lambda e, f, _: (first + e, 0, f)),
                whole((kinds, width)),
            ],
            scratch_shapes=[
                pltpu.VMEM((owners, slots, width), F32),
                pltpu.VMEM((owners, slots, width), F32),
                pltpu.VMEM((count, width), BF16),
                pltpu.VMEM((count, kinds), F32),
                pltpu.VMEM((count, BLOCK), F32),
                pltpu.VMEM((count, BLOCK), F32),
                pltpu.VMEM((count, width), F32),
                pltpu.VMEM((count, step), BF16),
            ],
        ),
        out_shape=(
            *backs,
            jax.ShapeDtypeStruct((local // experts, owners, slots, width), BF16),
            jax.ShapeDtypeStruct((local, count, inner), BF16),
            jax.ShapeDtypeStruct((kinds, width), F32),
        ),
        input_output_aliases=aliases,
        compiler_params=params(),
        cost_estimate=cost(22),
        name="experts",
    )(scalars + jnp.array([first, 0], jnp.int32), *arguments)


def expert_out_kernel(active_ref, down_ref, out_ref, sum_s, all_s):
    e, f = pl.program_id(0), pl.program_id(1)
    experts, blocks = pl.num_programs(0), pl.num_programs(1)
    part = dot(active_ref[0], down_ref[0])

    @pl.when(f == 0)
    def _():
        sum_s[...] = part

    @pl.when(f > 0)
    def _():
        sum_s[...] += part

    @pl.when(f == blocks - 1)
    def _():
        here = pl.ds(pl.multiple_of(e * CAP, CAP), CAP)
        all_s[:, here, :] = sum_s[...].reshape(all_s.shape[0], CAP, all_s.shape[2])

    @pl.when((e == experts - 1) & (f == blocks - 1))
    def _():
        out_ref[...] = all_s[...].astype(BF16)


def expert_outputs(active, down_weight, blocks=1):
    experts, count, inner = active.shape
    width = down_weight.shape[2]
    step, owners = inner // blocks, count // CAP
    shape = (owners, experts * CAP, width)
    return pl.pallas_call(
        expert_out_kernel,
        grid=(experts, blocks),
        in_specs=[
            pl.BlockSpec((1, count, step), lambda e, f: (e, 0, f)),
            pl.BlockSpec((1, step, width), lambda e, f: (e, f, 0)),
        ],
        out_specs=whole(shape),
        out_shape=jax.ShapeDtypeStruct(shape, BF16),
        scratch_shapes=[pltpu.VMEM((count, width), F32), pltpu.VMEM(shape, F32)],
        compiler_params=params(),
        cost_estimate=cost(0.01),
        name="expert_outputs",
    )(active, down_weight)


def expert_wgrad_kernel(
    scalar_ref, rows_ref, grads_ref, up_ref, down_ref, router_ref, *rest, first
):
    up_out, down_out, x_s, g_s = rest[-4:]
    expert, tile = first + pl.program_id(0), pl.program_id(1)
    count, width = x_s.shape
    for side in range(2):

        @pl.when(expert % 2 == side)
        def _():
            part = slice(side * CAP, (side + 1) * CAP)
            x = rows_ref[...].astype(F32)[:, 0, :, part, :].reshape(count, width).astype(BF16)
            x_s[...] = x
            _, _, gate = expert_gate(x, router_ref[...], scalar_ref[0] + expert)
            g = grads_ref[...].astype(F32)[:, :, part, :].reshape(count, width)
            g_s[...] = (gate * g).astype(BF16)

    x, g = x_s[...], g_s[...]
    value, slope = gelu_parts(dot(x, up_ref[0]))
    inner_grad = (dot(g, down_ref[0], NT) * slope).astype(BF16)

    @pl.when(tile == 0)
    def _():
        down_out[0] = dot(value.astype(BF16), g, TN)
        up_out[0] = dot(x, inner_grad, TN)

    @pl.when(tile > 0)
    def _():
        down_out[0] += dot(value.astype(BF16), g, TN)
        up_out[0] += dot(x, inner_grad, TN)


def expert_wgrads(rows, grads, up_weight, down_weight, router, scalars, first, experts, old):
    groups, chunks, owners, _, width = rows.shape
    local, _, inner = up_weight.shape
    each = local // chunks
    share = inner // groups
    taken = max(min(groups, 32 // owners), 1)
    count = taken * owners * CAP

    def rows_at(e, t, _):
        return (t, (first + e) // each, 0, (first + e) % each // 2, 0)

    in_specs = [
        pl.BlockSpec((taken, 1, owners, 2 * CAP, width), rows_at),
        pl.BlockSpec((taken, owners, 2 * CAP, width), lambda e, t, _: (t, 0, (first + e) // 2, 0)),
        pl.BlockSpec((1, width, share), lambda e, t, s: (first + e, 0, s[1])),
        pl.BlockSpec((1, share, width), lambda e, t, s: (first + e, s[1], 0)),
        whole(router.shape),
    ]
    arguments = (rows, grads, up_weight, down_weight, router)
    aliases = {}
    if old is not None:
        aliases = {6: 0, 7: 1}
        in_specs += [pl.BlockSpec(memory_space=pl.ANY)] * 2
        arguments += tuple(old)
    return pl.pallas_call(
        functools.partial(expert_wgrad_kernel, first=first),
        grid_spec=pltpu.PrefetchScalarGridSpec(
            num_scalar_prefetch=1,
            grid=(experts, groups // taken),
            in_specs=in_specs,
            out_specs=[
                pl.BlockSpec((1, width, share), lambda j, t, _: (first + j, 0, 0)),
                pl.BlockSpec((1, share, width), lambda j, t, _: (first + j, 0, 0)),
            ],
            scratch_shapes=[
                pltpu.VMEM((count, width), BF16),
                pltpu.VMEM((count, width), BF16),
            ],
        ),
        out_shape=(
            jax.ShapeDtypeStruct((local, width, share), F32),
            jax.ShapeDtypeStruct((local, share, width), F32),
        ),
        input_output_aliases=aliases,
        compiler_params=params(),
        cost_estimate=cost(0.01),
        name="expert_wgrads",
    )(scalars, *arguments)


def residual_kernel(
    half_ref, col_ref, residual_ref, gain_ref, grad_ref, outw_ref, ctx_ref, router_ref, *rest
):
    back_refs, rest = rest[:-8], rest[-8:]
    gain_grad_ref, residual_grad_ref, mine_ref, away_ref, ctx_grad_ref, early_s, sem0, sem1 = rest
    whole_backs = back_refs[0][...]
    if len(back_refs) > 1:
        whole_backs = jnp.concatenate([back[...] for back in back_refs], axis=0)
    chosen = hot_rows(col_ref[:, 0:1], col_ref[:, 1:2], whole_backs.shape[0], 0)
    n2_grad = dot(chosen, whole_backs)
    residual = residual_ref[...]
    factor = rms(residual)
    unit = residual * factor
    gain_grad_ref[...] = jnp.sum(n2_grad * unit, axis=0, keepdims=True)
    scaled = n2_grad * gain_ref[...]
    centre = jnp.mean(scaled * unit, axis=-1, keepdims=True)
    residual_grad = grad_ref[...].astype(F32) + factor * (scaled - unit * centre)
    residual_grad_ref[...] = residual_grad
    branch_grad = residual_grad.astype(BF16)
    width, kinds = ctx_ref.shape[0], router_ref.shape[0]
    rows = early_s.shape[1]
    used = (width + kinds) // 2
    copies = []
    for k, (out, sem) in enumerate(((mine_ref, sem0), (away_ref, sem1))):
        part = half_ref[0] ^ k
        ctx = ctx_ref[pl.ds(pl.multiple_of(part * (width // 2), width // 2), width // 2), :]
        early_s[k, : width // 2, :] = dot(ctx, branch_grad).astype(BF16)
        router = router_ref[pl.ds(pl.multiple_of(part * (kinds // 2), kinds // 2), kinds // 2), :]
        early_s[k, width // 2 : used, :] = router.astype(BF16)
        if used < rows:
            early_s[k, used:, :] = jnp.zeros((rows - used, width), BF16)
        copies.append(
            pltpu.make_async_copy(early_s.at[k], out.at[pl.ds(3 * width // 2, rows)], sem)
        )
        copies[k].start()
    ctx_grad_ref[...] = dot(branch_grad, outw_ref[...], NT).astype(BF16)
    for copy in copies:
        copy.wait()


def residual_backward(
    half, place_col, residual, gain2, out_grad, outw, ctx_t, router_grad, backs, rows
):
    length, width = residual.shape
    early = rows - 3 * width // 2
    in_vmem = pl.BlockSpec(memory_space=pltpu.VMEM)
    anywhere = pl.BlockSpec(memory_space=pl.ANY)
    buffer = jax.ShapeDtypeStruct((rows, width), BF16)
    return pl.pallas_call(
        residual_kernel,
        in_specs=[pl.BlockSpec(memory_space=pltpu.SMEM)] + [in_vmem] * (7 + len(backs)),
        out_specs=[in_vmem, in_vmem, anywhere, anywhere, in_vmem],
        out_shape=(
            jax.ShapeDtypeStruct((1, width), F32),
            jax.ShapeDtypeStruct((length, width), F32),
            buffer,
            buffer,
            jax.ShapeDtypeStruct((length, width), BF16),
        ),
        scratch_shapes=[
            pltpu.VMEM((2, early, width), BF16),
            pltpu.SemaphoreType.DMA,
            pltpu.SemaphoreType.DMA,
        ],
        compiler_params=params(),
        cost_estimate=cost(0.01),
        name="residual_backward",
    )(half, place_col, residual, gain2[None], out_grad, outw, ctx_t, router_grad, *backs)


def attention_backward_kernel(
    half_ref, q_ref, k_ref, v_ref, dctx_ref, probs_ref, n1t_ref, _, __,
    dq_ref, dk_ref, dv_ref, mine_ref, away_ref, bias_ref,
    dqt_s, dk_s, dv_s, diagonal_s,
):
    length = q_ref.shape[0]
    spans, _ = windows(length)
    first_head = iota((BLOCK, PAIR), 1) < HEAD_DIM
    top = iota((PAIR, BLOCK), 0) < HEAD_DIM
    scale = HEAD_DIM ** (-0.5)
    dk_s[...] = jnp.zeros_like(dk_s)
    dv_s[...] = jnp.zeros_like(dv_s)
    diagonal_s[...] = jnp.zeros_like(diagonal_s)

    def stack(values):
        values = values.astype(F32)
        return jnp.concatenate(
            [jnp.where(first_head, values, 0.0), jnp.where(first_head, 0.0, values)], axis=0
        ).astype(BF16)

    for q0, k0, keys, row in spans:
        q = stack(q_ref[q0 : q0 + BLOCK, :])
        dctx = stack(dctx_ref[q0 : q0 + BLOCK, :])
        span = slice(k0, k0 + keys)
        probs = probs_ref[0, row : row + keys, :]
        prob_side = dot(v_ref[span, :], dctx, NT)
        halves = []
        for side in range(2):
            lanes = slice(side * BLOCK, (side + 1) * BLOCK)
            p = probs[:, lanes].astype(F32)
            d = prob_side[:, lanes]
            centre = jnp.sum(p * d, axis=0, keepdims=True)
            s = p * (d - centre)
            diagonal_s[WINDOW * BLOCK - keys :, lanes] += s
            halves.append(s.astype(BF16))
        score_grad = jnp.concatenate(halves, axis=1)
        dk_s[span, :] += dot(score_grad, q)
        dv_s[span, :] += dot(probs, dctx)
        both = dot(k_ref[span, :], score_grad, TN)
        dqt_s[:, q0 : q0 + BLOCK] = jnp.where(top, both[:, :BLOCK], both[:, BLOCK:])
    dq = (dqt_s[...].T * scale).astype(BF16)
    dk = (dk_s[...] * scale).astype(BF16)
    dv = dv_s[...].astype(BF16)
    dq_ref[...] = dq
    dk_ref[...] = dk
    dv_ref[...] = dv
    width = n1t_ref.shape[0]
    for k, out in enumerate((mine_ref, away_ref)):
        part = pl.multiple_of((half_ref[0] ^ k) * (width // 2), width // 2)
        n1t = n1t_ref[pl.ds(part, width // 2), :]
        for j, rows in enumerate((dq, dk, dv)):
            there = slice(j * (width // 2), (j + 1) * (width // 2))
            out[there, :] = dot(n1t, rows).astype(BF16)
    bias_ref[...] = jnp.zeros_like(bias_ref)
    for side in range(2):
        lanes = slice(side * BLOCK, (side + 1) * BLOCK)
        pieces = []
        for m in range(WINDOW):
            place = (WINDOW - 1 - m) * BLOCK
            block = diagonal_s[place : place + BLOCK, lanes]
            skewed = jnp.zeros((8, 2 * BLOCK), F32)
            for k in range(0, BLOCK, 8):
                eight = block[k : k + 8, :]
                wide = jnp.concatenate([eight, jnp.zeros_like(eight)], axis=1)
                skewed += wide if k == 0 else pltpu.roll(wide, 2 * BLOCK - k, 1)
            for bit in (1, 2, 4):
                moved = pltpu.roll(skewed, 2 * BLOCK - bit, 1)
                skewed = jnp.where(iota(skewed.shape, 0) & bit != 0, moved, skewed)
            pieces.append(jnp.sum(skewed, axis=0, keepdims=True))
        for m in range(WINDOW):
            total = pieces[m][:, :BLOCK]
            if m + 1 < WINDOW:
                total = total + pieces[m + 1][:, BLOCK:]
            bias_ref[0, side : side + 1, m * BLOCK : (m + 1) * BLOCK] = total


def attention_backward(half, qkv, ctx_grad, probs, n1_t, mine, away):
    length, width = ctx_grad.shape
    stored = probs.shape[1]
    pairs = width // PAIR
    span = WINDOW * BLOCK
    column = pl.BlockSpec((length, PAIR), lambda p, _: (0, p))
    summed = pl.BlockSpec((3 * width // 2, PAIR), lambda p, _: (0, p))
    anywhere = pl.BlockSpec(memory_space=pl.ANY)
    rows = jax.ShapeDtypeStruct((length, width), BF16)
    return pl.pallas_call(
        attention_backward_kernel,
        grid_spec=pltpu.PrefetchScalarGridSpec(
            num_scalar_prefetch=1,
            grid=(pairs,),
            in_specs=[
                column,
                pl.BlockSpec((length, PAIR), lambda p, _: (0, pairs + p)),
                pl.BlockSpec((length, PAIR), lambda p, _: (0, 2 * pairs + p)),
                column,
                pl.BlockSpec((1, stored, 2 * BLOCK), lambda p, _: (p, 0, 0)),
                whole(n1_t.shape),
                anywhere,
                anywhere,
            ],
            out_specs=[
                column,
                column,
                column,
                summed,
                summed,
                pl.BlockSpec((1, 8, span), lambda p, _: (p, 0, 0)),
            ],
            scratch_shapes=[
                pltpu.VMEM((PAIR, length), F32),
                pltpu.VMEM((length, PAIR), F32),
                pltpu.VMEM((length, PAIR), F32),
                pltpu.VMEM((span, 2 * BLOCK), F32),
            ],
        ),
        out_shape=(
            rows,
            rows,
            rows,
            jax.ShapeDtypeStruct(mine.shape, BF16),
            jax.ShapeDtypeStruct(away.shape, BF16),
            jax.ShapeDtypeStruct((pairs, 8, span), F32),
        ),
        input_output_aliases={7: 3, 8: 4},
        compiler_params=params(),
        cost_estimate=cost(96),
        name="attention_backward",
    )(half, qkv, qkv, qkv, ctx_grad, probs, n1_t, mine, away)


def input_kernel(x_ref, gain_ref, residual_grad_ref, qkvw_ref, *rest):
    parts, (grad_ref, gain_grad_ref) = rest[:-2], rest[-2:]
    x = x_ref[...].astype(F32)
    factor = rms(x)
    unit = x * factor
    n1_grad = None
    at = 0
    for part in parts:
        columns = part.shape[1]
        term = dot(part[...], qkvw_ref[:, at : at + columns], NT)
        n1_grad = term if n1_grad is None else n1_grad + term
        at += columns
    gain_grad_ref[...] = jnp.sum(n1_grad * unit, axis=0, keepdims=True)
    scaled = n1_grad * gain_ref[...]
    centre = jnp.mean(scaled * unit, axis=-1, keepdims=True)
    grad_ref[...] = (residual_grad_ref[...] + factor * (scaled - unit * centre)).astype(BF16)


def input_backward(x, gain1, residual_grad, qkvw, parts):
    length, width = x.shape
    return pl.pallas_call(
        input_kernel,
        out_shape=(
            jax.ShapeDtypeStruct((length, width), BF16),
            jax.ShapeDtypeStruct((1, width), F32),
        ),
        compiler_params=params(),
        cost_estimate=cost(0.01),
        name="input_backward",
    )(x, gain1[None], residual_grad, qkvw, *parts)


SHORT_ROWS = 16
STAT_ROW = 12
BIAS_ROW = 13


def output_kernel(
    col_ref, residual_ref, validc_ref, rows_ref, stat_ref, gain1_ref, gain2_ref, by_ref, bucket_ref,
    block_ref, short_ref, distance_s,
):
    chosen = hot_rows(col_ref[:, 2:3], col_ref[:, 3:4], rows_ref.shape[0], 0)
    mixture = dot(chosen, rows_ref[...])
    output = residual_ref[...] + mixture
    block_ref[...] = output.astype(BF16)
    valid = validc_ref[...].astype(F32)
    short_ref[...] = jnp.zeros_like(short_ref)
    for k in range(gain1_ref.shape[1] // BLOCK):
        lanes = slice(k * BLOCK, (k + 1) * BLOCK)
        short_ref[k : k + 1, :] = gain1_ref[:, lanes]
        short_ref[6 + k : 7 + k, :] = gain2_ref[:, lanes]
    lane = iota((1, BLOCK), 1)
    stats = jnp.where(lane == 0, jnp.sum(valid * output * output), 0.0)
    stats = jnp.where(lane == 1, jnp.sum(stat_ref[...]), stats)
    stats = jnp.where(lane == 2, jnp.sum(valid * mixture * mixture), stats)
    short_ref[STAT_ROW : STAT_ROW + 1, :] = jnp.where(lane == 3, jnp.sum(valid), stats)
    distance_s[...] = jnp.zeros_like(distance_s)
    for head in range(HEADS):
        distance_s[head : head + 1, :] = by_ref[head // 2, head % 2 : head % 2 + 1, :]
    buckets = iota((BLOCK, distance_s.shape[1]), 0) & (NBUCKET - 1)
    hot = jnp.where(buckets == bucket_ref[...], 1.0, 0.0)
    sums = dot(distance_s[...], hot, NT, HIGHEST)
    packed = BLOCK // NBUCKET
    own = iota(sums.shape, 1) // NBUCKET == iota(sums.shape, 0) % packed
    sums = jnp.where(own, sums, 0.0)
    for k in range(HEADS // packed):
        rows = sums[k * packed : (k + 1) * packed, :]
        short_ref[BIAS_ROW + k : BIAS_ROW + k + 1, :] = jnp.sum(rows, axis=0, keepdims=True)


def block_output(
    place_col, residual, valid, rows, branch_stat, gain1_grad, gain2_grad, by_distance, bucket_table
):
    length, width = residual.shape
    span = by_distance.shape[2]
    return pl.pallas_call(
        output_kernel,
        out_shape=(
            jax.ShapeDtypeStruct((length, width), BF16),
            jax.ShapeDtypeStruct((SHORT_ROWS, BLOCK), F32),
        ),
        scratch_shapes=[pltpu.VMEM((-(-HEADS // 8) * 8, span), F32)],
        compiler_params=params(),
        cost_estimate=cost(0.01),
        name="block_output",
    )(
        place_col, residual, valid.T, rows, branch_stat, gain1_grad, gain2_grad, by_distance,
        bucket_table[None, :span],
    )


def swap(values, axis, bit):
    size = lax.axis_size(axis)
    return lax.ppermute(values, axis, [(i, i ^ bit) for i in range(size)])


def axis_bits(axis):
    size = lax.axis_size(axis)
    bits = []
    bit = 1
    while bit < size:
        bits.append((axis, bit))
        bit *= 2
    return bits


def spread(keep, away):
    arrived = swap(away, "expert", 1)
    found = []
    for j in range(keep.shape[0]):
        for part in (keep[j], arrived[j]):
            found.append(swap(part, "expert", 2 * j) if j else part)
    return found


def spread_direct(keep, away):
    found = [keep[0]]
    for k in range(1, 2 * keep.shape[0]):
        found.append(swap((keep, away)[k % 2][k // 2], "expert", k))
    return found


def after(values, *others):
    return lax.optimization_barrier((values, others))[0]


def levels():
    groups, owners = lax.axis_size("dp"), lax.axis_size("expert")
    dp, expert = lax.axis_index("dp"), lax.axis_index("expert")
    axes = ("dp", "expert")

    def sender(width, fold):
        def send(values, k):
            def target(i):
                d, e = fold(i // owners, i % owners, k)
                return d * owners + e

            return lax.ppermute(values, axes, [(i, target(i)) for i in range(groups * owners)])

        return send

    return [
        (2, dp % 2, sender(2, lambda d, e, k: (d ^ k, e))),
        (
            groups,
            dp // 2 * 2 + expert % 2,
            sender(groups, lambda d, e, k: (d ^ (k // 2 * 2), e ^ (k % 2))),
        ),
        (owners // 2, expert // 2, sender(owners // 2, lambda d, e, k: (d, e ^ (2 * k)))),
    ]


def halve_kernel(place_ref, mine_ref, arrived_ref, *out_refs):
    rows = out_refs[0].shape[0]
    for k, out in enumerate(out_refs):
        here = pl.ds(pl.multiple_of((place_ref[0] ^ k) * rows, 16), rows)
        out[...] = (mine_ref[here, :].astype(F32) + arrived_ref[here, :].astype(F32)).astype(BF16)


def halve(place, mine, arrived, count):
    rows, width = mine.shape
    in_vmem = pl.BlockSpec(memory_space=pltpu.VMEM)
    return pl.pallas_call(
        halve_kernel,
        in_specs=[pl.BlockSpec(memory_space=pltpu.SMEM), in_vmem, in_vmem],
        out_shape=[jax.ShapeDtypeStruct((rows // count, width), BF16)] * count,
        compiler_params=params(),
        cost_estimate=cost(0.01),
        name="halve",
    )(place.astype(jnp.int32)[None], mine, arrived)


def sum_everywhere(mine, away, fillers):
    steps = levels()
    fillers = iter(fillers)

    def fill(terms, ready):
        found = [run(ready) for run in next(fillers, ())]
        return after(terms, *found) if found else terms

    _, _, send = steps[0]
    arrived = fill(send(away, 1), (mine, away))
    blocks = None
    for count, place, send in steps[1:]:
        if blocks is None:
            blocks = halve(place, mine, arrived, count)
        else:
            share = values.shape[0] // count
            blocks = [
                lax.dynamic_slice_in_dim(values, (place ^ k) * share, share, 0)
                for k in range(count)
            ]
        sent = fill([send(blocks[k], k) for k in range(1, count)], blocks)
        values = sum(t.astype(F32) for t in [blocks[0]] + sent).astype(BF16)
    for count, place, send in reversed(steps[1:]):
        share = values.shape[0]
        sent = fill([send(values, k) for k in range(1, count)], values)
        found = jnp.zeros((count * share, values.shape[1]), BF16)
        for k, piece in enumerate([values] + sent):
            found = lax.dynamic_update_slice_in_dim(found, piece, (place ^ k) * share, 0)
        values = found
    _, _, send = steps[0]
    other = fill(send(values, 1), values)
    for rest in fillers:
        for run in rest:
            run(values)
    return values, other


def widen_kernel(half_ref, rows_ref, *rest):
    qkv_ref, outw_ref = rest[-2:]
    j = pl.program_id(0)

    @pl.when(j < 3)
    def _():
        qkv_ref[...] = rows_ref[...].astype(F32)

    @pl.when(j == 3)
    def _():
        outw_ref[...] = rows_ref[...].astype(F32)


def widen(half, rows, width, old):
    taken = width // 2
    in_specs = [pl.BlockSpec((taken, width), lambda j, _: (j, 0))]
    arguments = (rows,)
    aliases = {}
    if old is not None:
        in_specs += [pl.BlockSpec(memory_space=pl.ANY)] * 2
        arguments += tuple(old)
        aliases = {2: 0, 3: 1}
    return pl.pallas_call(
        widen_kernel,
        grid_spec=pltpu.PrefetchScalarGridSpec(
            num_scalar_prefetch=1,
            grid=(4,),
            in_specs=in_specs,
            out_specs=[
                pl.BlockSpec((taken, width), lambda j, s: (s[0], jnp.minimum(j, 2))),
                pl.BlockSpec((taken, width), lambda j, s: (s[0], 0)),
            ],
        ),
        out_shape=(
            jax.ShapeDtypeStruct((width, 3 * width), F32),
            jax.ShapeDtypeStruct((width, width), F32),
        ),
        input_output_aliases=aliases,
        compiler_params=params(),
        cost_estimate=cost(4),
        name="widen",
    )(half, *arguments)


def sum_small(values):
    axes = ("dp", "expert")
    devices = lax.axis_size("dp") * lax.axis_size("expert")
    sent = jnp.broadcast_to(values[None], (devices,) + values.shape)
    return jnp.sum(lax.all_to_all(sent, axes, 0, 0, tiled=True), axis=0)


def on_device(
    hidden_in, doc_ids, valid_mask, expert_ids, bucket_table, norm1_gain, qkv_weight, position_bias,
    out_weight, norm2_gain, router_weight, up_weight, down_weight, out_grad,
):
    length, width = hidden_in.shape
    local = up_weight.shape[0]
    owners = lax.axis_size("expert")
    groups = lax.axis_size("dp")
    devices = owners * groups
    kinds = router_weight.shape[1]
    chunks = 2 if local % 4 == 0 else 1
    each = local // chunks
    half = owners // 2
    me = lax.axis_index("expert").astype(jnp.int32)
    group = lax.axis_index("dp").astype(jnp.int32)
    scalars = jnp.stack([me * local, me])
    group_scalars = jnp.stack([me * local, group])

    owner, inside = expert_ids // local, expert_ids % local
    far = owner ^ me
    chunk, within = inside // each, inside % each
    last = chunk == chunks - 1
    turned = far % 2 * half + far // 2
    send_ids = (chunk * owners + jnp.where(chunk == 0, turned, owner)) * each + within
    keep_ids = (chunk * owners + jnp.where(last, far, owner)) * each + within
    place_row, place_col, grad_rows = route(
        expert_ids, send_ids, keep_ids, out_grad, owners * local * CAP
    )
    to_owners = functools.partial(
        lax.all_to_all, axis_name="expert", split_axis=0, concat_axis=0, tiled=True
    )
    grads = to_owners(grad_rows.reshape(owners, local * CAP, width))
    size = owners * each * CAP
    probs, qkv, n1_t, ctx_t, residual, branch_stat, keep, away, *other = attention_forward(
        hidden_in, norm1_gain, qkv_weight, out_weight, norm2_gain, doc_ids, valid_mask,
        bucket_table, position_bias, place_row, (size // 2, size // 2) + (size,) * (chunks - 1),
    )
    shape = (half, each * CAP, width)
    rows = spread(keep.reshape(shape), away.reshape(shape))
    first_row = rows[1]
    backs, router_parts = [], []
    carried = None
    side = active_grads(after(grads, first_row), down_weight, 0, each)
    for c in range(chunks):
        later = later_side = None
        if c + 1 < chunks:
            later = [to_owners(after(other[c], side, *rows).reshape(owners, each * CAP, width))]
        *back, rows_all, active, router_part = run_experts(
            rows, side, up_weight, router_weight, scalars, c * each, carried, c + 1 == chunks
        )
        carried = rows_all, active
        if c + 1 < chunks:
            backs.append(to_owners(back[0]))
            later_side = active_grads(
                after(grads, router_part), down_weight, (c + 1) * each, each
            )
        rows, side = later, later_side
        router_parts.append(router_part)
    keep, away = back
    last_backs = spread_direct(keep, away)
    outs = expert_outputs(after(active, keep, away), down_weight)
    backs = after(backs + last_backs, outs)
    router_grad = functools.reduce(jnp.add, router_parts)
    backs = [b.reshape(-1, width) for b in backs]

    core = (group % 2)[None]
    unit_rows = 16 * groups * max(half // 16, 1)
    sum_rows = -(-(4 * width + kinds) // (2 * unit_rows)) * unit_rows
    gain2_grad, residual_grad, mine, away, ctx_grad = residual_backward(
        core, place_col, residual, norm2_gain, out_grad, out_weight, ctx_t, router_grad, backs,
        sum_rows,
    )
    dq, dk, dv, mine, away, by_distance = attention_backward(
        core, qkv, ctx_grad, probs, n1_t, mine, away
    )
    outs = to_owners(after(outs, *backs)).reshape(owners * local * CAP, width)
    rows_gathered = lax.all_gather(after(rows_all, last_backs[1]), "dp")
    grads_gathered = lax.all_gather(after(grads, first_row), "dp")
    expert_grads = [None]

    def some_experts(first, count, ready):
        expert_grads[0] = expert_wgrads(
            rows_gathered, after(grads_gathered, ready), up_weight, down_weight, router_weight,
            group_scalars, first, count, expert_grads[0],
        )
        return expert_grads[0]

    results = {}

    def first_norm(ready):
        results["input"] = input_backward(
            hidden_in, norm1_gain, after(residual_grad, ready), qkv_weight, (dq, dk, dv)
        )
        return results["input"]

    def last_sum(ready):
        results["output"] = block_output(
            place_col, residual, valid_mask, after(outs, ready), branch_stat, results["input"][1],
            gain2_grad, by_distance, bucket_table,
        )
        return results["output"]

    def short_sums(ready):
        results["short"] = sum_small(results["output"][1])
        return [results["short"]]

    sizes = [local]
    if local % 8 == 0:
        sizes = [local * 3 // 8, local // 8, local // 8, local * 3 // 8]
    starts = [sum(sizes[:k]) for k in range(len(sizes))]
    experts = [
        [functools.partial(some_experts, at, size)] for at, size in zip(starts, sizes, strict=True)
    ]
    experts += [[]] * (4 - len(experts))
    fillers = [[first_norm], experts[0], [last_sum] + experts[1], [short_sums] + experts[2]]
    fillers += [experts[3]]
    mine, other = sum_everywhere(mine, away, fillers)
    block_out, input_grad = results["output"][0], results["input"][0]
    short = results["short"]
    gain_rows = width // BLOCK
    gain1_sum = short[:gain_rows].reshape(-1)
    gain2_sum = short[6 : 6 + gain_rows].reshape(-1)
    bias_sum = short[BIAS_ROW:].reshape(-1, NBUCKET)[:HEADS].T
    stat_sums = short[STAT_ROW]
    rms_stats = jnp.sqrt(stat_sums[:3] / (jnp.maximum(stat_sums[3], 1.0) * width))
    wide = widen(core, mine, width, None)
    qkv_sum, outw_sum = widen(1 - core, other, width, wide)
    used = slice(2 * width, 2 * width + kinds // 2)
    first = core[0] == 0
    router_sum = jnp.concatenate(
        [
            jnp.where(first, mine[used], other[used]),
            jnp.where(first, other[used], mine[used]),
        ]
    ).astype(F32)
    return (
        block_out,
        input_grad,
        gain1_sum,
        qkv_sum,
        bias_sum,
        outw_sum,
        gain2_sum,
        router_sum.T,
        *expert_grads[0],
        rms_stats,
    )


def solution(mesh):
    spread = P(("dp", "expert"), None)
    placed = (spread,) * 4 + (P(),) * 7 + (P("expert", None, None),) * 2 + (spread,)
    return jax.shard_map(
        on_device,
        mesh=mesh,
        in_specs=placed,
        out_specs=(spread, spread)
        + (P(),) * 6
        + (P("expert", None, "dp"), P("expert", "dp", None), P()),
        check_vma=False,
    )
```

```python
import functools

import jax
import jax.numpy as jnp
from jax import lax
from jax.experimental import pallas as pl
from jax.experimental.pallas import tpu as pltpu
from jax.sharding import PartitionSpec as P

HEADS = 12
HEAD_DIM = 64
NBUCKET = 32
CAP = 24
BLOCK = 128
WINDOW = 3
PAIR = 2 * HEAD_DIM
EPSILON = 1e-06
NEGATIVE = -1e30
HIGHEST = lax.Precision.HIGHEST
BF16 = jnp.bfloat16
F32 = jnp.float32
SUBSTEPS = 6
VMEM_LIMIT = 58 * 1024 * 1024


NN = (((1,), (0,)), ((), ()))
NT = (((1,), (1,)), ((), ()))
TN = (((0,), (0,)), ((), ()))


def dot(left, right, dims=NN, precision=None):
    return lax.dot_general(left, right, dims, precision=precision, preferred_element_type=F32)


def iota(shape, dim):
    return lax.broadcasted_iota(jnp.int32, shape, dim)


def whole(shape):
    return pl.BlockSpec(shape, lambda *_: (0,) * len(shape))


def params(**more):
    return pltpu.CompilerParams(vmem_limit_bytes=VMEM_LIMIT, **more)


def cost(microseconds):
    return pl.CostEstimate(
        flops=int(microseconds * 1.1e9), bytes_accessed=1000, transcendentals=0
    )


def windows(length):
    found = []
    row = 0
    for number in range(length // BLOCK):
        first = max(number - WINDOW + 1, 0)
        keys = (number - first + 1) * BLOCK
        found.append((number * BLOCK, first * BLOCK, keys, row))
        row += keys
    return found, row


def rms(values):
    return lax.rsqrt(jnp.mean(values * values, axis=-1, keepdims=True) + EPSILON)


def hot_columns(row0, row1, count, offset):
    slots = iota((count, row0.shape[1]), 0) + offset
    return jnp.where((slots == row0) | (slots == row1), 1.0, 0.0).astype(BF16)


def hot_rows(col0, col1, count, offset):
    slots = iota((col0.shape[0], count), 1) + offset
    return jnp.where((slots == col0) | (slots == col1), 1.0, 0.0).astype(BF16)


def route_kernel(ids_ref, send_ref, keep_ref, grad_ref, row_ref, col_ref, rows_ref):
    length = grad_ref.shape[0]
    experts = rows_ref.shape[0] // CAP
    before = iota((length, length), 0) < iota((length, length), 1)
    upper = jnp.where(before, 1.0, 0.0).astype(BF16)
    after = iota((length, length), 0) > iota((length, length), 1)
    lower = jnp.where(after, 1.0, 0.0).astype(BF16)
    number = iota((experts, length), 0)
    hot = [number == ids_ref[c : c + 1, :] for c in range(2)]
    both = jnp.where(hot[0] | hot[1], 1.0, 0.0).astype(BF16)
    rank = dot(both, upper)
    rows = []
    for c in range(2):
        mine = jnp.sum(jnp.where(hot[c], rank, 0.0), axis=0, keepdims=True).astype(jnp.int32)
        rows.append(ids_ref[c : c + 1, :] * CAP + mine)
        row_ref[c : c + 1, :] = send_ref[c : c + 1, :] * CAP + mine
    number = iota((length, experts), 1)
    hot = [number == keep_ref[:, c : c + 1] for c in range(2)]
    both = jnp.where(hot[0] | hot[1], 1.0, 0.0).astype(BF16)
    rank = dot(lower, both)
    for c in range(2):
        mine = jnp.sum(jnp.where(hot[c], rank, 0.0), axis=1, keepdims=True).astype(jnp.int32)
        for kind in range(2):
            at = slice(2 * kind + c, 2 * kind + c + 1)
            col_ref[:, at] = keep_ref[:, at] * CAP + mine
    chosen = hot_columns(rows[0], rows[1], rows_ref.shape[0], 0)
    rows_ref[...] = dot(chosen, grad_ref[...]).astype(BF16)


def route(ids, send_ids, keep_ids, out_grad, slots):
    length, width = out_grad.shape
    return pl.pallas_call(
        route_kernel,
        out_shape=(
            jax.ShapeDtypeStruct((2, length), jnp.int32),
            jax.ShapeDtypeStruct((length, 4), jnp.int32),
            jax.ShapeDtypeStruct((slots, width), BF16),
        ),
        compiler_params=params(),
        cost_estimate=cost(5),
        name="route",
    )(ids.T, send_ids.T, jnp.concatenate([keep_ids, ids], axis=1), out_grad)


def forward_kernel(
    x_ref, gain1_ref, qkvw_ref, outw_ref, gain2_ref, docr_ref, docc_ref, validc_ref, bucket_ref,
    pbias_ref, row_ref,
    probs_ref, qkv_ref, n1t_ref, ctx_ref, residual_ref, stat_ref, *rest,
):
    rows_refs, (mask_s, bias_s, toeplitz_s) = rest[:-3], rest[-3:]
    pair = pl.program_id(0)
    length, width = x_ref.shape
    spans, _ = windows(length)

    @pl.when(pair == 0)
    def _():
        x = x_ref[...].astype(F32)
        n1 = (x * rms(x) * gain1_ref[...]).astype(BF16)
        n1t_ref[...] = n1.T
        for j in range(3):
            part = slice(j * width, (j + 1) * width)
            qkv_ref[:, part] = dot(n1, qkvw_ref[:, part]).astype(BF16)
        for q0, k0, keys, row in spans:
            shape = (keys, BLOCK)
            distance = (iota(shape, 1) + q0) - (iota(shape, 0) + k0)
            allowed = (
                (distance >= 0)
                & (docc_ref[k0 : k0 + keys, :] == docr_ref[:, q0 : q0 + BLOCK])
                & ((validc_ref[k0 : k0 + keys, :] == 1) | (distance == 0))
            )
            mask_s[row : row + keys, :] = jnp.where(allowed, 0.0, NEGATIVE)
        span = bias_s.shape[1]
        hot = jnp.where(iota((NBUCKET, span), 0) == bucket_ref[...], 1.0, 0.0)
        bias_s[...] = dot(pbias_ref[...], hot, precision=HIGHEST)

    for side in range(2):
        head_bias = bias_s[pl.ds(2 * pair + side, 1), :]
        for m in range(WINDOW):
            ahead = head_bias[:, m * BLOCK : (m + 1) * BLOCK]
            back = max(m - 1, 0)
            behind = head_bias[:, back * BLOCK : (back + 1) * BLOCK]
            lanes = jnp.broadcast_to(
                jnp.concatenate([ahead, behind], axis=1), (BLOCK, 2 * BLOCK)
            )
            rolled = pltpu.roll(lanes, 0, 1, stride=1, stride_axis=0)
            place = (WINDOW - 1 - m) * BLOCK
            toeplitz_s[place : place + BLOCK, side * BLOCK : (side + 1) * BLOCK] = rolled[
                :, :BLOCK
            ]

    at = pl.multiple_of(pair * PAIR, PAIR)
    first_head = iota((BLOCK, PAIR), 1) < HEAD_DIM
    top = iota((PAIR, BLOCK), 0) < HEAD_DIM
    for q0, k0, keys, row in spans:
        q = qkv_ref[q0 : q0 + BLOCK, pl.ds(at, PAIR)].astype(F32) * HEAD_DIM ** (-0.5)
        stacked = jnp.concatenate(
            [jnp.where(first_head, q, 0.0), jnp.where(first_head, 0.0, q)], axis=0
        ).astype(BF16)
        k = qkv_ref[k0 : k0 + keys, pl.ds(pl.multiple_of(width + at, PAIR), PAIR)]
        v = qkv_ref[k0 : k0 + keys, pl.ds(pl.multiple_of(2 * width + at, PAIR), PAIR)]
        scores = dot(k, stacked, NT)
        masked = mask_s[row : row + keys, :]
        for side in range(2):
            lanes = slice(side * BLOCK, (side + 1) * BLOCK)
            s = scores[:, lanes] + toeplitz_s[WINDOW * BLOCK - keys :, lanes] + masked
            peak = jnp.max(s, axis=0, keepdims=True)
            e = jnp.exp(s - peak)
            total = jnp.sum(e, axis=0, keepdims=True)
            probs_ref[0, row : row + keys, lanes] = (e * (1.0 / total)).astype(BF16)
        both = dot(v, probs_ref[0, row : row + keys, :], TN)
        ctx = jnp.where(top, both[:, :BLOCK], both[:, BLOCK:])
        ctx_ref[pl.ds(at, PAIR), q0 : q0 + BLOCK] = ctx.astype(BF16)

    @pl.when(pair == pl.num_programs(0) - 1)
    def _():
        branch = dot(ctx_ref[...], outw_ref[...], TN)
        valid = validc_ref[...].astype(F32)
        stat_ref[...] = jnp.sum(valid * branch * branch, axis=0, keepdims=True)
        residual = x_ref[...].astype(F32) + branch
        residual_ref[...] = residual
        n2 = (residual * rms(residual) * gain2_ref[...]).astype(BF16)
        offset = 0
        for out in rows_refs:
            chosen = hot_columns(row_ref[0:1, :], row_ref[1:2, :], out.shape[0], offset)
            out[...] = dot(chosen, n2).astype(BF16)
            offset += out.shape[0]


def attention_forward(
    x, gain1, qkvw, outw, gain2, docs, valid, bucket_table, position_bias, place_row, sizes
):
    length, width = x.shape
    _, stored = windows(length)
    pairs = width // PAIR
    span = WINDOW * BLOCK
    padded_heads = -(-HEADS // 8) * 8
    bias_t = jnp.zeros((padded_heads, NBUCKET), F32).at[:HEADS].set(position_bias.T)
    arguments = (
        x, gain1[None], qkvw, outw, gain2[None], docs, docs.T, valid.T,
        bucket_table[None, :span], bias_t, place_row,
    )
    out_shape = (
        jax.ShapeDtypeStruct((pairs, stored, 2 * BLOCK), BF16),
        jax.ShapeDtypeStruct((length, 3 * width), BF16),
        jax.ShapeDtypeStruct((width, length), BF16),
        jax.ShapeDtypeStruct((width, length), BF16),
        jax.ShapeDtypeStruct((length, width), F32),
        jax.ShapeDtypeStruct((1, width), F32),
    ) + tuple(jax.ShapeDtypeStruct((n, width), BF16) for n in sizes)
    return pl.pallas_call(
        forward_kernel,
        grid=(pairs,),
        in_specs=[whole(a.shape) for a in arguments],
        out_specs=[pl.BlockSpec((1, stored, 2 * BLOCK), lambda p: (p, 0, 0))]
        + [whole(s.shape) for s in out_shape[1:]],
        out_shape=out_shape,
        scratch_shapes=[
            pltpu.VMEM((stored, BLOCK), F32),
            pltpu.VMEM((padded_heads, span), F32),
            pltpu.VMEM((span, 2 * BLOCK), F32),
        ],
        compiler_params=params(),
        cost_estimate=cost(22),
        name="attention_forward",
    )(*arguments)


def expert_gate(rows, router, expert):
    logits = dot(rows, router)
    shifted = jnp.exp(logits - jnp.max(logits, axis=-1, keepdims=True))
    probs = shifted / jnp.sum(shifted, axis=-1, keepdims=True)
    mine = iota(probs.shape, 1) == expert
    return probs, mine, jnp.sum(jnp.where(mine, probs, 0.0), axis=-1, keepdims=True)


GELU_SCALE = 0.7978845608028654
GELU_CUBE = 0.044715


def gelu_parts(v):
    square = v * v
    t = jnp.tanh(v * (GELU_SCALE + (GELU_SCALE * GELU_CUBE) * square))
    half = 0.5 * v
    value = half + half * t
    slope = 0.5 + 0.5 * t + half * (1.0 - t * t) * (
        GELU_SCALE + (3.0 * GELU_SCALE * GELU_CUBE) * square
    )
    return value, slope


def active_grad_kernel(grads_ref, down_ref, out_ref, g_s, grads_s, *, first):
    e, f = pl.program_id(0), pl.program_id(1)

    @pl.when((e == 0) & (f == 0))
    def _():
        grads_s[...] = grads_ref[...].astype(F32)

    @pl.when(f == 0)
    def _():
        here = pl.ds(pl.multiple_of((first + e) * CAP, CAP), CAP)
        g_s[...] = grads_s[:, here, :].reshape(g_s.shape).astype(BF16)

    out_ref[0] = dot(g_s[...], down_ref[0], NT).astype(BF16)


def active_grads(grads, down_weight, first, experts, blocks=1):
    owners, _, width = grads.shape
    inner = down_weight.shape[1]
    step, count = inner // blocks, owners * CAP
    return pl.pallas_call(
        functools.partial(active_grad_kernel, first=first),
        grid=(experts, blocks),
        in_specs=[
            whole(grads.shape),
            pl.BlockSpec((1, step, width), lambda e, f: (first + e, f, 0)),
        ],
        out_specs=pl.BlockSpec((1, count, step), lambda e, f: (e, 0, f)),
        out_shape=jax.ShapeDtypeStruct((experts, count, inner), BF16),
        scratch_shapes=[pltpu.VMEM((count, width), BF16), pltpu.VMEM(grads.shape, F32)],
        compiler_params=params(),
        cost_estimate=cost(0.01),
        name="active_grads",
    )(grads, down_weight)


def expert_kernel(scalar_ref, *refs, parts, aliased, last):
    rows_refs, refs = refs[:parts], refs[parts:]
    side_ref, up_ref, router_ref = refs[:3]
    refs = refs[3 + aliased :]
    backs = max(last, 1)
    back_refs, refs = refs[:backs], refs[backs:]
    all_ref, active_ref, router_grad_ref = refs[:3]
    rows_s, back_s, x_s, probs_s, gate_s, sum_s, dx_s, grad_s = refs[3:]
    e, f = pl.program_id(0), pl.program_id(1)
    experts, blocks = pl.num_programs(0), pl.num_programs(1)
    me = scalar_ref[1]
    expert = scalar_ref[0] + e
    count, width = x_s.shape
    owners = rows_s.shape[0]
    here = pl.ds(pl.multiple_of(e * CAP, CAP), CAP)

    @pl.when((e == 0) & (f == 0))
    def _():
        if parts == 1:
            all_ref[0] = rows_refs[0][...]
            rows_s[...] = rows_refs[0][...].astype(F32)
        else:
            for k in range(parts):
                all_ref[0, me ^ k] = rows_refs[k][...]
                rows_s[me ^ k] = rows_refs[k][...].astype(F32)
        router_grad_ref[...] = jnp.zeros_like(router_grad_ref)

    @pl.when(f == 0)
    def _():
        x = rows_s[:, here, :].reshape(count, width).astype(BF16)
        x_s[...] = x
        probs, _, gate = expert_gate(x, router_ref[...], expert)
        probs_s[...] = probs
        gate_s[...] = jnp.broadcast_to(gate, gate_s.shape)
        sum_s[...] = jnp.zeros_like(sum_s)
        dx_s[...] = jnp.zeros_like(dx_s)

    gate = gate_s[:, :1]
    x = x_s[...]
    step = up_ref.shape[2] // SUBSTEPS
    total = None
    inner = dot(x, up_ref[0, :, :step])
    for s in range(SUBSTEPS):
        here_f = slice(s * step, (s + 1) * step)
        later = dot(x, up_ref[0, :, (s + 1) * step : (s + 2) * step]) if s + 1 < SUBSTEPS else None
        value, slope = gelu_parts(inner)
        side = side_ref[0, :, here_f].astype(F32) * gate
        part = jnp.sum(value * side, axis=-1, keepdims=True)
        total = part if total is None else total + part
        active_ref[0, :, here_f] = (gate * value).astype(BF16)
        grad_s[:, here_f] = (side * slope).astype(BF16)
        inner = later
    sum_s[...] += total
    dx_s[...] += dot(grad_s[...], up_ref[0], NT)

    @pl.when(f == blocks - 1)
    def _():
        probs = probs_s[...]
        mine = iota(probs.shape, 1) == expert
        logit_grad = (sum_s[:, :1] * (jnp.where(mine, 1.0, 0.0) - probs)).astype(BF16)
        router_grad_ref[...] += dot(logit_grad, x_s[...], TN)
        dx = dx_s[...] + dot(logit_grad, router_ref[...], NT)
        back_s[:, here, :] = dx.reshape(owners, CAP, width)

    @pl.when((e == experts - 1) & (f == blocks - 1))
    def _():
        if last:
            for k in range(owners):
                back_refs[k][...] = back_s[me ^ k].astype(BF16)
        else:
            back_refs[0][...] = back_s[...].astype(BF16)


def run_experts(
    rows, side, up_weight, router, scalars, first, old, last
):
    parts = len(rows)
    slots, width = rows[0].shape[-2:]
    owners = parts if parts > 1 else rows[0].shape[0]
    experts = slots // CAP
    local, _, inner = up_weight.shape
    count, kinds = owners * CAP, router.shape[1]
    blocks = 1 if count <= 256 else 3
    step = inner // blocks
    backs = [jax.ShapeDtypeStruct((owners, slots, width), BF16)]
    if last:
        backs = [jax.ShapeDtypeStruct((slots, width), BF16)] * owners
    in_specs = [whole(r.shape) for r in rows] + [
        pl.BlockSpec((1, count, step), lambda e, f, _: (e, 0, f)),
        pl.BlockSpec((1, width, step), lambda e, f, _: (first + e, 0, f)),
        whole(router.shape),
    ]
    arguments = (*rows, side, up_weight, router)
    aliases = {}
    if old is not None:
        aliases = {1 + len(arguments) + k: len(backs) + k for k in range(2)}
        in_specs += [pl.BlockSpec(memory_space=pl.ANY)] * 2
        arguments += tuple(old)
    return pl.pallas_call(
        functools.partial(expert_kernel, parts=parts, aliased=len(aliases), last=owners if last else 0),
        grid_spec=pltpu.PrefetchScalarGridSpec(
            num_scalar_prefetch=1,
            grid=(experts, blocks),
            in_specs=in_specs,
            out_specs=[whole(back.shape) for back in backs]
            + [
                pl.BlockSpec((1, owners, slots, width), lambda e, f, _: (first // experts, 0, 0, 0)),
                pl.BlockSpec((1, count, step), lambda e, f, _: (first + e, 0, f)),
                whole((kinds, width)),
            ],
            scratch_shapes=[
                pltpu.VMEM((owners, slots, width), F32),
                pltpu.VMEM((owners, slots, width), F32),
                pltpu.VMEM((count, width), BF16),
                pltpu.VMEM((count, kinds), F32),
                pltpu.VMEM((count, BLOCK), F32),
                pltpu.VMEM((count, BLOCK), F32),
                pltpu.VMEM((count, width), F32),
                pltpu.VMEM((count, step), BF16),
            ],
        ),
        out_shape=(
            *backs,
            jax.ShapeDtypeStruct((local // experts, owners, slots, width), BF16),
            jax.ShapeDtypeStruct((local, count, inner), BF16),
            jax.ShapeDtypeStruct((kinds, width), F32),
        ),
        input_output_aliases=aliases,
        compiler_params=params(),
        cost_estimate=cost(22),
        name="experts",
    )(scalars + jnp.array([first, 0], jnp.int32), *arguments)


def expert_out_kernel(active_ref, down_ref, out_ref, sum_s, all_s):
    e, f = pl.program_id(0), pl.program_id(1)
    experts, blocks = pl.num_programs(0), pl.num_programs(1)
    part = dot(active_ref[0], down_ref[0])

    @pl.when(f == 0)
    def _():
        sum_s[...] = part

    @pl.when(f > 0)
    def _():
        sum_s[...] += part

    @pl.when(f == blocks - 1)
    def _():
        here = pl.ds(pl.multiple_of(e * CAP, CAP), CAP)
        all_s[:, here, :] = sum_s[...].reshape(all_s.shape[0], CAP, all_s.shape[2])

    @pl.when((e == experts - 1) & (f == blocks - 1))
    def _():
        out_ref[...] = all_s[...].astype(BF16)


def expert_outputs(active, down_weight, blocks=1):
    experts, count, inner = active.shape
    width = down_weight.shape[2]
    step, owners = inner // blocks, count // CAP
    shape = (owners, experts * CAP, width)
    return pl.pallas_call(
        expert_out_kernel,
        grid=(experts, blocks),
        in_specs=[
            pl.BlockSpec((1, count, step), lambda e, f: (e, 0, f)),
            pl.BlockSpec((1, step, width), lambda e, f: (e, f, 0)),
        ],
        out_specs=whole(shape),
        out_shape=jax.ShapeDtypeStruct(shape, BF16),
        scratch_shapes=[pltpu.VMEM((count, width), F32), pltpu.VMEM(shape, F32)],
        compiler_params=params(),
        cost_estimate=cost(0.01),
        name="expert_outputs",
    )(active, down_weight)


def expert_wgrad_kernel(
    scalar_ref, rows_ref, grads_ref, up_ref, down_ref, router_ref, *rest, first
):
    up_out, down_out, x_s, g_s = rest[-4:]
    expert, tile = first + pl.program_id(0), pl.program_id(1)
    count, width = x_s.shape
    for side in range(2):

        @pl.when(expert % 2 == side)
        def _():
            part = slice(side * CAP, (side + 1) * CAP)
            x = rows_ref[...].astype(F32)[:, 0, :, part, :].reshape(count, width).astype(BF16)
            x_s[...] = x
            _, _, gate = expert_gate(x, router_ref[...], scalar_ref[0] + expert)
            g = grads_ref[...].astype(F32)[:, :, part, :].reshape(count, width)
            g_s[...] = (gate * g).astype(BF16)

    x, g = x_s[...], g_s[...]
    value, slope = gelu_parts(dot(x, up_ref[0]))
    inner_grad = (dot(g, down_ref[0], NT) * slope).astype(BF16)

    @pl.when(tile == 0)
    def _():
        down_out[0] = dot(value.astype(BF16), g, TN)
        up_out[0] = dot(x, inner_grad, TN)

    @pl.when(tile > 0)
    def _():
        down_out[0] += dot(value.astype(BF16), g, TN)
        up_out[0] += dot(x, inner_grad, TN)


def expert_wgrads(rows, grads, up_weight, down_weight, router, scalars, first, experts, old):
    groups, chunks, owners, _, width = rows.shape
    local, _, inner = up_weight.shape
    each = local // chunks
    share = inner // groups
    taken = max(min(groups, 32 // owners), 1)
    count = taken * owners * CAP

    def rows_at(e, t, _):
        return (t, (first + e) // each, 0, (first + e) % each // 2, 0)

    in_specs = [
        pl.BlockSpec((taken, 1, owners, 2 * CAP, width), rows_at),
        pl.BlockSpec((taken, owners, 2 * CAP, width), lambda e, t, _: (t, 0, (first + e) // 2, 0)),
        pl.BlockSpec((1, width, share), lambda e, t, s: (first + e, 0, s[1])),
        pl.BlockSpec((1, share, width), lambda e, t, s: (first + e, s[1], 0)),
        whole(router.shape),
    ]
    arguments = (rows, grads, up_weight, down_weight, router)
    aliases = {}
    if old is not None:
        aliases = {6: 0, 7: 1}
        in_specs += [pl.BlockSpec(memory_space=pl.ANY)] * 2
        arguments += tuple(old)
    return pl.pallas_call(
        functools.partial(expert_wgrad_kernel, first=first),
        grid_spec=pltpu.PrefetchScalarGridSpec(
            num_scalar_prefetch=1,
            grid=(experts, groups // taken),
            in_specs=in_specs,
            out_specs=[
                pl.BlockSpec((1, width, share), lambda j, t, _: (first + j, 0, 0)),
                pl.BlockSpec((1, share, width), lambda j, t, _: (first + j, 0, 0)),
            ],
            scratch_shapes=[
                pltpu.VMEM((count, width), BF16),
                pltpu.VMEM((count, width), BF16),
            ],
        ),
        out_shape=(
            jax.ShapeDtypeStruct((local, width, share), F32),
            jax.ShapeDtypeStruct((local, share, width), F32),
        ),
        input_output_aliases=aliases,
        compiler_params=params(),
        cost_estimate=cost(0.01),
        name="expert_wgrads",
    )(scalars, *arguments)


def residual_kernel(
    half_ref, col_ref, residual_ref, gain_ref, grad_ref, outw_ref, ctx_ref, router_ref, *rest
):
    back_refs, rest = rest[:-8], rest[-8:]
    gain_grad_ref, residual_grad_ref, mine_ref, away_ref, ctx_grad_ref, early_s, sem0, sem1 = rest
    whole_backs = back_refs[0][...]
    if len(back_refs) > 1:
        whole_backs = jnp.concatenate([back[...] for back in back_refs], axis=0)
    chosen = hot_rows(col_ref[:, 0:1], col_ref[:, 1:2], whole_backs.shape[0], 0)
    n2_grad = dot(chosen, whole_backs)
    residual = residual_ref[...]
    factor = rms(residual)
    unit = residual * factor
    gain_grad_ref[...] = jnp.sum(n2_grad * unit, axis=0, keepdims=True)
    scaled = n2_grad * gain_ref[...]
    centre = jnp.mean(scaled * unit, axis=-1, keepdims=True)
    residual_grad = grad_ref[...].astype(F32) + factor * (scaled - unit * centre)
    residual_grad_ref[...] = residual_grad
    branch_grad = residual_grad.astype(BF16)
    width, kinds = ctx_ref.shape[0], router_ref.shape[0]
    rows = early_s.shape[1]
    used = (width + kinds) // 2
    copies = []
    for k, (out, sem) in enumerate(((mine_ref, sem0), (away_ref, sem1))):
        part = half_ref[0] ^ k
        ctx = ctx_ref[pl.ds(pl.multiple_of(part * (width // 2), width // 2), width // 2), :]
        early_s[k, : width // 2, :] = dot(ctx, branch_grad).astype(BF16)
        router = router_ref[pl.ds(pl.multiple_of(part * (kinds // 2), kinds // 2), kinds // 2), :]
        early_s[k, width // 2 : used, :] = router.astype(BF16)
        if used < rows:
            early_s[k, used:, :] = jnp.zeros((rows - used, width), BF16)
        copies.append(
            pltpu.make_async_copy(early_s.at[k], out.at[pl.ds(3 * width // 2, rows)], sem)
        )
        copies[k].start()
    ctx_grad_ref[...] = dot(branch_grad, outw_ref[...], NT).astype(BF16)
    for copy in copies:
        copy.wait()


def residual_backward(
    half, place_col, residual, gain2, out_grad, outw, ctx_t, router_grad, backs, rows
):
    length, width = residual.shape
    early = rows - 3 * width // 2
    in_vmem = pl.BlockSpec(memory_space=pltpu.VMEM)
    anywhere = pl.BlockSpec(memory_space=pl.ANY)
    buffer = jax.ShapeDtypeStruct((rows, width), BF16)
    return pl.pallas_call(
        residual_kernel,
        in_specs=[pl.BlockSpec(memory_space=pltpu.SMEM)] + [in_vmem] * (7 + len(backs)),
        out_specs=[in_vmem, in_vmem, anywhere, anywhere, in_vmem],
        out_shape=(
            jax.ShapeDtypeStruct((1, width), F32),
            jax.ShapeDtypeStruct((length, width), F32),
            buffer,
            buffer,
            jax.ShapeDtypeStruct((length, width), BF16),
        ),
        scratch_shapes=[
            pltpu.VMEM((2, early, width), BF16),
            pltpu.SemaphoreType.DMA,
            pltpu.SemaphoreType.DMA,
        ],
        compiler_params=params(),
        cost_estimate=cost(0.01),
        name="residual_backward",
    )(half, place_col, residual, gain2[None], out_grad, outw, ctx_t, router_grad, *backs)


def attention_backward_kernel(
    half_ref, q_ref, k_ref, v_ref, dctx_ref, probs_ref, n1t_ref, _, __,
    dq_ref, dk_ref, dv_ref, mine_ref, away_ref, bias_ref,
    dqt_s, dk_s, dv_s, diagonal_s,
):
    length = q_ref.shape[0]
    spans, _ = windows(length)
    first_head = iota((BLOCK, PAIR), 1) < HEAD_DIM
    top = iota((PAIR, BLOCK), 0) < HEAD_DIM
    scale = HEAD_DIM ** (-0.5)
    dk_s[...] = jnp.zeros_like(dk_s)
    dv_s[...] = jnp.zeros_like(dv_s)
    diagonal_s[...] = jnp.zeros_like(diagonal_s)

    def stack(values):
        values = values.astype(F32)
        return jnp.concatenate(
            [jnp.where(first_head, values, 0.0), jnp.where(first_head, 0.0, values)], axis=0
        ).astype(BF16)

    for q0, k0, keys, row in spans:
        q = stack(q_ref[q0 : q0 + BLOCK, :])
        dctx = stack(dctx_ref[q0 : q0 + BLOCK, :])
        span = slice(k0, k0 + keys)
        probs = probs_ref[0, row : row + keys, :]
        prob_side = dot(v_ref[span, :], dctx, NT)
        halves = []
        for side in range(2):
            lanes = slice(side * BLOCK, (side + 1) * BLOCK)
            p = probs[:, lanes].astype(F32)
            d = prob_side[:, lanes]
            centre = jnp.sum(p * d, axis=0, keepdims=True)
            s = p * (d - centre)
            diagonal_s[WINDOW * BLOCK - keys :, lanes] += s
            halves.append(s.astype(BF16))
        score_grad = jnp.concatenate(halves, axis=1)
        dk_s[span, :] += dot(score_grad, q)
        dv_s[span, :] += dot(probs, dctx)
        both = dot(k_ref[span, :], score_grad, TN)
        dqt_s[:, q0 : q0 + BLOCK] = jnp.where(top, both[:, :BLOCK], both[:, BLOCK:])
    dq = (dqt_s[...].T * scale).astype(BF16)
    dk = (dk_s[...] * scale).astype(BF16)
    dv = dv_s[...].astype(BF16)
    dq_ref[...] = dq
    dk_ref[...] = dk
    dv_ref[...] = dv
    width = n1t_ref.shape[0]
    for k, out in enumerate((mine_ref, away_ref)):
        part = pl.multiple_of((half_ref[0] ^ k) * (width // 2), width // 2)
        n1t = n1t_ref[pl.ds(part, width // 2), :]
        for j, rows in enumerate((dq, dk, dv)):
            there = slice(j * (width // 2), (j + 1) * (width // 2))
            out[there, :] = dot(n1t, rows).astype(BF16)
    bias_ref[...] = jnp.zeros_like(bias_ref)
    for side in range(2):
        lanes = slice(side * BLOCK, (side + 1) * BLOCK)
        pieces = []
        for m in range(WINDOW):
            place = (WINDOW - 1 - m) * BLOCK
            block = diagonal_s[place : place + BLOCK, lanes]
            skewed = jnp.zeros((8, 2 * BLOCK), F32)
            for k in range(0, BLOCK, 8):
                eight = block[k : k + 8, :]
                wide = jnp.concatenate([eight, jnp.zeros_like(eight)], axis=1)
                skewed += wide if k == 0 else pltpu.roll(wide, 2 * BLOCK - k, 1)
            for bit in (1, 2, 4):
                moved = pltpu.roll(skewed, 2 * BLOCK - bit, 1)
                skewed = jnp.where(iota(skewed.shape, 0) & bit != 0, moved, skewed)
            pieces.append(jnp.sum(skewed, axis=0, keepdims=True))
        for m in range(WINDOW):
            total = pieces[m][:, :BLOCK]
            if m + 1 < WINDOW:
                total = total + pieces[m + 1][:, BLOCK:]
            bias_ref[0, side : side + 1, m * BLOCK : (m + 1) * BLOCK] = total


def attention_backward(half, qkv, ctx_grad, probs, n1_t, mine, away):
    length, width = ctx_grad.shape
    stored = probs.shape[1]
    pairs = width // PAIR
    span = WINDOW * BLOCK
    column = pl.BlockSpec((length, PAIR), lambda p, _: (0, p))
    summed = pl.BlockSpec((3 * width // 2, PAIR), lambda p, _: (0, p))
    anywhere = pl.BlockSpec(memory_space=pl.ANY)
    rows = jax.ShapeDtypeStruct((length, width), BF16)
    return pl.pallas_call(
        attention_backward_kernel,
        grid_spec=pltpu.PrefetchScalarGridSpec(
            num_scalar_prefetch=1,
            grid=(pairs,),
            in_specs=[
                column,
                pl.BlockSpec((length, PAIR), lambda p, _: (0, pairs + p)),
                pl.BlockSpec((length, PAIR), lambda p, _: (0, 2 * pairs + p)),
                column,
                pl.BlockSpec((1, stored, 2 * BLOCK), lambda p, _: (p, 0, 0)),
                whole(n1_t.shape),
                anywhere,
                anywhere,
            ],
            out_specs=[
                column,
                column,
                column,
                summed,
                summed,
                pl.BlockSpec((1, 8, span), lambda p, _: (p, 0, 0)),
            ],
            scratch_shapes=[
                pltpu.VMEM((PAIR, length), F32),
                pltpu.VMEM((length, PAIR), F32),
                pltpu.VMEM((length, PAIR), F32),
                pltpu.VMEM((span, 2 * BLOCK), F32),
            ],
        ),
        out_shape=(
            rows,
            rows,
            rows,
            jax.ShapeDtypeStruct(mine.shape, BF16),
            jax.ShapeDtypeStruct(away.shape, BF16),
            jax.ShapeDtypeStruct((pairs, 8, span), F32),
        ),
        input_output_aliases={7: 3, 8: 4},
        compiler_params=params(),
        cost_estimate=cost(96),
        name="attention_backward",
    )(half, qkv, qkv, qkv, ctx_grad, probs, n1_t, mine, away)


def input_kernel(x_ref, gain_ref, residual_grad_ref, qkvw_ref, *rest):
    parts, (grad_ref, gain_grad_ref) = rest[:-2], rest[-2:]
    x = x_ref[...].astype(F32)
    factor = rms(x)
    unit = x * factor
    n1_grad = None
    at = 0
    for part in parts:
        columns = part.shape[1]
        term = dot(part[...], qkvw_ref[:, at : at + columns], NT)
        n1_grad = term if n1_grad is None else n1_grad + term
        at += columns
    gain_grad_ref[...] = jnp.sum(n1_grad * unit, axis=0, keepdims=True)
    scaled = n1_grad * gain_ref[...]
    centre = jnp.mean(scaled * unit, axis=-1, keepdims=True)
    grad_ref[...] = (residual_grad_ref[...] + factor * (scaled - unit * centre)).astype(BF16)


def input_backward(x, gain1, residual_grad, qkvw, parts):
    length, width = x.shape
    return pl.pallas_call(
        input_kernel,
        out_shape=(
            jax.ShapeDtypeStruct((length, width), BF16),
            jax.ShapeDtypeStruct((1, width), F32),
        ),
        compiler_params=params(),
        cost_estimate=cost(0.01),
        name="input_backward",
    )(x, gain1[None], residual_grad, qkvw, *parts)


SHORT_ROWS = 16
STAT_ROW = 12
BIAS_ROW = 13


def output_kernel(
    col_ref, residual_ref, validc_ref, rows_ref, stat_ref, gain1_ref, gain2_ref, by_ref, bucket_ref,
    block_ref, short_ref, distance_s,
):
    chosen = hot_rows(col_ref[:, 2:3], col_ref[:, 3:4], rows_ref.shape[0], 0)
    mixture = dot(chosen, rows_ref[...])
    output = residual_ref[...] + mixture
    block_ref[...] = output.astype(BF16)
    valid = validc_ref[...].astype(F32)
    short_ref[...] = jnp.zeros_like(short_ref)
    for k in range(gain1_ref.shape[1] // BLOCK):
        lanes = slice(k * BLOCK, (k + 1) * BLOCK)
        short_ref[k : k + 1, :] = gain1_ref[:, lanes]
        short_ref[6 + k : 7 + k, :] = gain2_ref[:, lanes]
    lane = iota((1, BLOCK), 1)
    stats = jnp.where(lane == 0, jnp.sum(valid * output * output), 0.0)
    stats = jnp.where(lane == 1, jnp.sum(stat_ref[...]), stats)
    stats = jnp.where(lane == 2, jnp.sum(valid * mixture * mixture), stats)
    short_ref[STAT_ROW : STAT_ROW + 1, :] = jnp.where(lane == 3, jnp.sum(valid), stats)
    distance_s[...] = jnp.zeros_like(distance_s)
    for head in range(HEADS):
        distance_s[head : head + 1, :] = by_ref[head // 2, head % 2 : head % 2 + 1, :]
    buckets = iota((BLOCK, distance_s.shape[1]), 0) & (NBUCKET - 1)
    hot = jnp.where(buckets == bucket_ref[...], 1.0, 0.0)
    sums = dot(distance_s[...], hot, NT, HIGHEST)
    packed = BLOCK // NBUCKET
    own = iota(sums.shape, 1) // NBUCKET == iota(sums.shape, 0) % packed
    sums = jnp.where(own, sums, 0.0)
    for k in range(HEADS // packed):
        rows = sums[k * packed : (k + 1) * packed, :]
        short_ref[BIAS_ROW + k : BIAS_ROW + k + 1, :] = jnp.sum(rows, axis=0, keepdims=True)


def block_output(
    place_col, residual, valid, rows, branch_stat, gain1_grad, gain2_grad, by_distance, bucket_table
):
    length, width = residual.shape
    span = by_distance.shape[2]
    return pl.pallas_call(
        output_kernel,
        out_shape=(
            jax.ShapeDtypeStruct((length, width), BF16),
            jax.ShapeDtypeStruct((SHORT_ROWS, BLOCK), F32),
        ),
        scratch_shapes=[pltpu.VMEM((-(-HEADS // 8) * 8, span), F32)],
        compiler_params=params(),
        cost_estimate=cost(0.01),
        name="block_output",
    )(
        place_col, residual, valid.T, rows, branch_stat, gain1_grad, gain2_grad, by_distance,
        bucket_table[None, :span],
    )


def swap(values, axis, bit):
    size = lax.axis_size(axis)
    return lax.ppermute(values, axis, [(i, i ^ bit) for i in range(size)])


def axis_bits(axis):
    size = lax.axis_size(axis)
    bits = []
    bit = 1
    while bit < size:
        bits.append((axis, bit))
        bit *= 2
    return bits


def spread(parts):
    nearest = swap(parts[1], "expert", 1)
    far = [after(part, nearest) for part in parts[4:]]
    parts = parts[:4] + far
    return [parts[0], nearest] + [swap(parts[k], "expert", k) for k in range(2, len(parts))]


def relay(keep, away):
    arrived = swap(away, "expert", 1)
    keep = after(keep, arrived)
    found = []
    for j in range(keep.shape[0]):
        for part in (keep[j], arrived[j]):
            found.append(swap(part, "expert", 2 * j) if j else part)
    return found


def after(values, *others):
    return lax.optimization_barrier((values, others))[0]


def levels():
    groups, owners = lax.axis_size("dp"), lax.axis_size("expert")
    dp, expert = lax.axis_index("dp"), lax.axis_index("expert")
    axes = ("dp", "expert")

    def sender(width, fold):
        def send(values, k):
            def target(i):
                d, e = fold(i // owners, i % owners, k)
                return d * owners + e

            return lax.ppermute(values, axes, [(i, target(i)) for i in range(groups * owners)])

        return send

    return [
        (2, dp % 2, sender(2, lambda d, e, k: (d ^ k, e))),
        (
            groups,
            dp // 2 * 2 + expert % 2,
            sender(groups, lambda d, e, k: (d ^ (k // 2 * 2), e ^ (k % 2))),
        ),
        (owners // 2, expert // 2, sender(owners // 2, lambda d, e, k: (d, e ^ (2 * k)))),
    ]


def halve_kernel(place_ref, mine_ref, arrived_ref, *out_refs):
    rows = out_refs[0].shape[0]
    for k, out in enumerate(out_refs):
        here = pl.ds(pl.multiple_of((place_ref[0] ^ k) * rows, 16), rows)
        out[...] = (mine_ref[here, :].astype(F32) + arrived_ref[here, :].astype(F32)).astype(BF16)


def halve(place, mine, arrived, count):
    rows, width = mine.shape
    in_vmem = pl.BlockSpec(memory_space=pltpu.VMEM)
    return pl.pallas_call(
        halve_kernel,
        in_specs=[pl.BlockSpec(memory_space=pltpu.SMEM), in_vmem, in_vmem],
        out_shape=[jax.ShapeDtypeStruct((rows // count, width), BF16)] * count,
        compiler_params=params(),
        cost_estimate=cost(0.01),
        name="halve",
    )(place.astype(jnp.int32)[None], mine, arrived)


def sum_everywhere(mine, away, fillers):
    steps = levels()
    fillers = iter(fillers)

    def fill(terms, ready):
        found = [run(ready) for run in next(fillers, ())]
        return after(terms, *found) if found else terms

    _, _, send = steps[0]
    arrived = fill(send(away, 1), (mine, away))
    blocks = None
    for count, place, send in steps[1:]:
        if blocks is None:
            blocks = halve(place, mine, arrived, count)
        else:
            share = values.shape[0] // count
            blocks = [
                lax.dynamic_slice_in_dim(values, (place ^ k) * share, share, 0)
                for k in range(count)
            ]
        sent = fill([send(blocks[k], k) for k in range(1, count)], blocks)
        values = sum(t.astype(F32) for t in [blocks[0]] + sent).astype(BF16)
    for count, place, send in reversed(steps[1:]):
        share = values.shape[0]
        sent = fill([send(values, k) for k in range(1, count)], values)
        found = jnp.zeros((count * share, values.shape[1]), BF16)
        for k, piece in enumerate([values] + sent):
            found = lax.dynamic_update_slice_in_dim(found, piece, (place ^ k) * share, 0)
        values = found
    _, _, send = steps[0]
    other = fill(send(values, 1), values)
    for rest in fillers:
        for run in rest:
            run(values)
    return values, other


def widen_kernel(half_ref, rows_ref, *rest):
    qkv_ref, outw_ref = rest[-2:]
    j = pl.program_id(0)

    @pl.when(j < 3)
    def _():
        qkv_ref[...] = rows_ref[...].astype(F32)

    @pl.when(j == 3)
    def _():
        outw_ref[...] = rows_ref[...].astype(F32)


def widen(half, rows, width, old):
    taken = width // 2
    in_specs = [pl.BlockSpec((taken, width), lambda j, _: (j, 0))]
    arguments = (rows,)
    aliases = {}
    if old is not None:
        in_specs += [pl.BlockSpec(memory_space=pl.ANY)] * 2
        arguments += tuple(old)
        aliases = {2: 0, 3: 1}
    return pl.pallas_call(
        widen_kernel,
        grid_spec=pltpu.PrefetchScalarGridSpec(
            num_scalar_prefetch=1,
            grid=(4,),
            in_specs=in_specs,
            out_specs=[
                pl.BlockSpec((taken, width), lambda j, s: (s[0], jnp.minimum(j, 2))),
                pl.BlockSpec((taken, width), lambda j, s: (s[0], 0)),
            ],
        ),
        out_shape=(
            jax.ShapeDtypeStruct((width, 3 * width), F32),
            jax.ShapeDtypeStruct((width, width), F32),
        ),
        input_output_aliases=aliases,
        compiler_params=params(),
        cost_estimate=cost(4),
        name="widen",
    )(half, *arguments)


def sum_small(values):
    axes = ("dp", "expert")
    devices = lax.axis_size("dp") * lax.axis_size("expert")
    sent = jnp.broadcast_to(values[None], (devices,) + values.shape)
    return jnp.sum(lax.all_to_all(sent, axes, 0, 0, tiled=True), axis=0)


def on_device(
    hidden_in, doc_ids, valid_mask, expert_ids, bucket_table, norm1_gain, qkv_weight, position_bias,
    out_weight, norm2_gain, router_weight, up_weight, down_weight, out_grad,
):
    length, width = hidden_in.shape
    local = up_weight.shape[0]
    owners = lax.axis_size("expert")
    groups = lax.axis_size("dp")
    devices = owners * groups
    kinds = router_weight.shape[1]
    chunks = 2 if local % 4 == 0 else 1
    each = local // chunks
    half = owners // 2
    me = lax.axis_index("expert").astype(jnp.int32)
    group = lax.axis_index("dp").astype(jnp.int32)
    scalars = jnp.stack([me * local, me])
    group_scalars = jnp.stack([me * local, group])

    owner, inside = expert_ids // local, expert_ids % local
    far = owner ^ me
    chunk, within = inside // each, inside % each
    last = chunk == chunks - 1
    turned = far % 2 * half + far // 2
    send_ids = (chunk * owners + jnp.where(chunk == 0, turned, owner)) * each + within
    keep_ids = (chunk * owners + jnp.where(last, far, owner)) * each + within
    place_row, place_col, grad_rows = route(
        expert_ids, send_ids, keep_ids, out_grad, owners * local * CAP
    )
    to_owners = functools.partial(
        lax.all_to_all, axis_name="expert", split_axis=0, concat_axis=0, tiled=True
    )
    grads = to_owners(grad_rows.reshape(owners, local * CAP, width))
    size = owners * each * CAP
    probs, qkv, n1_t, ctx_t, residual, branch_stat, keep, away, *other = attention_forward(
        hidden_in, norm1_gain, qkv_weight, out_weight, norm2_gain, doc_ids, valid_mask,
        bucket_table, position_bias, place_row, (size // 2, size // 2) + (size,) * (chunks - 1),
    )
    shape = (half, each * CAP, width)
    rows = relay(keep.reshape(shape), away.reshape(shape))
    latest_rows = rows
    backs, router_parts = [], []
    carried = None
    side = first_side = active_grads(after(grads, rows[0]), down_weight, 0, each)
    for c in range(chunks):
        later = None
        if c + 1 < chunks:
            later = [to_owners(after(other[c], side, *rows).reshape(owners, each * CAP, width))]
        *back, rows_all, active, router_part = run_experts(
            rows, side, up_weight, router_weight, scalars, c * each, carried, c + 1 == chunks
        )
        carried = rows_all, active
        if c + 1 < chunks:
            backs.append(to_owners(back[0]))
            side = active_grads(after(grads, router_part), down_weight, (c + 1) * each, each)
        rows = later
        router_parts.append(router_part)
    last_backs = spread(back)
    outs = expert_outputs(after(active, back), down_weight)
    backs = after(backs + last_backs, outs)
    router_grad = functools.reduce(jnp.add, router_parts)
    backs = [b.reshape(-1, width) for b in backs]

    core = (group % 2)[None]
    unit_rows = 16 * groups * max(half // 16, 1)
    sum_rows = -(-(4 * width + kinds) // (2 * unit_rows)) * unit_rows
    gain2_grad, residual_grad, mine, away, ctx_grad = residual_backward(
        core, place_col, residual, norm2_gain, out_grad, out_weight, ctx_t, router_grad, backs,
        sum_rows,
    )
    dq, dk, dv, mine, away, by_distance = attention_backward(
        core, qkv, ctx_grad, probs, n1_t, mine, away
    )
    outs = to_owners(after(outs, *backs)).reshape(owners * local * CAP, width)
    rows_gathered = lax.all_gather(after(rows_all, last_backs[1]), "dp")
    grads_gathered = lax.all_gather(after(grads, first_side, *latest_rows), "dp")
    expert_grads = [None]

    def some_experts(first, count, ready):
        expert_grads[0] = expert_wgrads(
            rows_gathered, after(grads_gathered, ready), up_weight, down_weight, router_weight,
            group_scalars, first, count, expert_grads[0],
        )
        return expert_grads[0]

    results = {}

    def first_norm(ready):
        results["input"] = input_backward(
            hidden_in, norm1_gain, after(residual_grad, ready), qkv_weight, (dq, dk, dv)
        )
        return results["input"]

    def last_sum(ready):
        results["output"] = block_output(
            place_col, residual, valid_mask, after(outs, ready), branch_stat, results["input"][1],
            gain2_grad, by_distance, bucket_table,
        )
        return results["output"]

    def short_sums(ready):
        results["short"] = sum_small(results["output"][1])
        return [results["short"]]

    sizes = [local]
    if local % 8 == 0:
        sizes = [local // 2, 0, local // 8, local * 3 // 8]
    starts = [sum(sizes[:k]) for k in range(len(sizes))]
    experts = [
        [functools.partial(some_experts, at, size)] if size else []
        for at, size in zip(starts, sizes, strict=True)
    ]
    experts += [[]] * (4 - len(experts))
    fillers = [[first_norm], experts[0], [last_sum] + experts[1], [short_sums] + experts[2]]
    fillers += [experts[3]]
    mine, other = sum_everywhere(mine, away, fillers)
    block_out, input_grad = results["output"][0], results["input"][0]
    short = results["short"]
    gain_rows = width // BLOCK
    gain1_sum = short[:gain_rows].reshape(-1)
    gain2_sum = short[6 : 6 + gain_rows].reshape(-1)
    bias_sum = short[BIAS_ROW:].reshape(-1, NBUCKET)[:HEADS].T
    stat_sums = short[STAT_ROW]
    rms_stats = jnp.sqrt(stat_sums[:3] / (jnp.maximum(stat_sums[3], 1.0) * width))
    wide = widen(core, mine, width, None)
    qkv_sum, outw_sum = widen(1 - core, other, width, wide)
    used = slice(2 * width, 2 * width + kinds // 2)
    first = core[0] == 0
    router_sum = jnp.concatenate(
        [
            jnp.where(first, mine[used], other[used]),
            jnp.where(first, other[used], mine[used]),
        ]
    ).astype(F32)
    return (
        block_out,
        input_grad,
        gain1_sum,
        qkv_sum,
        bias_sum,
        outw_sum,
        gain2_sum,
        router_sum.T,
        *expert_grads[0],
        rms_stats,
    )


def solution(mesh):
    spread = P(("dp", "expert"), None)
    placed = (spread,) * 4 + (P(),) * 7 + (P("expert", None, None),) * 2 + (spread,)
    return jax.shard_map(
        on_device,
        mesh=mesh,
        in_specs=placed,
        out_specs=(spread, spread)
        + (P(),) * 6
        + (P("expert", None, "dp"), P("expert", "dp", None), P()),
        check_vma=False,
    )
```

```python
import functools

import jax
import jax.numpy as jnp
from jax import lax
from jax.experimental import pallas as pl
from jax.experimental.pallas import tpu as pltpu
from jax.sharding import PartitionSpec as P

HEADS = 12
HEAD_DIM = 64
NBUCKET = 32
CAP = 24
BLOCK = 128
WINDOW = 3
PAIR = 2 * HEAD_DIM
EPSILON = 1e-06
NEGATIVE = -1e30
HIGHEST = lax.Precision.HIGHEST
BF16 = jnp.bfloat16
F32 = jnp.float32
SUBSTEPS = 6
VMEM_LIMIT = 58 * 1024 * 1024


NN = (((1,), (0,)), ((), ()))
NT = (((1,), (1,)), ((), ()))
TN = (((0,), (0,)), ((), ()))


def dot(left, right, dims=NN, precision=None):
    return lax.dot_general(left, right, dims, precision=precision, preferred_element_type=F32)


def iota(shape, dim):
    return lax.broadcasted_iota(jnp.int32, shape, dim)


def whole(shape):
    return pl.BlockSpec(shape, lambda *_: (0,) * len(shape))


def params(**more):
    return pltpu.CompilerParams(vmem_limit_bytes=VMEM_LIMIT, **more)


def cost(microseconds):
    return pl.CostEstimate(
        flops=int(microseconds * 1.1e9), bytes_accessed=1000, transcendentals=0
    )


def windows(length):
    found = []
    row = 0
    for number in range(length // BLOCK):
        first = max(number - WINDOW + 1, 0)
        keys = (number - first + 1) * BLOCK
        found.append((number * BLOCK, first * BLOCK, keys, row))
        row += keys
    return found, row


def rms(values):
    return lax.rsqrt(jnp.mean(values * values, axis=-1, keepdims=True) + EPSILON)


def hot_columns(row0, row1, count, offset):
    slots = iota((count, row0.shape[1]), 0) + offset
    return jnp.where((slots == row0) | (slots == row1), 1.0, 0.0).astype(BF16)


def hot_rows(col0, col1, count, offset):
    slots = iota((col0.shape[0], count), 1) + offset
    return jnp.where((slots == col0) | (slots == col1), 1.0, 0.0).astype(BF16)


def id_parts(ids, local, each):
    inside = ids & (local - 1)
    return ids >> (local.bit_length() - 1), inside >> (each.bit_length() - 1), inside & (each - 1)


def route_kernel(me_ref, ids_ref, grad_ref, row_ref, rows_ref, *, local, each):
    length = grad_ref.shape[0]
    experts = rows_ref.shape[0] // CAP
    owners = experts // local
    before = iota((length, length), 0) < iota((length, length), 1)
    upper = jnp.where(before, 1.0, 0.0).astype(BF16)
    number = iota((experts, length), 0)
    hot = [number == ids_ref[c : c + 1, :] for c in range(2)]
    both = jnp.where(hot[0] | hot[1], 1.0, 0.0).astype(BF16)
    rank = dot(both, upper)
    rows = []
    for c in range(2):
        ids = ids_ref[c : c + 1, :]
        mine = jnp.sum(jnp.where(hot[c], rank, 0.0), axis=0, keepdims=True).astype(jnp.int32)
        rows.append(ids * CAP + mine)
        owner, chunk, within = id_parts(ids, local, each)
        far = owner ^ me_ref[0]
        turned = (far & 1) * (owners // 2) + (far >> 1)
        place = (chunk * owners + jnp.where(chunk == 0, turned, owner)) * each + within
        row_ref[c : c + 1, :] = place * CAP + mine
    chosen = hot_columns(rows[0], rows[1], rows_ref.shape[0], 0)
    rows_ref[...] = dot(chosen, grad_ref[...]).astype(BF16)


def route(ids, me, out_grad, slots, local, each):
    length, width = out_grad.shape
    in_vmem = pl.BlockSpec(memory_space=pltpu.VMEM)
    return pl.pallas_call(
        functools.partial(route_kernel, local=local, each=each),
        in_specs=[pl.BlockSpec(memory_space=pltpu.SMEM)] + [in_vmem] * 2,
        out_shape=(
            jax.ShapeDtypeStruct((2, length), jnp.int32),
            jax.ShapeDtypeStruct((slots, width), BF16),
        ),
        compiler_params=params(),
        cost_estimate=cost(5),
        name="route",
    )(me[None], ids.T, out_grad)


def return_places(ids_ref, me, col_ref, experts, local, each):
    length = ids_ref.shape[0]
    owners = experts // local
    after_it = iota((length, length), 0) > iota((length, length), 1)
    lower = jnp.where(after_it, 1.0, 0.0).astype(BF16)
    number = iota((length, experts), 1)
    hot = [number == ids_ref[:, c : c + 1] for c in range(2)]
    both = jnp.where(hot[0] | hot[1], 1.0, 0.0).astype(BF16)
    rank = dot(lower, both)
    for c in range(2):
        ids = ids_ref[:, c : c + 1]
        mine = jnp.sum(jnp.where(hot[c], rank, 0.0), axis=1, keepdims=True).astype(jnp.int32)
        owner, chunk, within = id_parts(ids, local, each)
        ends = chunk == local // each - 1
        place = (chunk * owners + jnp.where(ends, owner ^ me, owner)) * each + within
        col_ref[:, c : c + 1] = place * CAP + mine
        col_ref[:, 2 + c : 3 + c] = ids * CAP + mine


def forward_kernel(
    x_ref, gain1_ref, qkvw_ref, outw_ref, gain2_ref, docr_ref, docc_ref, validc_ref, bucket_ref,
    pbias_ref, row_ref, ids_ref, me_ref,
    probs_ref, qkv_ref, n1t_ref, ctx_ref, residual_ref, stat_ref, col_ref, *rest, local, each,
):
    rows_refs, (mask_s, bias_s, toeplitz_s) = rest[:-3], rest[-3:]
    pair = pl.program_id(0)
    length, width = x_ref.shape
    spans, _ = windows(length)

    @pl.when(pair == 0)
    def _():
        x = x_ref[...].astype(F32)
        n1 = (x * rms(x) * gain1_ref[...]).astype(BF16)
        n1t_ref[...] = n1.T
        for j in range(3):
            part = slice(j * width, (j + 1) * width)
            qkv_ref[:, part] = dot(n1, qkvw_ref[:, part]).astype(BF16)
        for q0, k0, keys, row in spans:
            shape = (keys, BLOCK)
            distance = (iota(shape, 1) + q0) - (iota(shape, 0) + k0)
            allowed = (
                (distance >= 0)
                & (docc_ref[k0 : k0 + keys, :] == docr_ref[:, q0 : q0 + BLOCK])
                & ((validc_ref[k0 : k0 + keys, :] == 1) | (distance == 0))
            )
            mask_s[row : row + keys, :] = jnp.where(allowed, 0.0, NEGATIVE)
        experts = sum(r.shape[0] for r in rows_refs) // CAP
        return_places(ids_ref, me_ref[0], col_ref, experts, local, each)
        span = bias_s.shape[1]
        hot = jnp.where(iota((NBUCKET, span), 0) == bucket_ref[...], 1.0, 0.0)
        bias_s[...] = dot(pbias_ref[...], hot, precision=HIGHEST)

    for side in range(2):
        head_bias = bias_s[pl.ds(2 * pair + side, 1), :]
        for m in range(WINDOW):
            ahead = head_bias[:, m * BLOCK : (m + 1) * BLOCK]
            back = max(m - 1, 0)
            behind = head_bias[:, back * BLOCK : (back + 1) * BLOCK]
            lanes = jnp.broadcast_to(
                jnp.concatenate([ahead, behind], axis=1), (BLOCK, 2 * BLOCK)
            )
            rolled = pltpu.roll(lanes, 0, 1, stride=1, stride_axis=0)
            place = (WINDOW - 1 - m) * BLOCK
            toeplitz_s[place : place + BLOCK, side * BLOCK : (side + 1) * BLOCK] = rolled[
                :, :BLOCK
            ]

    at = pl.multiple_of(pair * PAIR, PAIR)
    first_head = iota((BLOCK, PAIR), 1) < HEAD_DIM
    top = iota((PAIR, BLOCK), 0) < HEAD_DIM
    for q0, k0, keys, row in spans:
        q = qkv_ref[q0 : q0 + BLOCK, pl.ds(at, PAIR)].astype(F32) * HEAD_DIM ** (-0.5)
        stacked = jnp.concatenate(
            [jnp.where(first_head, q, 0.0), jnp.where(first_head, 0.0, q)], axis=0
        ).astype(BF16)
        k = qkv_ref[k0 : k0 + keys, pl.ds(pl.multiple_of(width + at, PAIR), PAIR)]
        v = qkv_ref[k0 : k0 + keys, pl.ds(pl.multiple_of(2 * width + at, PAIR), PAIR)]
        scores = dot(k, stacked, NT)
        masked = mask_s[row : row + keys, :]
        for side in range(2):
            lanes = slice(side * BLOCK, (side + 1) * BLOCK)
            s = scores[:, lanes] + toeplitz_s[WINDOW * BLOCK - keys :, lanes] + masked
            peak = jnp.max(s, axis=0, keepdims=True)
            e = jnp.exp(s - peak)
            total = jnp.sum(e, axis=0, keepdims=True)
            probs_ref[0, row : row + keys, lanes] = (e * (1.0 / total)).astype(BF16)
        both = dot(v, probs_ref[0, row : row + keys, :], TN)
        ctx = jnp.where(top, both[:, :BLOCK], both[:, BLOCK:])
        ctx_ref[pl.ds(at, PAIR), q0 : q0 + BLOCK] = ctx.astype(BF16)

    @pl.when(pair == pl.num_programs(0) - 1)
    def _():
        branch = dot(ctx_ref[...], outw_ref[...], TN)
        valid = validc_ref[...].astype(F32)
        stat_ref[...] = jnp.sum(valid * branch * branch, axis=0, keepdims=True)
        residual = x_ref[...].astype(F32) + branch
        residual_ref[...] = residual
        n2 = (residual * rms(residual) * gain2_ref[...]).astype(BF16)
        offset = 0
        for out in rows_refs:
            chosen = hot_columns(row_ref[0:1, :], row_ref[1:2, :], out.shape[0], offset)
            out[...] = dot(chosen, n2).astype(BF16)
            offset += out.shape[0]


def attention_forward(
    x, gain1, qkvw, outw, gain2, docs, valid, bucket_table, position_bias, place_row, ids, me,
    sizes, local, each,
):
    length, width = x.shape
    _, stored = windows(length)
    pairs = width // PAIR
    span = WINDOW * BLOCK
    padded_heads = -(-HEADS // 8) * 8
    bias_t = jnp.zeros((padded_heads, NBUCKET), F32).at[:HEADS].set(position_bias.T)
    arguments = (
        x, gain1[None], qkvw, outw, gain2[None], docs, docs.T, valid.T,
        bucket_table[None, :span], bias_t, place_row, ids,
    )
    out_shape = (
        jax.ShapeDtypeStruct((pairs, stored, 2 * BLOCK), BF16),
        jax.ShapeDtypeStruct((length, 3 * width), BF16),
        jax.ShapeDtypeStruct((width, length), BF16),
        jax.ShapeDtypeStruct((width, length), BF16),
        jax.ShapeDtypeStruct((length, width), F32),
        jax.ShapeDtypeStruct((1, width), F32),
        jax.ShapeDtypeStruct((length, 4), jnp.int32),
    ) + tuple(jax.ShapeDtypeStruct((n, width), BF16) for n in sizes)
    return pl.pallas_call(
        functools.partial(forward_kernel, local=local, each=each),
        grid=(pairs,),
        in_specs=[whole(a.shape) for a in arguments] + [pl.BlockSpec(memory_space=pltpu.SMEM)],
        out_specs=[pl.BlockSpec((1, stored, 2 * BLOCK), lambda p: (p, 0, 0))]
        + [whole(s.shape) for s in out_shape[1:]],
        out_shape=out_shape,
        scratch_shapes=[
            pltpu.VMEM((stored, BLOCK), F32),
            pltpu.VMEM((padded_heads, span), F32),
            pltpu.VMEM((span, 2 * BLOCK), F32),
        ],
        compiler_params=params(),
        cost_estimate=cost(22),
        name="attention_forward",
    )(*arguments, me[None])


def expert_gate(rows, router, expert):
    logits = dot(rows, router)
    shifted = jnp.exp(logits - jnp.max(logits, axis=-1, keepdims=True))
    probs = shifted / jnp.sum(shifted, axis=-1, keepdims=True)
    mine = iota(probs.shape, 1) == expert
    return probs, mine, jnp.sum(jnp.where(mine, probs, 0.0), axis=-1, keepdims=True)


GELU_SCALE = 0.7978845608028654
GELU_CUBE = 0.044715


def gelu_parts(v):
    square = v * v
    t = jnp.tanh(v * (GELU_SCALE + (GELU_SCALE * GELU_CUBE) * square))
    half = 0.5 * v
    value = half + half * t
    slope = 0.5 + 0.5 * t + half * (1.0 - t * t) * (
        GELU_SCALE + (3.0 * GELU_SCALE * GELU_CUBE) * square
    )
    return value, slope


def active_grad_kernel(grads_ref, down_ref, out_ref, g_s, grads_s, *, first):
    e, f = pl.program_id(0), pl.program_id(1)

    @pl.when((e == 0) & (f == 0))
    def _():
        grads_s[...] = grads_ref[...].astype(F32)

    @pl.when(f == 0)
    def _():
        here = pl.ds(pl.multiple_of((first + e) * CAP, CAP), CAP)
        g_s[...] = grads_s[:, here, :].reshape(g_s.shape).astype(BF16)

    out_ref[0] = dot(g_s[...], down_ref[0], NT).astype(BF16)


def active_grads(grads, down_weight, first, experts, blocks=1):
    owners, _, width = grads.shape
    inner = down_weight.shape[1]
    step, count = inner // blocks, owners * CAP
    return pl.pallas_call(
        functools.partial(active_grad_kernel, first=first),
        grid=(experts, blocks),
        in_specs=[
            whole(grads.shape),
            pl.BlockSpec((1, step, width), lambda e, f: (first + e, f, 0)),
        ],
        out_specs=pl.BlockSpec((1, count, step), lambda e, f: (e, 0, f)),
        out_shape=jax.ShapeDtypeStruct((experts, count, inner), BF16),
        scratch_shapes=[pltpu.VMEM((count, width), BF16), pltpu.VMEM(grads.shape, F32)],
        compiler_params=params(),
        cost_estimate=cost(0.01),
        name="active_grads",
    )(grads, down_weight)


def expert_kernel(scalar_ref, *refs, parts, aliased, last):
    rows_refs, refs = refs[:parts], refs[parts:]
    side_ref, up_ref, router_ref = refs[:3]
    refs = refs[3 + aliased :]
    backs = max(last, 1)
    back_refs, refs = refs[:backs], refs[backs:]
    all_ref, active_ref, router_grad_ref = refs[:3]
    rows_s, back_s, x_s, probs_s, gate_s, sum_s, dx_s, grad_s = refs[3:]
    e, f = pl.program_id(0), pl.program_id(1)
    experts, blocks = pl.num_programs(0), pl.num_programs(1)
    me = scalar_ref[1]
    expert = scalar_ref[0] + e
    count, width = x_s.shape
    owners = rows_s.shape[0]
    here = pl.ds(pl.multiple_of(e * CAP, CAP), CAP)

    @pl.when((e == 0) & (f == 0))
    def _():
        if parts == 1:
            all_ref[0] = rows_refs[0][...]
            rows_s[...] = rows_refs[0][...].astype(F32)
        else:
            for k in range(parts):
                all_ref[0, me ^ k] = rows_refs[k][...]
                rows_s[me ^ k] = rows_refs[k][...].astype(F32)
        router_grad_ref[...] = jnp.zeros_like(router_grad_ref)

    @pl.when(f == 0)
    def _():
        x = rows_s[:, here, :].reshape(count, width).astype(BF16)
        x_s[...] = x
        probs, _, gate = expert_gate(x, router_ref[...], expert)
        probs_s[...] = probs
        gate_s[...] = jnp.broadcast_to(gate, gate_s.shape)
        sum_s[...] = jnp.zeros_like(sum_s)
        dx_s[...] = jnp.zeros_like(dx_s)

    gate = gate_s[:, :1]
    x = x_s[...]
    step = up_ref.shape[2] // SUBSTEPS
    total = None
    inner = dot(x, up_ref[0, :, :step])
    for s in range(SUBSTEPS):
        here_f = slice(s * step, (s + 1) * step)
        later = dot(x, up_ref[0, :, (s + 1) * step : (s + 2) * step]) if s + 1 < SUBSTEPS else None
        value, slope = gelu_parts(inner)
        side = side_ref[0, :, here_f].astype(F32) * gate
        part = jnp.sum(value * side, axis=-1, keepdims=True)
        total = part if total is None else total + part
        active_ref[0, :, here_f] = (gate * value).astype(BF16)
        grad_s[:, here_f] = (side * slope).astype(BF16)
        inner = later
    sum_s[...] += total
    dx_s[...] += dot(grad_s[...], up_ref[0], NT)

    @pl.when(f == blocks - 1)
    def _():
        probs = probs_s[...]
        mine = iota(probs.shape, 1) == expert
        logit_grad = (sum_s[:, :1] * (jnp.where(mine, 1.0, 0.0) - probs)).astype(BF16)
        router_grad_ref[...] += dot(logit_grad, x_s[...], TN)
        dx = dx_s[...] + dot(logit_grad, router_ref[...], NT)
        back_s[:, here, :] = dx.reshape(owners, CAP, width)

    @pl.when((e == experts - 1) & (f == blocks - 1))
    def _():
        if last:
            for k in range(owners):
                back_refs[k][...] = back_s[me ^ k].astype(BF16)
        else:
            back_refs[0][...] = back_s[...].astype(BF16)


def run_experts(
    rows, side, up_weight, router, scalars, first, old, last
):
    parts = len(rows)
    slots, width = rows[0].shape[-2:]
    owners = parts if parts > 1 else rows[0].shape[0]
    experts = slots // CAP
    local, _, inner = up_weight.shape
    count, kinds = owners * CAP, router.shape[1]
    blocks = 1 if count <= 256 else 3
    step = inner // blocks
    backs = [jax.ShapeDtypeStruct((owners, slots, width), BF16)]
    if last:
        backs = [jax.ShapeDtypeStruct((slots, width), BF16)] * owners
    in_specs = [whole(r.shape) for r in rows] + [
        pl.BlockSpec((1, count, step), lambda e, f, _: (e, 0, f)),
        pl.BlockSpec((1, width, step), lambda e, f, _: (first + e, 0, f)),
        whole(router.shape),
    ]
    arguments = (*rows, side, up_weight, router)
    aliases = {}
    if old is not None:
        aliases = {1 + len(arguments) + k: len(backs) + k for k in range(2)}
        in_specs += [pl.BlockSpec(memory_space=pl.ANY)] * 2
        arguments += tuple(old)
    return pl.pallas_call(
        functools.partial(expert_kernel, parts=parts, aliased=len(aliases), last=owners if last else 0),
        grid_spec=pltpu.PrefetchScalarGridSpec(
            num_scalar_prefetch=1,
            grid=(experts, blocks),
            in_specs=in_specs,
            out_specs=[whole(back.shape) for back in backs]
            + [
                pl.BlockSpec((1, owners, slots, width), lambda e, f, _: (first // experts, 0, 0, 0)),
                pl.BlockSpec((1, count, step), lambda e, f, _: (first + e, 0, f)),
                whole((kinds, width)),
            ],
            scratch_shapes=[
                pltpu.VMEM((owners, slots, width), F32),
                pltpu.VMEM((owners, slots, width), F32),
                pltpu.VMEM((count, width), BF16),
                pltpu.VMEM((count, kinds), F32),
                pltpu.VMEM((count, BLOCK), F32),
                pltpu.VMEM((count, BLOCK), F32),
                pltpu.VMEM((count, width), F32),
                pltpu.VMEM((count, step), BF16),
            ],
        ),
        out_shape=(
            *backs,
            jax.ShapeDtypeStruct((local // experts, owners, slots, width), BF16),
            jax.ShapeDtypeStruct((local, count, inner), BF16),
            jax.ShapeDtypeStruct((kinds, width), F32),
        ),
        input_output_aliases=aliases,
        compiler_params=params(),
        cost_estimate=cost(22),
        name="experts",
    )(scalars + jnp.array([first, 0], jnp.int32), *arguments)


def expert_out_kernel(active_ref, down_ref, out_ref, sum_s, all_s):
    e, f = pl.program_id(0), pl.program_id(1)
    experts, blocks = pl.num_programs(0), pl.num_programs(1)
    part = dot(active_ref[0], down_ref[0])

    @pl.when(f == 0)
    def _():
        sum_s[...] = part

    @pl.when(f > 0)
    def _():
        sum_s[...] += part

    @pl.when(f == blocks - 1)
    def _():
        here = pl.ds(pl.multiple_of(e * CAP, CAP), CAP)
        all_s[:, here, :] = sum_s[...].reshape(all_s.shape[0], CAP, all_s.shape[2])

    @pl.when((e == experts - 1) & (f == blocks - 1))
    def _():
        out_ref[...] = all_s[...].astype(BF16)


def expert_outputs(active, down_weight, blocks=1):
    experts, count, inner = active.shape
    width = down_weight.shape[2]
    step, owners = inner // blocks, count // CAP
    shape = (owners, experts * CAP, width)
    return pl.pallas_call(
        expert_out_kernel,
        grid=(experts, blocks),
        in_specs=[
            pl.BlockSpec((1, count, step), lambda e, f: (e, 0, f)),
            pl.BlockSpec((1, step, width), lambda e, f: (e, f, 0)),
        ],
        out_specs=whole(shape),
        out_shape=jax.ShapeDtypeStruct(shape, BF16),
        scratch_shapes=[pltpu.VMEM((count, width), F32), pltpu.VMEM(shape, F32)],
        compiler_params=params(),
        cost_estimate=cost(0.01),
        name="expert_outputs",
    )(active, down_weight)


def expert_wgrad_kernel(
    scalar_ref, rows_ref, grads_ref, up_ref, down_ref, router_ref, *rest, first
):
    up_out, down_out, x_s, g_s = rest[-4:]
    expert, tile = first + pl.program_id(0), pl.program_id(1)
    count, width = x_s.shape
    for side in range(2):

        @pl.when(expert % 2 == side)
        def _():
            part = slice(side * CAP, (side + 1) * CAP)
            x = rows_ref[...].astype(F32)[:, 0, :, part, :].reshape(count, width).astype(BF16)
            x_s[...] = x
            _, _, gate = expert_gate(x, router_ref[...], scalar_ref[0] + expert)
            g = grads_ref[...].astype(F32)[:, :, part, :].reshape(count, width)
            g_s[...] = (gate * g).astype(BF16)

    x, g = x_s[...], g_s[...]
    value, slope = gelu_parts(dot(x, up_ref[0]))
    inner_grad = (dot(g, down_ref[0], NT) * slope).astype(BF16)

    @pl.when(tile == 0)
    def _():
        down_out[0] = dot(value.astype(BF16), g, TN)
        up_out[0] = dot(x, inner_grad, TN)

    @pl.when(tile > 0)
    def _():
        down_out[0] += dot(value.astype(BF16), g, TN)
        up_out[0] += dot(x, inner_grad, TN)


def expert_wgrads(rows, grads, up_weight, down_weight, router, scalars, first, experts, old):
    groups, chunks, owners, _, width = rows.shape
    local, _, inner = up_weight.shape
    each = local // chunks
    share = inner // groups
    taken = max(min(groups, 32 // owners), 1)
    count = taken * owners * CAP

    def rows_at(e, t, _):
        return (t, (first + e) // each, 0, (first + e) % each // 2, 0)

    in_specs = [
        pl.BlockSpec((taken, 1, owners, 2 * CAP, width), rows_at),
        pl.BlockSpec((taken, owners, 2 * CAP, width), lambda e, t, _: (t, 0, (first + e) // 2, 0)),
        pl.BlockSpec((1, width, share), lambda e, t, s: (first + e, 0, s[1])),
        pl.BlockSpec((1, share, width), lambda e, t, s: (first + e, s[1], 0)),
        whole(router.shape),
    ]
    arguments = (rows, grads, up_weight, down_weight, router)
    aliases = {}
    if old is not None:
        aliases = {6: 0, 7: 1}
        in_specs += [pl.BlockSpec(memory_space=pl.ANY)] * 2
        arguments += tuple(old)
    return pl.pallas_call(
        functools.partial(expert_wgrad_kernel, first=first),
        grid_spec=pltpu.PrefetchScalarGridSpec(
            num_scalar_prefetch=1,
            grid=(experts, groups // taken),
            in_specs=in_specs,
            out_specs=[
                pl.BlockSpec((1, width, share), lambda j, t, _: (first + j, 0, 0)),
                pl.BlockSpec((1, share, width), lambda j, t, _: (first + j, 0, 0)),
            ],
            scratch_shapes=[
                pltpu.VMEM((count, width), BF16),
                pltpu.VMEM((count, width), BF16),
            ],
        ),
        out_shape=(
            jax.ShapeDtypeStruct((local, width, share), F32),
            jax.ShapeDtypeStruct((local, share, width), F32),
        ),
        input_output_aliases=aliases,
        compiler_params=params(),
        cost_estimate=cost(0.01),
        name="expert_wgrads",
    )(scalars, *arguments)


def residual_kernel(
    half_ref, col_ref, residual_ref, gain_ref, grad_ref, outw_ref, ctx_ref, router_ref, *rest
):
    back_refs, rest = rest[:-8], rest[-8:]
    gain_grad_ref, residual_grad_ref, mine_ref, away_ref, ctx_grad_ref, early_s, sem0, sem1 = rest
    whole_backs = back_refs[0][...]
    if len(back_refs) > 1:
        whole_backs = jnp.concatenate([back[...] for back in back_refs], axis=0)
    chosen = hot_rows(col_ref[:, 0:1], col_ref[:, 1:2], whole_backs.shape[0], 0)
    n2_grad = dot(chosen, whole_backs)
    residual = residual_ref[...]
    factor = rms(residual)
    unit = residual * factor
    gain_grad_ref[...] = jnp.sum(n2_grad * unit, axis=0, keepdims=True)
    scaled = n2_grad * gain_ref[...]
    centre = jnp.mean(scaled * unit, axis=-1, keepdims=True)
    residual_grad = grad_ref[...].astype(F32) + factor * (scaled - unit * centre)
    residual_grad_ref[...] = residual_grad
    branch_grad = residual_grad.astype(BF16)
    width, kinds = ctx_ref.shape[0], router_ref.shape[0]
    rows = early_s.shape[1]
    used = (width + kinds) // 2
    copies = []
    for k, (out, sem) in enumerate(((mine_ref, sem0), (away_ref, sem1))):
        part = half_ref[0] ^ k
        ctx = ctx_ref[pl.ds(pl.multiple_of(part * (width // 2), width // 2), width // 2), :]
        early_s[k, : width // 2, :] = dot(ctx, branch_grad).astype(BF16)
        router = router_ref[pl.ds(pl.multiple_of(part * (kinds // 2), kinds // 2), kinds // 2), :]
        early_s[k, width // 2 : used, :] = router.astype(BF16)
        if used < rows:
            early_s[k, used:, :] = jnp.zeros((rows - used, width), BF16)
        copies.append(
            pltpu.make_async_copy(early_s.at[k], out.at[pl.ds(3 * width // 2, rows)], sem)
        )
        copies[k].start()
    ctx_grad_ref[...] = dot(branch_grad, outw_ref[...], NT).astype(BF16)
    for copy in copies:
        copy.wait()


def residual_backward(
    half, place_col, residual, gain2, out_grad, outw, ctx_t, router_grad, backs, rows
):
    length, width = residual.shape
    early = rows - 3 * width // 2
    in_vmem = pl.BlockSpec(memory_space=pltpu.VMEM)
    anywhere = pl.BlockSpec(memory_space=pl.ANY)
    buffer = jax.ShapeDtypeStruct((rows, width), BF16)
    return pl.pallas_call(
        residual_kernel,
        in_specs=[pl.BlockSpec(memory_space=pltpu.SMEM)] + [in_vmem] * (7 + len(backs)),
        out_specs=[in_vmem, in_vmem, anywhere, anywhere, in_vmem],
        out_shape=(
            jax.ShapeDtypeStruct((1, width), F32),
            jax.ShapeDtypeStruct((length, width), F32),
            buffer,
            buffer,
            jax.ShapeDtypeStruct((length, width), BF16),
        ),
        scratch_shapes=[
            pltpu.VMEM((2, early, width), BF16),
            pltpu.SemaphoreType.DMA,
            pltpu.SemaphoreType.DMA,
        ],
        compiler_params=params(),
        cost_estimate=cost(0.01),
        name="residual_backward",
    )(half, place_col, residual, gain2[None], out_grad, outw, ctx_t, router_grad, *backs)


def attention_backward_kernel(
    half_ref, q_ref, k_ref, v_ref, dctx_ref, probs_ref, n1t_ref, _, __,
    dq_ref, dk_ref, dv_ref, mine_ref, away_ref, bias_ref,
    dqt_s, dk_s, dv_s, diagonal_s,
):
    length = q_ref.shape[0]
    spans, _ = windows(length)
    first_head = iota((BLOCK, PAIR), 1) < HEAD_DIM
    top = iota((PAIR, BLOCK), 0) < HEAD_DIM
    scale = HEAD_DIM ** (-0.5)
    dk_s[...] = jnp.zeros_like(dk_s)
    dv_s[...] = jnp.zeros_like(dv_s)
    diagonal_s[...] = jnp.zeros_like(diagonal_s)

    def stack(values):
        values = values.astype(F32)
        return jnp.concatenate(
            [jnp.where(first_head, values, 0.0), jnp.where(first_head, 0.0, values)], axis=0
        ).astype(BF16)

    for q0, k0, keys, row in spans:
        q = stack(q_ref[q0 : q0 + BLOCK, :])
        dctx = stack(dctx_ref[q0 : q0 + BLOCK, :])
        span = slice(k0, k0 + keys)
        probs = probs_ref[0, row : row + keys, :]
        prob_side = dot(v_ref[span, :], dctx, NT)
        halves = []
        for side in range(2):
            lanes = slice(side * BLOCK, (side + 1) * BLOCK)
            p = probs[:, lanes].astype(F32)
            d = prob_side[:, lanes]
            centre = jnp.sum(p * d, axis=0, keepdims=True)
            s = p * (d - centre)
            diagonal_s[WINDOW * BLOCK - keys :, lanes] += s
            halves.append(s.astype(BF16))
        score_grad = jnp.concatenate(halves, axis=1)
        dk_s[span, :] += dot(score_grad, q)
        dv_s[span, :] += dot(probs, dctx)
        both = dot(k_ref[span, :], score_grad, TN)
        dqt_s[:, q0 : q0 + BLOCK] = jnp.where(top, both[:, :BLOCK], both[:, BLOCK:])
    dq = (dqt_s[...].T * scale).astype(BF16)
    dk = (dk_s[...] * scale).astype(BF16)
    dv = dv_s[...].astype(BF16)
    dq_ref[...] = dq
    dk_ref[...] = dk
    dv_ref[...] = dv
    width = n1t_ref.shape[0]
    for k, out in enumerate((mine_ref, away_ref)):
        part = pl.multiple_of((half_ref[0] ^ k) * (width // 2), width // 2)
        n1t = n1t_ref[pl.ds(part, width // 2), :]
        two = dot(n1t, jnp.concatenate([dq, dk], axis=1))
        out[: width // 2, :] = two[:, :PAIR].astype(BF16)
        out[width // 2 : width, :] = two[:, PAIR:].astype(BF16)
        out[width:, :] = dot(n1t, dv).astype(BF16)
    bias_ref[...] = jnp.zeros_like(bias_ref)
    for side in range(2):
        lanes = slice(side * BLOCK, (side + 1) * BLOCK)
        pieces = []
        for m in range(WINDOW):
            place = (WINDOW - 1 - m) * BLOCK
            block = diagonal_s[place : place + BLOCK, lanes]
            skewed = jnp.zeros((8, 2 * BLOCK), F32)
            for k in range(0, BLOCK, 8):
                eight = block[k : k + 8, :]
                wide = jnp.concatenate([eight, jnp.zeros_like(eight)], axis=1)
                skewed += wide if k == 0 else pltpu.roll(wide, 2 * BLOCK - k, 1)
            for bit in (1, 2, 4):
                moved = pltpu.roll(skewed, 2 * BLOCK - bit, 1)
                skewed = jnp.where(iota(skewed.shape, 0) & bit != 0, moved, skewed)
            pieces.append(jnp.sum(skewed, axis=0, keepdims=True))
        for m in range(WINDOW):
            total = pieces[m][:, :BLOCK]
            if m + 1 < WINDOW:
                total = total + pieces[m + 1][:, BLOCK:]
            bias_ref[0, side : side + 1, m * BLOCK : (m + 1) * BLOCK] = total


def attention_backward(half, qkv, ctx_grad, probs, n1_t, mine, away):
    length, width = ctx_grad.shape
    stored = probs.shape[1]
    pairs = width // PAIR
    span = WINDOW * BLOCK
    column = pl.BlockSpec((length, PAIR), lambda p, _: (0, p))
    summed = pl.BlockSpec((3 * width // 2, PAIR), lambda p, _: (0, p))
    anywhere = pl.BlockSpec(memory_space=pl.ANY)
    rows = jax.ShapeDtypeStruct((length, width), BF16)
    return pl.pallas_call(
        attention_backward_kernel,
        grid_spec=pltpu.PrefetchScalarGridSpec(
            num_scalar_prefetch=1,
            grid=(pairs,),
            in_specs=[
                column,
                pl.BlockSpec((length, PAIR), lambda p, _: (0, pairs + p)),
                pl.BlockSpec((length, PAIR), lambda p, _: (0, 2 * pairs + p)),
                column,
                pl.BlockSpec((1, stored, 2 * BLOCK), lambda p, _: (p, 0, 0)),
                whole(n1_t.shape),
                anywhere,
                anywhere,
            ],
            out_specs=[
                column,
                column,
                column,
                summed,
                summed,
                pl.BlockSpec((1, 8, span), lambda p, _: (p, 0, 0)),
            ],
            scratch_shapes=[
                pltpu.VMEM((PAIR, length), F32),
                pltpu.VMEM((length, PAIR), F32),
                pltpu.VMEM((length, PAIR), F32),
                pltpu.VMEM((span, 2 * BLOCK), F32),
            ],
        ),
        out_shape=(
            rows,
            rows,
            rows,
            jax.ShapeDtypeStruct(mine.shape, BF16),
            jax.ShapeDtypeStruct(away.shape, BF16),
            jax.ShapeDtypeStruct((pairs, 8, span), F32),
        ),
        input_output_aliases={7: 3, 8: 4},
        compiler_params=params(),
        cost_estimate=cost(96),
        name="attention_backward",
    )(half, qkv, qkv, qkv, ctx_grad, probs, n1_t, mine, away)


def input_kernel(x_ref, gain_ref, residual_grad_ref, qkvw_ref, *rest):
    parts, (grad_ref, gain_grad_ref) = rest[:-2], rest[-2:]
    x = x_ref[...].astype(F32)
    factor = rms(x)
    unit = x * factor
    n1_grad = None
    at = 0
    for part in parts:
        columns = part.shape[1]
        term = dot(part[...], qkvw_ref[:, at : at + columns], NT)
        n1_grad = term if n1_grad is None else n1_grad + term
        at += columns
    gain_grad_ref[...] = jnp.sum(n1_grad * unit, axis=0, keepdims=True)
    scaled = n1_grad * gain_ref[...]
    centre = jnp.mean(scaled * unit, axis=-1, keepdims=True)
    grad_ref[...] = (residual_grad_ref[...] + factor * (scaled - unit * centre)).astype(BF16)


def input_backward(x, gain1, residual_grad, qkvw, parts):
    length, width = x.shape
    return pl.pallas_call(
        input_kernel,
        out_shape=(
            jax.ShapeDtypeStruct((length, width), BF16),
            jax.ShapeDtypeStruct((1, width), F32),
        ),
        compiler_params=params(),
        cost_estimate=cost(0.01),
        name="input_backward",
    )(x, gain1[None], residual_grad, qkvw, *parts)


SHORT_ROWS = 16
STAT_ROW = 12
BIAS_ROW = 13


def output_kernel(
    col_ref, residual_ref, validc_ref, rows_ref, stat_ref, gain1_ref, gain2_ref, by_ref, bucket_ref,
    block_ref, short_ref, distance_s,
):
    chosen = hot_rows(col_ref[:, 2:3], col_ref[:, 3:4], rows_ref.shape[0], 0)
    mixture = dot(chosen, rows_ref[...])
    output = residual_ref[...] + mixture
    block_ref[...] = output.astype(BF16)
    valid = validc_ref[...].astype(F32)
    short_ref[...] = jnp.zeros_like(short_ref)
    for k in range(gain1_ref.shape[1] // BLOCK):
        lanes = slice(k * BLOCK, (k + 1) * BLOCK)
        short_ref[k : k + 1, :] = gain1_ref[:, lanes]
        short_ref[6 + k : 7 + k, :] = gain2_ref[:, lanes]
    lane = iota((1, BLOCK), 1)
    stats = jnp.where(lane == 0, jnp.sum(valid * output * output), 0.0)
    stats = jnp.where(lane == 1, jnp.sum(stat_ref[...]), stats)
    stats = jnp.where(lane == 2, jnp.sum(valid * mixture * mixture), stats)
    short_ref[STAT_ROW : STAT_ROW + 1, :] = jnp.where(lane == 3, jnp.sum(valid), stats)
    distance_s[...] = jnp.zeros_like(distance_s)
    for head in range(HEADS):
        distance_s[head : head + 1, :] = by_ref[head // 2, head % 2 : head % 2 + 1, :]
    buckets = iota((BLOCK, distance_s.shape[1]), 0) & (NBUCKET - 1)
    hot = jnp.where(buckets == bucket_ref[...], 1.0, 0.0)
    sums = dot(distance_s[...], hot, NT, HIGHEST)
    packed = BLOCK // NBUCKET
    own = iota(sums.shape, 1) // NBUCKET == iota(sums.shape, 0) % packed
    sums = jnp.where(own, sums, 0.0)
    for k in range(HEADS // packed):
        rows = sums[k * packed : (k + 1) * packed, :]
        short_ref[BIAS_ROW + k : BIAS_ROW + k + 1, :] = jnp.sum(rows, axis=0, keepdims=True)


def block_output(
    place_col, residual, valid, rows, branch_stat, gain1_grad, gain2_grad, by_distance, bucket_table
):
    length, width = residual.shape
    span = by_distance.shape[2]
    return pl.pallas_call(
        output_kernel,
        out_shape=(
            jax.ShapeDtypeStruct((length, width), BF16),
            jax.ShapeDtypeStruct((SHORT_ROWS, BLOCK), F32),
        ),
        scratch_shapes=[pltpu.VMEM((-(-HEADS // 8) * 8, span), F32)],
        compiler_params=params(),
        cost_estimate=cost(0.01),
        name="block_output",
    )(
        place_col, residual, valid.T, rows, branch_stat, gain1_grad, gain2_grad, by_distance,
        bucket_table[None, :span],
    )


def swap(values, axis, bit):
    size = lax.axis_size(axis)
    return lax.ppermute(values, axis, [(i, i ^ bit) for i in range(size)])


def axis_bits(axis):
    size = lax.axis_size(axis)
    bits = []
    bit = 1
    while bit < size:
        bits.append((axis, bit))
        bit *= 2
    return bits


def spread(parts):
    nearest = swap(parts[1], "expert", 1)
    far = [after(part, nearest) for part in parts[4:]]
    parts = parts[:4] + far
    return [parts[0], nearest] + [swap(parts[k], "expert", k) for k in range(2, len(parts))]


def relay(keep, away):
    arrived = swap(away, "expert", 1)
    keep = after(keep, arrived)
    found = []
    for j in range(keep.shape[0]):
        for part in (keep[j], arrived[j]):
            found.append(swap(part, "expert", 2 * j) if j else part)
    return found


def after(values, *others):
    return lax.optimization_barrier((values, others))[0]


def levels():
    groups, owners = lax.axis_size("dp"), lax.axis_size("expert")
    dp, expert = lax.axis_index("dp"), lax.axis_index("expert")
    axes = ("dp", "expert")

    def sender(width, fold):
        def send(values, k):
            def target(i):
                d, e = fold(i // owners, i % owners, k)
                return d * owners + e

            return lax.ppermute(values, axes, [(i, target(i)) for i in range(groups * owners)])

        return send

    return [
        (2, dp % 2, sender(2, lambda d, e, k: (d ^ k, e))),
        (
            groups,
            dp // 2 * 2 + expert % 2,
            sender(groups, lambda d, e, k: (d ^ (k // 2 * 2), e ^ (k % 2))),
        ),
        (owners // 2, expert // 2, sender(owners // 2, lambda d, e, k: (d, e ^ (2 * k)))),
    ]


def halve_kernel(place_ref, mine_ref, arrived_ref, *out_refs):
    rows = out_refs[0].shape[0]
    for k, out in enumerate(out_refs):
        here = pl.ds(pl.multiple_of((place_ref[0] ^ k) * rows, 16), rows)
        out[...] = (mine_ref[here, :].astype(F32) + arrived_ref[here, :].astype(F32)).astype(BF16)


def halve(place, mine, arrived, count):
    rows, width = mine.shape
    in_vmem = pl.BlockSpec(memory_space=pltpu.VMEM)
    return pl.pallas_call(
        halve_kernel,
        in_specs=[pl.BlockSpec(memory_space=pltpu.SMEM), in_vmem, in_vmem],
        out_shape=[jax.ShapeDtypeStruct((rows // count, width), BF16)] * count,
        compiler_params=params(),
        cost_estimate=cost(0.01),
        name="halve",
    )(place.astype(jnp.int32)[None], mine, arrived)


def sum_everywhere(mine, away, fillers):
    steps = levels()
    fillers = iter(fillers)

    def fill(terms, ready):
        found = [run(ready) for run in next(fillers, ())]
        return after(terms, *found) if found else terms

    _, _, send = steps[0]
    arrived = fill(send(away, 1), (mine, away))
    blocks = None
    for count, place, send in steps[1:]:
        if blocks is None:
            blocks = halve(place, mine, arrived, count)
        else:
            share = values.shape[0] // count
            blocks = [
                lax.dynamic_slice_in_dim(values, (place ^ k) * share, share, 0)
                for k in range(count)
            ]
        sent = fill([send(blocks[k], k) for k in range(1, count)], blocks)
        values = sum(t.astype(F32) for t in [blocks[0]] + sent).astype(BF16)
    for count, place, send in reversed(steps[1:]):
        share = values.shape[0]
        sent = fill([send(values, k) for k in range(1, count)], values)
        found = jnp.zeros((count * share, values.shape[1]), BF16)
        for k, piece in enumerate([values] + sent):
            found = lax.dynamic_update_slice_in_dim(found, piece, (place ^ k) * share, 0)
        values = found
    _, _, send = steps[0]
    other = fill(send(values, 1), values)
    for rest in fillers:
        for run in rest:
            run(values)
    return values, other


def widen_kernel(half_ref, rows_ref, *rest):
    qkv_ref, outw_ref = rest[-2:]
    j = pl.program_id(0)

    @pl.when(j < 3)
    def _():
        qkv_ref[...] = rows_ref[...].astype(F32)

    @pl.when(j == 3)
    def _():
        outw_ref[...] = rows_ref[...].astype(F32)


def widen(half, rows, width, old):
    taken = width // 2
    in_specs = [pl.BlockSpec((taken, width), lambda j, _: (j, 0))]
    arguments = (rows,)
    aliases = {}
    if old is not None:
        in_specs += [pl.BlockSpec(memory_space=pl.ANY)] * 2
        arguments += tuple(old)
        aliases = {2: 0, 3: 1}
    return pl.pallas_call(
        widen_kernel,
        grid_spec=pltpu.PrefetchScalarGridSpec(
            num_scalar_prefetch=1,
            grid=(4,),
            in_specs=in_specs,
            out_specs=[
                pl.BlockSpec((taken, width), lambda j, s: (s[0], jnp.minimum(j, 2))),
                pl.BlockSpec((taken, width), lambda j, s: (s[0], 0)),
            ],
        ),
        out_shape=(
            jax.ShapeDtypeStruct((width, 3 * width), F32),
            jax.ShapeDtypeStruct((width, width), F32),
        ),
        input_output_aliases=aliases,
        compiler_params=params(),
        cost_estimate=cost(4),
        name="widen",
    )(half, *arguments)


def sum_small(values):
    axes = ("dp", "expert")
    devices = lax.axis_size("dp") * lax.axis_size("expert")
    sent = jnp.broadcast_to(values[None], (devices,) + values.shape)
    return jnp.sum(lax.all_to_all(sent, axes, 0, 0, tiled=True), axis=0)


def on_device(
    hidden_in, doc_ids, valid_mask, expert_ids, bucket_table, norm1_gain, qkv_weight, position_bias,
    out_weight, norm2_gain, router_weight, up_weight, down_weight, out_grad,
):
    length, width = hidden_in.shape
    local = up_weight.shape[0]
    owners = lax.axis_size("expert")
    groups = lax.axis_size("dp")
    devices = owners * groups
    kinds = router_weight.shape[1]
    chunks = 2 if local % 4 == 0 else 1
    each = local // chunks
    half = owners // 2
    me = lax.axis_index("expert").astype(jnp.int32)
    group = lax.axis_index("dp").astype(jnp.int32)
    scalars = jnp.stack([me * local, me])
    group_scalars = jnp.stack([me * local, group])

    place_row, grad_rows = route(expert_ids, me, out_grad, owners * local * CAP, local, each)
    to_owners = functools.partial(
        lax.all_to_all, axis_name="expert", split_axis=0, concat_axis=0, tiled=True
    )
    grads = to_owners(grad_rows.reshape(owners, local * CAP, width))
    size = owners * each * CAP
    probs, qkv, n1_t, ctx_t, residual, branch_stat, place_col, keep, away, *other = attention_forward(
        hidden_in, norm1_gain, qkv_weight, out_weight, norm2_gain, doc_ids, valid_mask,
        bucket_table, position_bias, place_row, expert_ids, me,
        (size // 2, size // 2) + (size,) * (chunks - 1), local, each,
    )
    shape = (half, each * CAP, width)
    rows = relay(keep.reshape(shape), away.reshape(shape))
    latest_rows = rows
    backs, router_parts = [], []
    carried = None
    side = first_side = active_grads(after(grads, rows[0]), down_weight, 0, each)
    for c in range(chunks):
        later = None
        if c + 1 < chunks:
            later = [to_owners(after(other[c], side, *rows).reshape(owners, each * CAP, width))]
        *back, rows_all, active, router_part = run_experts(
            rows, side, up_weight, router_weight, scalars, c * each, carried, c + 1 == chunks
        )
        carried = rows_all, active
        if c + 1 < chunks:
            backs.append(to_owners(back[0]))
            side = active_grads(after(grads, router_part), down_weight, (c + 1) * each, each)
        rows = later
        router_parts.append(router_part)
    last_backs = spread(back)
    outs = expert_outputs(after(active, back), down_weight)
    backs = after(backs + last_backs, outs)
    router_grad = functools.reduce(jnp.add, router_parts)
    backs = [b.reshape(-1, width) for b in backs]

    core = (group % 2)[None]
    unit_rows = 16 * groups * max(half // 16, 1)
    sum_rows = -(-(4 * width + kinds) // (2 * unit_rows)) * unit_rows
    gain2_grad, residual_grad, mine, away, ctx_grad = residual_backward(
        core, place_col, residual, norm2_gain, out_grad, out_weight, ctx_t, router_grad, backs,
        sum_rows,
    )
    dq, dk, dv, mine, away, by_distance = attention_backward(
        core, qkv, ctx_grad, probs, n1_t, mine, away
    )
    outs = to_owners(after(outs, *backs)).reshape(owners * local * CAP, width)
    rows_gathered = lax.all_gather(after(rows_all, last_backs[1]), "dp")
    grads_gathered = lax.all_gather(after(grads, first_side, *latest_rows), "dp")
    expert_grads = [None]

    def some_experts(first, count, ready):
        expert_grads[0] = expert_wgrads(
            rows_gathered, after(grads_gathered, ready), up_weight, down_weight, router_weight,
            group_scalars, first, count, expert_grads[0],
        )
        return expert_grads[0]

    results = {}

    def first_norm(ready):
        results["input"] = input_backward(
            hidden_in, norm1_gain, after(residual_grad, ready), qkv_weight, (dq, dk, dv)
        )
        return results["input"]

    def last_sum(ready):
        results["output"] = block_output(
            place_col, residual, valid_mask, after(outs, ready), branch_stat, results["input"][1],
            gain2_grad, by_distance, bucket_table,
        )
        return results["output"]

    def short_sums(ready):
        results["short"] = sum_small(results["output"][1])
        return [results["short"]]

    sizes = [local]
    if local % 8 == 0:
        sizes = [local * 3 // 8, 0, local // 8, local // 2]
    starts = [sum(sizes[:k]) for k in range(len(sizes))]
    experts = [
        [functools.partial(some_experts, at, size)] if size else []
        for at, size in zip(starts, sizes, strict=True)
    ]
    experts += [[]] * (4 - len(experts))
    fillers = [[], [first_norm] + experts[0], [last_sum] + experts[1], [short_sums] + experts[2]]
    fillers += [experts[3]]
    mine, other = sum_everywhere(mine, away, fillers)
    block_out, input_grad = results["output"][0], results["input"][0]
    short = results["short"]
    gain_rows = width // BLOCK
    gain1_sum = short[:gain_rows].reshape(-1)
    gain2_sum = short[6 : 6 + gain_rows].reshape(-1)
    bias_sum = short[BIAS_ROW:].reshape(-1, NBUCKET)[:HEADS].T
    stat_sums = short[STAT_ROW]
    rms_stats = jnp.sqrt(stat_sums[:3] / (jnp.maximum(stat_sums[3], 1.0) * width))
    wide = widen(core, mine, width, None)
    qkv_sum, outw_sum = widen(1 - core, other, width, wide)
    used = slice(2 * width, 2 * width + kinds // 2)
    first = core[0] == 0
    router_sum = jnp.concatenate(
        [
            jnp.where(first, mine[used], other[used]),
            jnp.where(first, other[used], mine[used]),
        ]
    ).astype(F32)
    return (
        block_out,
        input_grad,
        gain1_sum,
        qkv_sum,
        bias_sum,
        outw_sum,
        gain2_sum,
        router_sum.T,
        *expert_grads[0],
        rms_stats,
    )


def solution(mesh):
    spread = P(("dp", "expert"), None)
    placed = (spread,) * 4 + (P(),) * 7 + (P("expert", None, None),) * 2 + (spread,)
    return jax.shard_map(
        on_device,
        mesh=mesh,
        in_specs=placed,
        out_specs=(spread, spread)
        + (P(),) * 6
        + (P("expert", None, "dp"), P("expert", "dp", None), P()),
        check_vma=False,
    )
```

```python
import functools

import jax
import jax.numpy as jnp
from jax import lax
from jax.experimental import pallas as pl
from jax.experimental.pallas import tpu as pltpu
from jax.sharding import PartitionSpec as P

HEADS = 12
HEAD_DIM = 64
NBUCKET = 32
CAP = 24
BLOCK = 128
WINDOW = 3
PAIR = 2 * HEAD_DIM
EPSILON = 1e-06
NEGATIVE = -1e30
HIGHEST = lax.Precision.HIGHEST
BF16 = jnp.bfloat16
F32 = jnp.float32
SUBSTEPS = 6
VMEM_LIMIT = 58 * 1024 * 1024


NN = (((1,), (0,)), ((), ()))
NT = (((1,), (1,)), ((), ()))
TN = (((0,), (0,)), ((), ()))


def dot(left, right, dims=NN, precision=None):
    return lax.dot_general(left, right, dims, precision=precision, preferred_element_type=F32)


def iota(shape, dim):
    return lax.broadcasted_iota(jnp.int32, shape, dim)


def whole(shape):
    return pl.BlockSpec(shape, lambda *_: (0,) * len(shape))


def params(**more):
    return pltpu.CompilerParams(vmem_limit_bytes=VMEM_LIMIT, **more)


def cost(microseconds):
    return pl.CostEstimate(
        flops=int(microseconds * 1.1e9), bytes_accessed=1000, transcendentals=0
    )


def windows(length):
    found = []
    row = 0
    for number in range(length // BLOCK):
        first = max(number - WINDOW + 1, 0)
        keys = (number - first + 1) * BLOCK
        found.append((number * BLOCK, first * BLOCK, keys, row))
        row += keys
    return found, row


def rms(values):
    return lax.rsqrt(jnp.mean(values * values, axis=-1, keepdims=True) + EPSILON)


def hot_columns(row0, row1, count, offset):
    slots = iota((count, row0.shape[1]), 0) + offset
    return jnp.where((slots == row0) | (slots == row1), 1.0, 0.0).astype(BF16)


def hot_rows(col0, col1, count, offset):
    slots = iota((col0.shape[0], count), 1) + offset
    return jnp.where((slots == col0) | (slots == col1), 1.0, 0.0).astype(BF16)


def id_parts(ids, local, each):
    inside = ids & (local - 1)
    return ids >> (local.bit_length() - 1), inside >> (each.bit_length() - 1), inside & (each - 1)


def route_kernel(me_ref, ids_ref, grad_ref, row_ref, rows_ref, *, local, each):
    length = grad_ref.shape[0]
    experts = rows_ref.shape[0] // CAP
    owners = experts // local
    before = iota((length, length), 0) < iota((length, length), 1)
    upper = jnp.where(before, 1.0, 0.0).astype(BF16)
    number = iota((experts, length), 0)
    hot = [number == ids_ref[c : c + 1, :] for c in range(2)]
    both = jnp.where(hot[0] | hot[1], 1.0, 0.0).astype(BF16)
    rank = dot(both, upper)
    rows = []
    for c in range(2):
        ids = ids_ref[c : c + 1, :]
        mine = jnp.sum(jnp.where(hot[c], rank, 0.0), axis=0, keepdims=True).astype(jnp.int32)
        rows.append(ids * CAP + mine)
        owner, chunk, within = id_parts(ids, local, each)
        far = owner ^ me_ref[0]
        turned = (far & 1) * (owners // 2) + (far >> 1)
        place = (chunk * owners + jnp.where(chunk == 0, turned, owner)) * each + within
        row_ref[c : c + 1, :] = place * CAP + mine
    chosen = hot_columns(rows[0], rows[1], rows_ref.shape[0], 0)
    rows_ref[...] = dot(chosen, grad_ref[...]).astype(BF16)


def route(ids, me, out_grad, slots, local, each):
    length, width = out_grad.shape
    in_vmem = pl.BlockSpec(memory_space=pltpu.VMEM)
    return pl.pallas_call(
        functools.partial(route_kernel, local=local, each=each),
        in_specs=[pl.BlockSpec(memory_space=pltpu.SMEM)] + [in_vmem] * 2,
        out_shape=(
            jax.ShapeDtypeStruct((2, length), jnp.int32),
            jax.ShapeDtypeStruct((slots, width), BF16),
        ),
        compiler_params=params(),
        cost_estimate=cost(5),
        name="route",
    )(me[None], ids.T, out_grad)


def return_places(ids_ref, me, col_ref, experts, local, each):
    length = ids_ref.shape[0]
    owners = experts // local
    after_it = iota((length, length), 0) > iota((length, length), 1)
    lower = jnp.where(after_it, 1.0, 0.0).astype(BF16)
    number = iota((length, experts), 1)
    hot = [number == ids_ref[:, c : c + 1] for c in range(2)]
    both = jnp.where(hot[0] | hot[1], 1.0, 0.0).astype(BF16)
    rank = dot(lower, both)
    for c in range(2):
        ids = ids_ref[:, c : c + 1]
        mine = jnp.sum(jnp.where(hot[c], rank, 0.0), axis=1, keepdims=True).astype(jnp.int32)
        owner, chunk, within = id_parts(ids, local, each)
        ends = chunk == local // each - 1
        place = (chunk * owners + jnp.where(ends, owner ^ me, owner)) * each + within
        col_ref[:, c : c + 1] = place * CAP + mine
        col_ref[:, 2 + c : 3 + c] = ids * CAP + mine


def forward_kernel(
    x_ref, gain1_ref, qkvw_ref, outw_ref, gain2_ref, docr_ref, docc_ref, validc_ref, bucket_ref,
    pbias_ref, row_ref, ids_ref, me_ref,
    probs_ref, qkv_ref, n1t_ref, ctx_ref, residual_ref, stat_ref, col_ref, *rest, local, each,
):
    rows_refs, (mask_s, bias_s, toeplitz_s) = rest[:-3], rest[-3:]
    pair = pl.program_id(0)
    length, width = x_ref.shape
    spans, _ = windows(length)

    @pl.when(pair == 0)
    def _():
        x = x_ref[...].astype(F32)
        n1 = (x * rms(x) * gain1_ref[...]).astype(BF16)
        n1t_ref[...] = n1.T
        for j in range(3):
            part = slice(j * width, (j + 1) * width)
            qkv_ref[:, part] = dot(n1, qkvw_ref[:, part]).astype(BF16)
        for q0, k0, keys, row in spans:
            shape = (keys, BLOCK)
            distance = (iota(shape, 1) + q0) - (iota(shape, 0) + k0)
            allowed = (
                (distance >= 0)
                & (docc_ref[k0 : k0 + keys, :] == docr_ref[:, q0 : q0 + BLOCK])
                & ((validc_ref[k0 : k0 + keys, :] == 1) | (distance == 0))
            )
            mask_s[row : row + keys, :] = jnp.where(allowed, 0.0, NEGATIVE)
        experts = sum(r.shape[0] for r in rows_refs) // CAP
        return_places(ids_ref, me_ref[0], col_ref, experts, local, each)
        span = bias_s.shape[1]
        hot = jnp.where(iota((NBUCKET, span), 0) == bucket_ref[...], 1.0, 0.0)
        bias_s[...] = dot(pbias_ref[...], hot, precision=HIGHEST)

    for side in range(2):
        head_bias = bias_s[pl.ds(2 * pair + side, 1), :]
        for m in range(WINDOW):
            ahead = head_bias[:, m * BLOCK : (m + 1) * BLOCK]
            back = max(m - 1, 0)
            behind = head_bias[:, back * BLOCK : (back + 1) * BLOCK]
            lanes = jnp.broadcast_to(
                jnp.concatenate([ahead, behind], axis=1), (BLOCK, 2 * BLOCK)
            )
            rolled = pltpu.roll(lanes, 0, 1, stride=1, stride_axis=0)
            place = (WINDOW - 1 - m) * BLOCK
            toeplitz_s[place : place + BLOCK, side * BLOCK : (side + 1) * BLOCK] = rolled[
                :, :BLOCK
            ]

    at = pl.multiple_of(pair * PAIR, PAIR)
    first_head = iota((BLOCK, PAIR), 1) < HEAD_DIM
    top = iota((PAIR, BLOCK), 0) < HEAD_DIM
    for q0, k0, keys, row in spans:
        q = qkv_ref[q0 : q0 + BLOCK, pl.ds(at, PAIR)].astype(F32) * HEAD_DIM ** (-0.5)
        stacked = jnp.concatenate(
            [jnp.where(first_head, q, 0.0), jnp.where(first_head, 0.0, q)], axis=0
        ).astype(BF16)
        k = qkv_ref[k0 : k0 + keys, pl.ds(pl.multiple_of(width + at, PAIR), PAIR)]
        v = qkv_ref[k0 : k0 + keys, pl.ds(pl.multiple_of(2 * width + at, PAIR), PAIR)]
        scores = dot(k, stacked, NT)
        masked = mask_s[row : row + keys, :]
        for side in range(2):
            lanes = slice(side * BLOCK, (side + 1) * BLOCK)
            s = scores[:, lanes] + toeplitz_s[WINDOW * BLOCK - keys :, lanes] + masked
            peak = jnp.max(s, axis=0, keepdims=True)
            e = jnp.exp(s - peak)
            total = jnp.sum(e, axis=0, keepdims=True)
            probs_ref[0, row : row + keys, lanes] = (e * (1.0 / total)).astype(BF16)
        both = dot(v, probs_ref[0, row : row + keys, :], TN)
        ctx = jnp.where(top, both[:, :BLOCK], both[:, BLOCK:])
        ctx_ref[pl.ds(at, PAIR), q0 : q0 + BLOCK] = ctx.astype(BF16)

    @pl.when(pair == pl.num_programs(0) - 1)
    def _():
        branch = dot(ctx_ref[...], outw_ref[...], TN)
        valid = validc_ref[...].astype(F32)
        stat_ref[...] = jnp.sum(valid * branch * branch, axis=0, keepdims=True)
        residual = x_ref[...].astype(F32) + branch
        residual_ref[...] = residual
        n2 = (residual * rms(residual) * gain2_ref[...]).astype(BF16)
        offset = 0
        for out in rows_refs:
            chosen = hot_columns(row_ref[0:1, :], row_ref[1:2, :], out.shape[0], offset)
            out[...] = dot(chosen, n2).astype(BF16)
            offset += out.shape[0]


def attention_forward(
    x, gain1, qkvw, outw, gain2, docs, valid, bucket_table, position_bias, place_row, ids, me,
    sizes, local, each,
):
    length, width = x.shape
    _, stored = windows(length)
    pairs = width // PAIR
    span = WINDOW * BLOCK
    padded_heads = -(-HEADS // 8) * 8
    bias_t = jnp.zeros((padded_heads, NBUCKET), F32).at[:HEADS].set(position_bias.T)
    arguments = (
        x, gain1[None], qkvw, outw, gain2[None], docs, docs.T, valid.T,
        bucket_table[None, :span], bias_t, place_row, ids,
    )
    out_shape = (
        jax.ShapeDtypeStruct((pairs, stored, 2 * BLOCK), BF16),
        jax.ShapeDtypeStruct((length, 3 * width), BF16),
        jax.ShapeDtypeStruct((width, length), BF16),
        jax.ShapeDtypeStruct((width, length), BF16),
        jax.ShapeDtypeStruct((length, width), F32),
        jax.ShapeDtypeStruct((1, width), F32),
        jax.ShapeDtypeStruct((length, 4), jnp.int32),
    ) + tuple(jax.ShapeDtypeStruct((n, width), BF16) for n in sizes)
    return pl.pallas_call(
        functools.partial(forward_kernel, local=local, each=each),
        grid=(pairs,),
        in_specs=[whole(a.shape) for a in arguments] + [pl.BlockSpec(memory_space=pltpu.SMEM)],
        out_specs=[pl.BlockSpec((1, stored, 2 * BLOCK), lambda p: (p, 0, 0))]
        + [whole(s.shape) for s in out_shape[1:]],
        out_shape=out_shape,
        scratch_shapes=[
            pltpu.VMEM((stored, BLOCK), F32),
            pltpu.VMEM((padded_heads, span), F32),
            pltpu.VMEM((span, 2 * BLOCK), F32),
        ],
        compiler_params=params(),
        cost_estimate=cost(22),
        name="attention_forward",
    )(*arguments, me[None])


def expert_gate(rows, router, expert):
    logits = dot(rows, router)
    shifted = jnp.exp(logits - jnp.max(logits, axis=-1, keepdims=True))
    probs = shifted / jnp.sum(shifted, axis=-1, keepdims=True)
    mine = iota(probs.shape, 1) == expert
    return probs, mine, jnp.sum(jnp.where(mine, probs, 0.0), axis=-1, keepdims=True)


GELU_SCALE = 0.7978845608028654
GELU_CUBE = 0.044715


def gelu_parts(v):
    square = v * v
    t = jnp.tanh(v * (GELU_SCALE + (GELU_SCALE * GELU_CUBE) * square))
    half = 0.5 * v
    value = half + half * t
    slope = 0.5 + 0.5 * t + half * (1.0 - t * t) * (
        GELU_SCALE + (3.0 * GELU_SCALE * GELU_CUBE) * square
    )
    return value, slope


def active_grad_kernel(grads_ref, down_ref, out_ref, g_s, grads_s):
    e, f = pl.program_id(0), pl.program_id(1)

    @pl.when((e == 0) & (f == 0))
    def _():
        grads_s[...] = grads_ref[...].astype(F32)

    @pl.when(f == 0)
    def _():
        here = pl.ds(pl.multiple_of(e * CAP, CAP), CAP)
        g_s[...] = grads_s[:, here, :].reshape(g_s.shape).astype(BF16)

    out_ref[0] = dot(g_s[...], down_ref[0], NT).astype(BF16)


def active_grads(grads, down_weight, first, experts, blocks=1):
    owners, _, width = grads.shape
    inner = down_weight.shape[1]
    step, count = inner // blocks, owners * CAP
    return pl.pallas_call(
        active_grad_kernel,
        grid=(experts, blocks),
        in_specs=[
            pl.BlockSpec((owners, experts * CAP, width), lambda e, f: (0, first // experts, 0)),
            pl.BlockSpec((1, step, width), lambda e, f: (first + e, f, 0)),
        ],
        out_specs=pl.BlockSpec((1, count, step), lambda e, f: (e, 0, f)),
        out_shape=jax.ShapeDtypeStruct((experts, count, inner), BF16),
        scratch_shapes=[pltpu.VMEM((count, width), BF16), pltpu.VMEM((owners, experts * CAP, width), F32)],
        compiler_params=params(),
        cost_estimate=cost(0.01),
        name="active_grads",
    )(grads, down_weight)


def expert_kernel(scalar_ref, *refs, parts, aliased, last):
    rows_refs, refs = refs[:parts], refs[parts:]
    side_ref, up_ref, router_ref = refs[:3]
    refs = refs[3 + aliased :]
    backs = max(last, 1)
    back_refs, refs = refs[:backs], refs[backs:]
    all_ref, active_ref, router_grad_ref = refs[:3]
    rows_s, back_s, x_s, probs_s, gate_s, sum_s, dx_s, grad_s = refs[3:]
    e, f = pl.program_id(0), pl.program_id(1)
    experts, blocks = pl.num_programs(0), pl.num_programs(1)
    me = scalar_ref[1]
    expert = scalar_ref[0] + e
    count, width = x_s.shape
    owners = rows_s.shape[0]
    here = pl.ds(pl.multiple_of(e * CAP, CAP), CAP)

    @pl.when((e == 0) & (f == 0))
    def _():
        if parts == 1:
            all_ref[0] = rows_refs[0][...]
            rows_s[...] = rows_refs[0][...].astype(F32)
        else:
            for k in range(parts):
                all_ref[0, me ^ k] = rows_refs[k][...]
                rows_s[me ^ k] = rows_refs[k][...].astype(F32)
        router_grad_ref[...] = jnp.zeros_like(router_grad_ref)

    @pl.when(f == 0)
    def _():
        x = rows_s[:, here, :].reshape(count, width).astype(BF16)
        x_s[...] = x
        probs, _, gate = expert_gate(x, router_ref[...], expert)
        probs_s[...] = probs
        gate_s[...] = jnp.broadcast_to(gate, gate_s.shape)
        sum_s[...] = jnp.zeros_like(sum_s)
        dx_s[...] = jnp.zeros_like(dx_s)

    gate = gate_s[:, :1]
    x = x_s[...]
    step = up_ref.shape[2] // SUBSTEPS
    total = None
    inner = dot(x, up_ref[0, :, :step])
    for s in range(SUBSTEPS):
        here_f = slice(s * step, (s + 1) * step)
        later = dot(x, up_ref[0, :, (s + 1) * step : (s + 2) * step]) if s + 1 < SUBSTEPS else None
        value, slope = gelu_parts(inner)
        side = side_ref[0, :, here_f].astype(F32) * gate
        part = jnp.sum(value * side, axis=-1, keepdims=True)
        total = part if total is None else total + part
        active_ref[0, :, here_f] = (gate * value).astype(BF16)
        grad_s[:, here_f] = (side * slope).astype(BF16)
        inner = later
    sum_s[...] += total
    dx_s[...] += dot(grad_s[...], up_ref[0], NT)

    @pl.when(f == blocks - 1)
    def _():
        probs = probs_s[...]
        mine = iota(probs.shape, 1) == expert
        logit_grad = (sum_s[:, :1] * (jnp.where(mine, 1.0, 0.0) - probs)).astype(BF16)
        router_grad_ref[...] += dot(logit_grad, x_s[...], TN)
        dx = dx_s[...] + dot(logit_grad, router_ref[...], NT)
        back_s[:, here, :] = dx.reshape(owners, CAP, width)

    @pl.when((e == experts - 1) & (f == blocks - 1))
    def _():
        if last:
            for k in range(owners):
                back_refs[k][...] = back_s[me ^ k].astype(BF16)
        else:
            back_refs[0][...] = back_s[...].astype(BF16)


def run_experts(
    rows, side, up_weight, router, scalars, first, old, last
):
    parts = len(rows)
    slots, width = rows[0].shape[-2:]
    owners = parts if parts > 1 else rows[0].shape[0]
    experts = slots // CAP
    local, _, inner = up_weight.shape
    count, kinds = owners * CAP, router.shape[1]
    blocks = 1 if count <= 256 else 3
    step = inner // blocks
    backs = [jax.ShapeDtypeStruct((owners, slots, width), BF16)]
    if last:
        backs = [jax.ShapeDtypeStruct((slots, width), BF16)] * owners
    in_specs = [whole(r.shape) for r in rows] + [
        pl.BlockSpec((1, count, step), lambda e, f, _: (e, 0, f)),
        pl.BlockSpec((1, width, step), lambda e, f, _: (first + e, 0, f)),
        whole(router.shape),
    ]
    arguments = (*rows, side, up_weight, router)
    aliases = {}
    if old is not None:
        aliases = {1 + len(arguments) + k: len(backs) + k for k in range(2)}
        in_specs += [pl.BlockSpec(memory_space=pl.ANY)] * 2
        arguments += tuple(old)
    return pl.pallas_call(
        functools.partial(expert_kernel, parts=parts, aliased=len(aliases), last=owners if last else 0),
        grid_spec=pltpu.PrefetchScalarGridSpec(
            num_scalar_prefetch=1,
            grid=(experts, blocks),
            in_specs=in_specs,
            out_specs=[whole(back.shape) for back in backs]
            + [
                pl.BlockSpec((1, owners, slots, width), lambda e, f, _: (first // experts, 0, 0, 0)),
                pl.BlockSpec((1, count, step), lambda e, f, _: (first + e, 0, f)),
                whole((kinds, width)),
            ],
            scratch_shapes=[
                pltpu.VMEM((owners, slots, width), F32),
                pltpu.VMEM((owners, slots, width), F32),
                pltpu.VMEM((count, width), BF16),
                pltpu.VMEM((count, kinds), F32),
                pltpu.VMEM((count, BLOCK), F32),
                pltpu.VMEM((count, BLOCK), F32),
                pltpu.VMEM((count, width), F32),
                pltpu.VMEM((count, step), BF16),
            ],
        ),
        out_shape=(
            *backs,
            jax.ShapeDtypeStruct((local // experts, owners, slots, width), BF16),
            jax.ShapeDtypeStruct((local, count, inner), BF16),
            jax.ShapeDtypeStruct((kinds, width), F32),
        ),
        input_output_aliases=aliases,
        compiler_params=params(),
        cost_estimate=cost(22),
        name="experts",
    )(scalars + jnp.array([first, 0], jnp.int32), *arguments)


def expert_out_kernel(active_ref, down_ref, out_ref, all_s):
    e, f = pl.program_id(0), pl.program_id(1)
    experts, blocks = pl.num_programs(0), pl.num_programs(1)
    here = pl.ds(pl.multiple_of(e * CAP, CAP), CAP)
    part = dot(active_ref[0], down_ref[0]).reshape(all_s.shape[0], CAP, all_s.shape[2])

    @pl.when(f == 0)
    def _():
        all_s[:, here, :] = part

    @pl.when(f > 0)
    def _():
        all_s[:, here, :] += part

    @pl.when((e == experts - 1) & (f == blocks - 1))
    def _():
        out_ref[...] = all_s[...].astype(BF16)


def expert_outputs(active, down_weight, blocks=1):
    experts, count, inner = active.shape
    width = down_weight.shape[2]
    step, owners = inner // blocks, count // CAP
    shape = (owners, experts * CAP, width)
    return pl.pallas_call(
        expert_out_kernel,
        grid=(experts, blocks),
        in_specs=[
            pl.BlockSpec((1, count, step), lambda e, f: (e, 0, f)),
            pl.BlockSpec((1, step, width), lambda e, f: (e, f, 0)),
        ],
        out_specs=whole(shape),
        out_shape=jax.ShapeDtypeStruct(shape, BF16),
        scratch_shapes=[pltpu.VMEM(shape, F32)],
        compiler_params=params(),
        cost_estimate=cost(0.01),
        name="expert_outputs",
    )(active, down_weight)


def expert_wgrad_kernel(
    scalar_ref, rows_ref, grads_ref, up_ref, down_ref, router_ref, *rest, first
):
    up_out, down_out, x_s, g_s = rest[-4:]
    expert, tile = first + pl.program_id(0), pl.program_id(1)
    count, width = x_s.shape
    for side in range(2):

        @pl.when(expert % 2 == side)
        def _():
            part = slice(side * CAP, (side + 1) * CAP)
            x = rows_ref[...].astype(F32)[:, 0, :, part, :].reshape(count, width).astype(BF16)
            x_s[...] = x
            _, _, gate = expert_gate(x, router_ref[...], scalar_ref[0] + expert)
            g = grads_ref[...].astype(F32)[:, :, part, :].reshape(count, width)
            g_s[...] = (gate * g).astype(BF16)

    x, g = x_s[...], g_s[...]
    value, slope = gelu_parts(dot(x, up_ref[0]))
    inner_grad = (dot(g, down_ref[0], NT) * slope).astype(BF16)

    @pl.when(tile == 0)
    def _():
        down_out[0] = dot(value.astype(BF16), g, TN)
        up_out[0] = dot(x, inner_grad, TN)

    @pl.when(tile > 0)
    def _():
        down_out[0] += dot(value.astype(BF16), g, TN)
        up_out[0] += dot(x, inner_grad, TN)


def expert_wgrads(rows, grads, up_weight, down_weight, router, scalars, first, experts, old):
    groups, chunks, owners, _, width = rows.shape
    local, _, inner = up_weight.shape
    each = local // chunks
    share = inner // groups
    taken = max(min(groups, 32 // owners), 1)
    count = taken * owners * CAP

    def rows_at(e, t, _):
        return (t, (first + e) // each, 0, (first + e) % each // 2, 0)

    in_specs = [
        pl.BlockSpec((taken, 1, owners, 2 * CAP, width), rows_at),
        pl.BlockSpec((taken, owners, 2 * CAP, width), lambda e, t, _: (t, 0, (first + e) // 2, 0)),
        pl.BlockSpec((1, width, share), lambda e, t, s: (first + e, 0, s[1])),
        pl.BlockSpec((1, share, width), lambda e, t, s: (first + e, s[1], 0)),
        whole(router.shape),
    ]
    arguments = (rows, grads, up_weight, down_weight, router)
    aliases = {}
    if old is not None:
        aliases = {6: 0, 7: 1}
        in_specs += [pl.BlockSpec(memory_space=pl.ANY)] * 2
        arguments += tuple(old)
    return pl.pallas_call(
        functools.partial(expert_wgrad_kernel, first=first),
        grid_spec=pltpu.PrefetchScalarGridSpec(
            num_scalar_prefetch=1,
            grid=(experts, groups // taken),
            in_specs=in_specs,
            out_specs=[
                pl.BlockSpec((1, width, share), lambda j, t, _: (first + j, 0, 0)),
                pl.BlockSpec((1, share, width), lambda j, t, _: (first + j, 0, 0)),
            ],
            scratch_shapes=[
                pltpu.VMEM((count, width), BF16),
                pltpu.VMEM((count, width), BF16),
            ],
        ),
        out_shape=(
            jax.ShapeDtypeStruct((local, width, share), F32),
            jax.ShapeDtypeStruct((local, share, width), F32),
        ),
        input_output_aliases=aliases,
        compiler_params=params(),
        cost_estimate=cost(0.01),
        name="expert_wgrads",
    )(scalars, *arguments)


def residual_kernel(
    half_ref, col_ref, residual_ref, gain_ref, grad_ref, outw_ref, ctx_ref, router_ref, *rest
):
    back_refs, rest = rest[:-8], rest[-8:]
    gain_grad_ref, residual_grad_ref, mine_ref, away_ref, ctx_grad_ref, early_s, sem0, sem1 = rest
    whole_backs = back_refs[0][...]
    if len(back_refs) > 1:
        whole_backs = jnp.concatenate([back[...] for back in back_refs], axis=0)
    chosen = hot_rows(col_ref[:, 0:1], col_ref[:, 1:2], whole_backs.shape[0], 0)
    n2_grad = dot(chosen, whole_backs)
    residual = residual_ref[...]
    factor = rms(residual)
    unit = residual * factor
    gain_grad_ref[...] = jnp.sum(n2_grad * unit, axis=0, keepdims=True)
    scaled = n2_grad * gain_ref[...]
    centre = jnp.mean(scaled * unit, axis=-1, keepdims=True)
    residual_grad = grad_ref[...].astype(F32) + factor * (scaled - unit * centre)
    residual_grad_ref[...] = residual_grad
    branch_grad = residual_grad.astype(BF16)
    width, kinds = ctx_ref.shape[0], router_ref.shape[0]
    rows = early_s.shape[1]
    used = (width + kinds) // 2
    copies = []
    for k, (out, sem) in enumerate(((mine_ref, sem0), (away_ref, sem1))):
        part = half_ref[0] ^ k
        ctx = ctx_ref[pl.ds(pl.multiple_of(part * (width // 2), width // 2), width // 2), :]
        early_s[k, : width // 2, :] = dot(ctx, branch_grad).astype(BF16)
        router = router_ref[pl.ds(pl.multiple_of(part * (kinds // 2), kinds // 2), kinds // 2), :]
        early_s[k, width // 2 : used, :] = router.astype(BF16)
        if used < rows:
            early_s[k, used:, :] = jnp.zeros((rows - used, width), BF16)
        copies.append(
            pltpu.make_async_copy(early_s.at[k], out.at[pl.ds(3 * width // 2, rows)], sem)
        )
        copies[k].start()
    ctx_grad_ref[...] = dot(branch_grad, outw_ref[...], NT).astype(BF16)
    for copy in copies:
        copy.wait()


def residual_backward(
    half, place_col, residual, gain2, out_grad, outw, ctx_t, router_grad, backs, rows
):
    length, width = residual.shape
    early = rows - 3 * width // 2
    in_vmem = pl.BlockSpec(memory_space=pltpu.VMEM)
    anywhere = pl.BlockSpec(memory_space=pl.ANY)
    buffer = jax.ShapeDtypeStruct((rows, width), BF16)
    return pl.pallas_call(
        residual_kernel,
        in_specs=[pl.BlockSpec(memory_space=pltpu.SMEM)] + [in_vmem] * (7 + len(backs)),
        out_specs=[in_vmem, in_vmem, anywhere, anywhere, in_vmem],
        out_shape=(
            jax.ShapeDtypeStruct((1, width), F32),
            jax.ShapeDtypeStruct((length, width), F32),
            buffer,
            buffer,
            jax.ShapeDtypeStruct((length, width), BF16),
        ),
        scratch_shapes=[
            pltpu.VMEM((2, early, width), BF16),
            pltpu.SemaphoreType.DMA,
            pltpu.SemaphoreType.DMA,
        ],
        compiler_params=params(),
        cost_estimate=cost(0.01),
        name="residual_backward",
    )(half, place_col, residual, gain2[None], out_grad, outw, ctx_t, router_grad, *backs)


def attention_backward_kernel(
    half_ref, q_ref, k_ref, v_ref, dctx_ref, probs_ref, n1t_ref, _, __,
    dq_ref, dk_ref, dv_ref, mine_ref, away_ref, bias_ref,
    dqt_s, dk_s, dv_s, diagonal_s,
):
    length = q_ref.shape[0]
    spans, _ = windows(length)
    first_head = iota((BLOCK, PAIR), 1) < HEAD_DIM
    top = iota((PAIR, BLOCK), 0) < HEAD_DIM
    scale = HEAD_DIM ** (-0.5)
    dk_s[...] = jnp.zeros_like(dk_s)
    dv_s[...] = jnp.zeros_like(dv_s)
    diagonal_s[...] = jnp.zeros_like(diagonal_s)

    def stack(values):
        values = values.astype(F32)
        return jnp.concatenate(
            [jnp.where(first_head, values, 0.0), jnp.where(first_head, 0.0, values)], axis=0
        ).astype(BF16)

    for q0, k0, keys, row in spans:
        q = stack(q_ref[q0 : q0 + BLOCK, :])
        dctx = stack(dctx_ref[q0 : q0 + BLOCK, :])
        span = slice(k0, k0 + keys)
        probs = probs_ref[0, row : row + keys, :]
        prob_side = dot(v_ref[span, :], dctx, NT)
        halves = []
        for side in range(2):
            lanes = slice(side * BLOCK, (side + 1) * BLOCK)
            p = probs[:, lanes].astype(F32)
            d = prob_side[:, lanes]
            centre = jnp.sum(p * d, axis=0, keepdims=True)
            s = p * (d - centre)
            diagonal_s[WINDOW * BLOCK - keys :, lanes] += s
            halves.append(s.astype(BF16))
        score_grad = jnp.concatenate(halves, axis=1)
        dk_s[span, :] += dot(score_grad, q)
        dv_s[span, :] += dot(probs, dctx)
        both = dot(k_ref[span, :], score_grad, TN)
        dqt_s[:, q0 : q0 + BLOCK] = jnp.where(top, both[:, :BLOCK], both[:, BLOCK:])
    dq = (dqt_s[...].T * scale).astype(BF16)
    dk = (dk_s[...] * scale).astype(BF16)
    dv = dv_s[...].astype(BF16)
    dq_ref[...] = dq
    dk_ref[...] = dk
    dv_ref[...] = dv
    width = n1t_ref.shape[0]
    for k, out in enumerate((mine_ref, away_ref)):
        part = pl.multiple_of((half_ref[0] ^ k) * (width // 2), width // 2)
        n1t = n1t_ref[pl.ds(part, width // 2), :]
        two = dot(n1t, jnp.concatenate([dq, dk], axis=1))
        out[: width // 2, :] = two[:, :PAIR].astype(BF16)
        out[width // 2 : width, :] = two[:, PAIR:].astype(BF16)
        out[width:, :] = dot(n1t, dv).astype(BF16)
    bias_ref[...] = jnp.zeros_like(bias_ref)
    for side in range(2):
        lanes = slice(side * BLOCK, (side + 1) * BLOCK)
        pieces = []
        for m in range(WINDOW):
            place = (WINDOW - 1 - m) * BLOCK
            block = diagonal_s[place : place + BLOCK, lanes]
            skewed = jnp.zeros((8, 2 * BLOCK), F32)
            for k in range(0, BLOCK, 8):
                eight = block[k : k + 8, :]
                wide = jnp.concatenate([eight, jnp.zeros_like(eight)], axis=1)
                skewed += wide if k == 0 else pltpu.roll(wide, 2 * BLOCK - k, 1)
            for bit in (1, 2, 4):
                moved = pltpu.roll(skewed, 2 * BLOCK - bit, 1)
                skewed = jnp.where(iota(skewed.shape, 0) & bit != 0, moved, skewed)
            pieces.append(jnp.sum(skewed, axis=0, keepdims=True))
        for m in range(WINDOW):
            total = pieces[m][:, :BLOCK]
            if m + 1 < WINDOW:
                total = total + pieces[m + 1][:, BLOCK:]
            bias_ref[0, side : side + 1, m * BLOCK : (m + 1) * BLOCK] = total


def attention_backward(half, qkv, ctx_grad, probs, n1_t, mine, away):
    length, width = ctx_grad.shape
    stored = probs.shape[1]
    pairs = width // PAIR
    span = WINDOW * BLOCK
    column = pl.BlockSpec((length, PAIR), lambda p, _: (0, p))
    summed = pl.BlockSpec((3 * width // 2, PAIR), lambda p, _: (0, p))
    anywhere = pl.BlockSpec(memory_space=pl.ANY)
    rows = jax.ShapeDtypeStruct((length, width), BF16)
    return pl.pallas_call(
        attention_backward_kernel,
        grid_spec=pltpu.PrefetchScalarGridSpec(
            num_scalar_prefetch=1,
            grid=(pairs,),
            in_specs=[
                column,
                pl.BlockSpec((length, PAIR), lambda p, _: (0, pairs + p)),
                pl.BlockSpec((length, PAIR), lambda p, _: (0, 2 * pairs + p)),
                column,
                pl.BlockSpec((1, stored, 2 * BLOCK), lambda p, _: (p, 0, 0)),
                whole(n1_t.shape),
                anywhere,
                anywhere,
            ],
            out_specs=[
                column,
                column,
                column,
                summed,
                summed,
                pl.BlockSpec((1, 8, span), lambda p, _: (p, 0, 0)),
            ],
            scratch_shapes=[
                pltpu.VMEM((PAIR, length), F32),
                pltpu.VMEM((length, PAIR), F32),
                pltpu.VMEM((length, PAIR), F32),
                pltpu.VMEM((span, 2 * BLOCK), F32),
            ],
        ),
        out_shape=(
            rows,
            rows,
            rows,
            jax.ShapeDtypeStruct(mine.shape, BF16),
            jax.ShapeDtypeStruct(away.shape, BF16),
            jax.ShapeDtypeStruct((pairs, 8, span), F32),
        ),
        input_output_aliases={7: 3, 8: 4},
        compiler_params=params(),
        cost_estimate=cost(96),
        name="attention_backward",
    )(half, qkv, qkv, qkv, ctx_grad, probs, n1_t, mine, away)


def input_kernel(x_ref, gain_ref, residual_grad_ref, qkvw_ref, *rest):
    parts, (grad_ref, gain_grad_ref) = rest[:-2], rest[-2:]
    x = x_ref[...].astype(F32)
    factor = rms(x)
    unit = x * factor
    n1_grad = None
    at = 0
    for part in parts:
        columns = part.shape[1]
        term = dot(part[...], qkvw_ref[:, at : at + columns], NT)
        n1_grad = term if n1_grad is None else n1_grad + term
        at += columns
    gain_grad_ref[...] = jnp.sum(n1_grad * unit, axis=0, keepdims=True)
    scaled = n1_grad * gain_ref[...]
    centre = jnp.mean(scaled * unit, axis=-1, keepdims=True)
    grad_ref[...] = (residual_grad_ref[...] + factor * (scaled - unit * centre)).astype(BF16)


def input_backward(x, gain1, residual_grad, qkvw, parts):
    length, width = x.shape
    return pl.pallas_call(
        input_kernel,
        out_shape=(
            jax.ShapeDtypeStruct((length, width), BF16),
            jax.ShapeDtypeStruct((1, width), F32),
        ),
        compiler_params=params(),
        cost_estimate=cost(0.01),
        name="input_backward",
    )(x, gain1[None], residual_grad, qkvw, *parts)


SHORT_ROWS = 16
STAT_ROW = 12
BIAS_ROW = 13


def output_kernel(
    col_ref, residual_ref, validc_ref, rows_ref, stat_ref, gain1_ref, gain2_ref, by_ref, bucket_ref,
    block_ref, sent_ref, distance_s, short_ref,
):
    chosen = hot_rows(col_ref[:, 2:3], col_ref[:, 3:4], rows_ref.shape[0], 0)
    mixture = dot(chosen, rows_ref[...])
    output = residual_ref[...] + mixture
    block_ref[...] = output.astype(BF16)
    valid = validc_ref[...].astype(F32)
    short_ref[...] = jnp.zeros_like(short_ref)
    for k in range(gain1_ref.shape[1] // BLOCK):
        lanes = slice(k * BLOCK, (k + 1) * BLOCK)
        short_ref[k : k + 1, :] = gain1_ref[:, lanes]
        short_ref[6 + k : 7 + k, :] = gain2_ref[:, lanes]
    lane = iota((1, BLOCK), 1)
    stats = jnp.where(lane == 0, jnp.sum(valid * output * output), 0.0)
    stats = jnp.where(lane == 1, jnp.sum(stat_ref[...]), stats)
    stats = jnp.where(lane == 2, jnp.sum(valid * mixture * mixture), stats)
    short_ref[STAT_ROW : STAT_ROW + 1, :] = jnp.where(lane == 3, jnp.sum(valid), stats)
    distance_s[...] = jnp.zeros_like(distance_s)
    for head in range(HEADS):
        distance_s[head : head + 1, :] = by_ref[head // 2, head % 2 : head % 2 + 1, :]
    buckets = iota((BLOCK, distance_s.shape[1]), 0) & (NBUCKET - 1)
    hot = jnp.where(buckets == bucket_ref[...], 1.0, 0.0)
    sums = dot(distance_s[...], hot, NT, HIGHEST)
    packed = BLOCK // NBUCKET
    own = iota(sums.shape, 1) // NBUCKET == iota(sums.shape, 0) % packed
    sums = jnp.where(own, sums, 0.0)
    for k in range(HEADS // packed):
        rows = sums[k * packed : (k + 1) * packed, :]
        short_ref[BIAS_ROW + k : BIAS_ROW + k + 1, :] = jnp.sum(rows, axis=0, keepdims=True)
    sent_ref[...] = jnp.broadcast_to(short_ref[...][None], sent_ref.shape)


def block_output(
    place_col, residual, valid, rows, branch_stat, gain1_grad, gain2_grad, by_distance, bucket_table,
    devices,
):
    length, width = residual.shape
    span = by_distance.shape[2]
    return pl.pallas_call(
        output_kernel,
        out_shape=(
            jax.ShapeDtypeStruct((length, width), BF16),
            jax.ShapeDtypeStruct((devices, SHORT_ROWS, BLOCK), F32),
        ),
        scratch_shapes=[
            pltpu.VMEM((-(-HEADS // 8) * 8, span), F32),
            pltpu.VMEM((SHORT_ROWS, BLOCK), F32),
        ],
        compiler_params=params(),
        cost_estimate=cost(0.01),
        name="block_output",
    )(
        place_col, residual, valid.T, rows, branch_stat, gain1_grad, gain2_grad, by_distance,
        bucket_table[None, :span],
    )


def swap(values, axis, bit):
    size = lax.axis_size(axis)
    return lax.ppermute(values, axis, [(i, i ^ bit) for i in range(size)])


def axis_bits(axis):
    size = lax.axis_size(axis)
    bits = []
    bit = 1
    while bit < size:
        bits.append((axis, bit))
        bit *= 2
    return bits


def spread(parts):
    nearest = swap(parts[1], "expert", 1)
    far = [after(part, nearest) for part in parts[4:]]
    parts = parts[:4] + far
    return [parts[0], nearest] + [swap(parts[k], "expert", k) for k in range(2, len(parts))]


def relay(keep, away):
    arrived = swap(away, "expert", 1)
    keep = after(keep, arrived)
    found = []
    for j in range(keep.shape[0]):
        for part in (keep[j], arrived[j]):
            found.append(swap(part, "expert", 2 * j) if j else part)
    return found


def after(values, *others):
    return lax.optimization_barrier((values, others))[0]


def levels():
    groups, owners = lax.axis_size("dp"), lax.axis_size("expert")
    dp, expert = lax.axis_index("dp"), lax.axis_index("expert")
    axes = ("dp", "expert")

    def sender(width, fold):
        def send(values, k):
            def target(i):
                d, e = fold(i // owners, i % owners, k)
                return d * owners + e

            return lax.ppermute(values, axes, [(i, target(i)) for i in range(groups * owners)])

        return send

    return [
        (2, dp % 2, sender(2, lambda d, e, k: (d ^ k, e))),
        (
            groups,
            dp // 2 * 2 + expert % 2,
            sender(groups, lambda d, e, k: (d ^ (k // 2 * 2), e ^ (k % 2))),
        ),
        (owners // 2, expert // 2, sender(owners // 2, lambda d, e, k: (d, e ^ (2 * k)))),
    ]


def halve_kernel(place_ref, mine_ref, arrived_ref, *out_refs):
    rows = out_refs[0].shape[0]
    for k, out in enumerate(out_refs):
        here = pl.ds(pl.multiple_of((place_ref[0] ^ k) * rows, 16), rows)
        out[...] = (mine_ref[here, :].astype(F32) + arrived_ref[here, :].astype(F32)).astype(BF16)


def halve(place, mine, arrived, count):
    rows, width = mine.shape
    in_vmem = pl.BlockSpec(memory_space=pltpu.VMEM)
    return pl.pallas_call(
        halve_kernel,
        in_specs=[pl.BlockSpec(memory_space=pltpu.SMEM), in_vmem, in_vmem],
        out_shape=[jax.ShapeDtypeStruct((rows // count, width), BF16)] * count,
        compiler_params=params(),
        cost_estimate=cost(0.01),
        name="halve",
    )(place.astype(jnp.int32)[None], mine, arrived)


def sum_everywhere(mine, away, fillers):
    steps = levels()
    fillers = iter(fillers)

    def fill(terms, ready):
        found = [run(ready) for run in next(fillers, ())]
        return after(terms, *found) if found else terms

    _, _, send = steps[0]
    arrived = fill(send(away, 1), (mine, away))
    blocks = None
    for count, place, send in steps[1:]:
        if blocks is None:
            blocks = halve(place, mine, arrived, count)
        else:
            share = values.shape[0] // count
            blocks = [
                lax.dynamic_slice_in_dim(values, (place ^ k) * share, share, 0)
                for k in range(count)
            ]
        sent = fill([send(blocks[k], k) for k in range(1, count)], blocks)
        values = sum(t.astype(F32) for t in [blocks[0]] + sent).astype(BF16)
    for count, place, send in reversed(steps[1:]):
        share = values.shape[0]
        sent = fill([send(values, k) for k in range(1, count)], values)
        found = jnp.zeros((count * share, values.shape[1]), BF16)
        for k, piece in enumerate([values] + sent):
            found = lax.dynamic_update_slice_in_dim(found, piece, (place ^ k) * share, 0)
        values = found
    _, _, send = steps[0]
    other = fill(send(values, 1), values)
    for rest in fillers:
        for run in rest:
            run(values)
    return values, other


def widen_kernel(half_ref, rows_ref, *rest):
    qkv_ref, outw_ref = rest[-2:]
    j = pl.program_id(0)

    @pl.when(j < 3)
    def _():
        qkv_ref[...] = rows_ref[...].astype(F32)

    @pl.when(j == 3)
    def _():
        outw_ref[...] = rows_ref[...].astype(F32)


def widen(half, rows, width, old):
    taken = width // 2
    in_specs = [pl.BlockSpec((taken, width), lambda j, _: (j, 0))]
    arguments = (rows,)
    aliases = {}
    if old is not None:
        in_specs += [pl.BlockSpec(memory_space=pl.ANY)] * 2
        arguments += tuple(old)
        aliases = {2: 0, 3: 1}
    return pl.pallas_call(
        widen_kernel,
        grid_spec=pltpu.PrefetchScalarGridSpec(
            num_scalar_prefetch=1,
            grid=(4,),
            in_specs=in_specs,
            out_specs=[
                pl.BlockSpec((taken, width), lambda j, s: (s[0], jnp.minimum(j, 2))),
                pl.BlockSpec((taken, width), lambda j, s: (s[0], 0)),
            ],
        ),
        out_shape=(
            jax.ShapeDtypeStruct((width, 3 * width), F32),
            jax.ShapeDtypeStruct((width, width), F32),
        ),
        input_output_aliases=aliases,
        compiler_params=params(),
        cost_estimate=cost(4),
        name="widen",
    )(half, *arguments)


def sum_small(sent):
    return jnp.sum(lax.all_to_all(sent, ("dp", "expert"), 0, 0, tiled=True), axis=0)


def on_device(
    hidden_in, doc_ids, valid_mask, expert_ids, bucket_table, norm1_gain, qkv_weight, position_bias,
    out_weight, norm2_gain, router_weight, up_weight, down_weight, out_grad,
):
    length, width = hidden_in.shape
    local = up_weight.shape[0]
    owners = lax.axis_size("expert")
    groups = lax.axis_size("dp")
    kinds = router_weight.shape[1]
    chunks = 2 if local % 4 == 0 else 1
    each = local // chunks
    half = owners // 2
    me = lax.axis_index("expert").astype(jnp.int32)
    group = lax.axis_index("dp").astype(jnp.int32)
    scalars = jnp.stack([me * local, me])
    group_scalars = jnp.stack([me * local, group])

    place_row, grad_rows = route(expert_ids, me, out_grad, owners * local * CAP, local, each)
    to_owners = functools.partial(
        lax.all_to_all, axis_name="expert", split_axis=0, concat_axis=0, tiled=True
    )
    grads = to_owners(grad_rows.reshape(owners, local * CAP, width))
    size = owners * each * CAP
    probs, qkv, n1_t, ctx_t, residual, branch_stat, place_col, keep, away, *other = attention_forward(
        hidden_in, norm1_gain, qkv_weight, out_weight, norm2_gain, doc_ids, valid_mask,
        bucket_table, position_bias, place_row, expert_ids, me,
        (size // 2, size // 2) + (size,) * (chunks - 1), local, each,
    )
    shape = (half, each * CAP, width)
    rows = relay(keep.reshape(shape), away.reshape(shape))
    latest_rows = rows
    backs, router_parts = [], []
    carried = None
    side = first_side = active_grads(after(grads, rows[0]), down_weight, 0, each)
    for c in range(chunks):
        later = None
        if c + 1 < chunks:
            later = [to_owners(after(other[c], side, *rows).reshape(owners, each * CAP, width))]
        *back, rows_all, active, router_part = run_experts(
            rows, side, up_weight, router_weight, scalars, c * each, carried, c + 1 == chunks
        )
        carried = rows_all, active
        if c + 1 < chunks:
            backs.append(to_owners(back[0]))
            side = active_grads(after(grads, router_part), down_weight, (c + 1) * each, each)
        rows = later
        router_parts.append(router_part)
    last_backs = spread(back)
    outs = expert_outputs(after(active, back), down_weight)
    backs = after(backs + last_backs, outs)
    router_grad = functools.reduce(jnp.add, router_parts)
    backs = [b.reshape(-1, width) for b in backs]

    core = (group % 2)[None]
    unit_rows = 16 * groups * max(half // 16, 1)
    sum_rows = -(-(4 * width + kinds) // (2 * unit_rows)) * unit_rows
    gain2_grad, residual_grad, mine, away, ctx_grad = residual_backward(
        core, place_col, residual, norm2_gain, out_grad, out_weight, ctx_t, router_grad, backs,
        sum_rows,
    )
    dq, dk, dv, mine, away, by_distance = attention_backward(
        core, qkv, ctx_grad, probs, n1_t, mine, away
    )
    outs = to_owners(after(outs, *backs)).reshape(owners * local * CAP, width)
    rows_gathered = lax.all_gather(after(rows_all, last_backs[1]), "dp")
    grads_gathered = lax.all_gather(after(grads, first_side, *latest_rows), "dp")
    expert_grads = [None]

    def some_experts(first, count, ready):
        expert_grads[0] = expert_wgrads(
            rows_gathered, after(grads_gathered, ready), up_weight, down_weight, router_weight,
            group_scalars, first, count, expert_grads[0],
        )
        return expert_grads[0]

    results = {}

    def first_norm(ready):
        results["input"] = input_backward(
            hidden_in, norm1_gain, after(residual_grad, ready), qkv_weight, (dq, dk, dv)
        )
        return results["input"]

    def last_sum(ready):
        results["output"] = block_output(
            place_col, residual, valid_mask, after(outs, ready), branch_stat, results["input"][1],
            gain2_grad, by_distance, bucket_table, owners * groups,
        )
        return results["output"]

    def short_sums(ready):
        results["short"] = sum_small(results["output"][1])
        return [results["short"]]

    sizes = [local]
    if local % 8 == 0:
        sizes = [local * 3 // 8, 0, local // 8, local // 2]
    starts = [sum(sizes[:k]) for k in range(len(sizes))]
    experts = [
        [functools.partial(some_experts, at, size)] if size else []
        for at, size in zip(starts, sizes, strict=True)
    ]
    experts += [[]] * (4 - len(experts))
    fillers = [[], [first_norm] + experts[0], [last_sum] + experts[1], [short_sums] + experts[2]]
    fillers += [experts[3]]
    mine, other = sum_everywhere(mine, away, fillers)
    block_out, input_grad = results["output"][0], results["input"][0]
    short = results["short"]
    gain_rows = width // BLOCK
    gain1_sum = short[:gain_rows].reshape(-1)
    gain2_sum = short[6 : 6 + gain_rows].reshape(-1)
    bias_sum = short[BIAS_ROW:].reshape(-1, NBUCKET)[:HEADS].T
    stat_sums = short[STAT_ROW]
    rms_stats = jnp.sqrt(stat_sums[:3] / (jnp.maximum(stat_sums[3], 1.0) * width))
    wide = widen(core, mine, width, None)
    qkv_sum, outw_sum = widen(1 - core, other, width, wide)
    used = slice(2 * width, 2 * width + kinds // 2)
    first = core[0] == 0
    router_sum = jnp.concatenate(
        [
            jnp.where(first, mine[used], other[used]),
            jnp.where(first, other[used], mine[used]),
        ]
    ).astype(F32)
    return (
        block_out,
        input_grad,
        gain1_sum,
        qkv_sum,
        bias_sum,
        outw_sum,
        gain2_sum,
        router_sum.T,
        *expert_grads[0],
        rms_stats,
    )


def solution(mesh):
    spread = P(("dp", "expert"), None)
    placed = (spread,) * 4 + (P(),) * 7 + (P("expert", None, None),) * 2 + (spread,)
    return jax.shard_map(
        on_device,
        mesh=mesh,
        in_specs=placed,
        out_specs=(spread, spread)
        + (P(),) * 6
        + (P("expert", None, "dp"), P("expert", "dp", None), P()),
        check_vma=False,
    )
```
